32 devices in a mesh: wide: 8 (over y, x, core), narrow: 4 (over z).
Axes of the slice: x: 2, y: 2, z: 4, core: 2. Of those that a mesh axis runs over, the one named last changes fastest.
Arguments:
- tokens: bfloat16 [4096, 2048], P(('wide', 'narrow')), may hold values from -6 to 6
- positions: int32 [4096], P(('wide', 'narrow')), may hold values from 0 to 127, as said below
- routes: int32 [4096, 8], P(('wide', 'narrow')), may hold values from 0 to 63, as said below
- cotangent: bfloat16 [4096, 2048], P(('wide', 'narrow')), may hold values from -6 to 6
- w_query: bfloat16 [2048, 2048], P(('wide', 'narrow')), may hold values from -0.125 to 0.125
- w_key: bfloat16 [2048, 2048], P(('wide', 'narrow')), may hold values from -0.125 to 0.125
- w_value: bfloat16 [2048, 2048], P(('wide', 'narrow')), may hold values from -0.125 to 0.125
- w_output: bfloat16 [2048, 2048], P(('wide', 'narrow')), may hold values from -1 to 1
- w_router: bfloat16 [2048, 64], P(('wide', 'narrow')), may hold values from -0.0625 to 0.0625
- gain_attn: bfloat16 [2048], P(('wide', 'narrow')), may hold values from 0.5 to 1.5
- gain_query: bfloat16 [2048], P(('wide', 'narrow')), may hold values from 0.5 to 1.5
- gain_key: bfloat16 [2048], P(('wide', 'narrow')), may hold values from 0.5 to 1.5
- gain_ffn: bfloat16 [2048], P(('wide', 'narrow')), may hold values from 0.5 to 1.5
- w_gate: bfloat16 [64, 2048, 1024], P('wide', 'narrow'), may hold values from -0.125 to 0.125
- w_up: bfloat16 [64, 2048, 1024], P('wide', 'narrow'), may hold values from -0.125 to 0.125
- w_down: bfloat16 [64, 1024, 2048], P('wide', 'narrow'), may hold values from -6 to 6
Outputs:
- block_out: bfloat16 [4096, 2048], P(('wide', 'narrow'))
- input_grad: bfloat16 [4096, 2048], P(('wide', 'narrow'))
- grad_w_query: float32 [2048, 2048], P(('wide', 'narrow'))
- grad_w_key: float32 [2048, 2048], P(('wide', 'narrow'))
- grad_w_value: float32 [2048, 2048], P(('wide', 'narrow'))
- grad_w_output: float32 [2048, 2048], P(('wide', 'narrow'))
- grad_w_router: float32 [2048, 64], P(('wide', 'narrow'))
- grad_gain_attn: float32 [2048], P(('wide', 'narrow'))
- grad_gain_query: float32 [2048], P(('wide', 'narrow'))
- grad_gain_key: float32 [2048], P(('wide', 'narrow'))
- grad_gain_ffn: float32 [2048], P(('wide', 'narrow'))
- grad_w_gate: float32 [64, 2048, 1024], P('wide', 'narrow')
- grad_w_up: float32 [64, 2048, 1024], P('wide', 'narrow')
- grad_w_down: float32 [64, 1024, 2048], P('wide', 'narrow')
- expert_counts: int32 [64], replicated
The draws below stay inside these ranges and needn't reach their ends.
Inputs may be any that keep to these rules, and one draw needn't show every extreme that they name: `positions`: positions count up by one inside a document and restart at 0 where a new document begins; every block of 128 tokens begins a document. A token's 8 routes are different experts. Among the rows of one device, no expert is named by more than 24 rows, and some expert is named by exactly 24.
All inputs are finite; a program needn't handle non-finite values.
Results may differ from the reference program's by a relative error of at most 0.017.
Values may be sent and summed in bfloat16 or wider, within the bound.
No kernel may reach another device: no remote copies, remote signals or barrier semaphores. Data moves between devices by JAX's collectives and lax.ppermute only.
A program may use at most 512 MiB of HBM per device.

```python
import jax
import jax.numpy as jnp
from jax import lax

D = 2048
H = 16
HD = 128
E = 64
TOPK = 8
FF = 1024
TOK_DEV = 128
CAP = 24
TOKENS = 4096


def draw_positions(key, part):
    key = jax.random.fold_in(key, 11)
    blocks = TOKENS // TOK_DEV
    offsets_in = jnp.arange(TOK_DEV, dtype=jnp.int32)
    starts = jax.random.randint(key, (blocks, TOK_DEV), 0, 48) == 0
    starts = jnp.logical_or(starts, offsets_in[None, :] == 0)
    first_block = jnp.arange(blocks, dtype=jnp.int32)[:, None] == 0
    starts = jnp.where(first_block, offsets_in[None, :] == 0, starts)
    begins = lax.cummax(jnp.where(starts, offsets_in[None, :], 0), axis=1)
    return (offsets_in[None, :] - begins).reshape(TOKENS).astype(jnp.int32)


def draw_routes(key, part):
    key = jax.random.fold_in(key, 23)
    blocks = TOKENS // TOK_DEV
    entries = TOK_DEV * TOPK
    light = 2 * (entries // E) - CAP
    key_jitter, key_start, key_order, key_tokens = jax.random.split(key, 4)
    jitter = jax.random.randint(key_jitter, (blocks,), 0, max(1, E // 4)).astype(jnp.int32)
    start = jax.random.randint(key_start, (), 0, E).astype(jnp.int32)
    shift = jnp.arange(blocks, dtype=jnp.int32) * E // blocks + jitter + start
    cyclic = jax.random.permutation(jax.random.fold_in(key_start, 5), E).astype(jnp.int32)
    place = (jnp.arange(E, dtype=jnp.int32)[None, :] - shift[:, None]) % E
    loads = jnp.where(place < E // 2, CAP, light).astype(jnp.int32)
    loads = loads[:, jnp.argsort(cyclic)]
    order = jax.vmap(lambda sub: jax.random.permutation(sub, E))(jax.random.split(key_order, blocks)).astype(jnp.int32)
    ordered_loads = jnp.take_along_axis(loads, order, axis=1)
    ends = jnp.cumsum(ordered_loads, axis=1).astype(jnp.int32)
    entry_ids = jnp.arange(entries, dtype=jnp.int32)

    def list_block(block_ends, block_order):
        index = jnp.sum((block_ends[None, :] <= entry_ids[:, None]).astype(jnp.int32), axis=1)
        return block_order[index]
    listing = jax.vmap(list_block)(ends, order)
    per_token = listing.reshape(blocks, TOPK, TOK_DEV).transpose(0, 2, 1)
    token_order = jax.vmap(lambda sub: jax.random.permutation(sub, TOK_DEV))(jax.random.split(key_tokens, blocks)).astype(jnp.int32)
    per_token = jnp.take_along_axis(per_token, token_order[:, :, None], axis=1)
    return per_token.reshape(TOKENS, TOPK).astype(jnp.int32)


def shard_levels(rng, extent, pieces, smallest, top_value):
    gain = 1.0
    for dim, blocks in pieces:
        steps = jax.random.uniform(jax.random.fold_in(jax.random.fold_in(rng, 6), dim), (blocks,), jnp.float32, smallest / len(pieces), top_value / len(pieces))
        gain = gain * jnp.repeat(jnp.exp(steps), extent[dim] // blocks).reshape((-1,) + (1,) * (len(extent) - 1 - dim))
    return gain


def normal_values(stream_key, shape, width, limit, shards=(), held_as=jnp.bfloat16):
    gain = shard_levels(stream_key, shape, shards, -0.22, 0.18) if shards else 1.0
    drawn = jax.random.normal(stream_key, shape, jnp.float32) * width * gain
    return jnp.minimum(jnp.maximum(drawn, -limit), limit).astype(held_as)


def setup_inputs(seed: int = 0) -> dict:
    arg_keys = jax.random.split(jax.random.key(seed), 17)
    return {
        "tokens": normal_values(arg_keys[0], (TOKENS, D), 1.0, 6.0, ((0, 32),)),
        "positions": draw_positions(jax.random.fold_in(arg_keys[16], 71), 0),
        "routes": draw_routes(jax.random.fold_in(arg_keys[16], 71), 0),
        "cotangent": normal_values(arg_keys[3], (TOKENS, D), 1.0, 6.0, ((0, 32),)),
        "w_query": normal_values(arg_keys[4], (D, D), D ** -0.5, 0.125, ((0, 32),)),
        "w_key": normal_values(arg_keys[5], (D, D), D ** -0.5, 0.125, ((0, 32),)),
        "w_value": normal_values(arg_keys[6], (D, D), D ** -0.5, 0.125, ((0, 32),)),
        "w_output": normal_values(arg_keys[7], (D, D), (D // 64) ** -0.5, 1.0, ((0, 32),)),
        "w_router": normal_values(arg_keys[8], (D, E), (4 * D) ** -0.5, 0.0625, ((0, 32),)),
        "gain_attn": jnp.clip(1.0 + 0.1 * jax.random.normal(arg_keys[9], (D,), jnp.float32), 0.5, 1.5).astype(jnp.bfloat16),
        "gain_query": jnp.clip(1.0 + 0.1 * jax.random.normal(arg_keys[10], (D,), jnp.float32), 0.5, 1.5).astype(jnp.bfloat16),
        "gain_key": jnp.clip(1.0 + 0.1 * jax.random.normal(arg_keys[11], (D,), jnp.float32), 0.5, 1.5).astype(jnp.bfloat16),
        "gain_ffn": jnp.clip(1.0 + 0.1 * jax.random.normal(arg_keys[12], (D,), jnp.float32), 0.5, 1.5).astype(jnp.bfloat16),
        "w_gate": normal_values(arg_keys[13], (E, D, FF), D ** -0.5, 0.125, ((0, 8), (1, 4))),
        "w_up": normal_values(arg_keys[14], (E, D, FF), D ** -0.5, 0.125, ((0, 8), (1, 4))),
        "w_down": normal_values(arg_keys[15], (E, FF, D), 1.0, 6.0, ((0, 8), (1, 4))),
    }


EPSILON = 1e-05
THETA_BASE = 10000.0
HIGHEST = lax.Precision.HIGHEST

@jax.custom_vjp
def low(v):
    return lax.optimization_barrier(v.astype(jnp.bfloat16)).astype(jnp.float32)

@jax.custom_vjp
def low_back(v):
    return v

def low_keep(v):
    return (low(v), None)

def low_pass(kept, grad):
    return (grad,)

def back_keep(v):
    return (v, None)

def back_low(kept, grad):
    return (low(grad),)
low.defvjp(low_keep, low_pass)
low_back.defvjp(back_keep, back_low)

def rms_scale(values, gain_vector):
    return values * lax.rsqrt(lax.optimization_barrier(jnp.mean(values * values, axis=-1, keepdims=True)) + EPSILON) * gain_vector

def softmax_rows(logits):
    shifted = logits - lax.optimization_barrier(jnp.max(logits, axis=-1, keepdims=True))
    powers = jnp.exp(shifted)
    return powers / lax.optimization_barrier(jnp.sum(powers, axis=-1, keepdims=True))

def rotate(values, positions):
    half_width = values.shape[-1] // 2
    frequency = THETA_BASE ** (-2.0 * jnp.arange(half_width, dtype=jnp.float32) / values.shape[-1])
    angles = positions.astype(jnp.float32)[:, None, None] * frequency[None, None, :]
    cosine = jnp.cos(angles)
    sine_part = jnp.sin(angles)
    first_half = values[..., :half_width]
    second_half = values[..., half_width:]
    return jnp.concatenate([first_half * cosine - second_half * sine_part, second_half * cosine + first_half * sine_part], axis=-1)

def expert_tables(routes):
    blocks = routes.shape[0] // TOK_DEV
    flat_routes = routes.reshape(blocks, TOK_DEV * TOPK).astype(jnp.int32)
    onehot = (flat_routes[:, :, None] == jnp.arange(E, dtype=jnp.int32)[None, None, :]).astype(jnp.int32)
    earlier = (jnp.cumsum(onehot, axis=1) - onehot).astype(jnp.int32)
    slot_rank = lax.optimization_barrier(jnp.sum(earlier * onehot, axis=2)).astype(jnp.int32)
    expert_counts = lax.optimization_barrier(jnp.sum(onehot, axis=(0, 1))).astype(jnp.int32)
    targets = (flat_routes * CAP + slot_rank).astype(jnp.int32)
    entries = jnp.arange(TOK_DEV * TOPK, dtype=jnp.int32)
    tables = jax.vmap(lambda target: jnp.full((E * CAP,), -1, jnp.int32).at[target].set(entries))(targets)
    tables = tables.reshape(blocks, E, CAP)
    offsets = (jnp.arange(blocks, dtype=jnp.int32) * TOK_DEV)[:, None, None]
    slot_live = tables >= 0
    sources = jnp.where(slot_live, offsets + tables // TOPK, 0).astype(jnp.int32)
    pick_index = jnp.where(slot_live, offsets * TOPK + tables, 0).astype(jnp.int32)
    sources = sources.transpose(1, 0, 2).reshape(E, blocks * CAP)
    pick_index = pick_index.transpose(1, 0, 2).reshape(E, blocks * CAP)
    slot_live = slot_live.transpose(1, 0, 2).reshape(E, blocks * CAP)
    return (sources, pick_index, slot_live, expert_counts)

def forward(tokens, w_query, w_key, w_value, w_output, w_router, gain_attn, gain_query, gain_key, gain_ffn, w_gate, w_up, w_down, positions, route_onehot, sources, pick_index, slot_live):
    token_count = tokens.shape[0]
    sequences = token_count // TOK_DEV
    score_scale = HD ** (-0.5)
    normed = low(rms_scale(tokens, gain_attn))
    query_raw = low_back(jnp.dot(normed, w_query, precision=HIGHEST))
    key_raw = low_back(jnp.dot(normed, w_key, precision=HIGHEST))
    values = low(low_back(jnp.dot(normed, w_value, precision=HIGHEST))).reshape(token_count, H, HD)
    queries = low(rotate(rms_scale(query_raw, gain_query).reshape(token_count, H, HD), positions))
    key_rows = low(rotate(rms_scale(key_raw, gain_key).reshape(token_count, H, HD), positions))
    causal = jnp.arange(TOK_DEV)[:, None] >= jnp.arange(TOK_DEV)[None, :]

    def attend(block_in):
        query_block, key_block, value_block = block_in
        logits = low_back(jnp.einsum('qhd,khd->hqk', query_block, key_block, precision=HIGHEST) * score_scale)
        attn_probs = low(softmax_rows(jnp.where(causal[None], logits, -1e+30)))
        return low(low_back(jnp.einsum('hqk,khd->qhd', attn_probs, value_block, precision=HIGHEST)))
    attended = lax.map(jax.checkpoint(attend), (queries.reshape(sequences, TOK_DEV, H, HD), key_rows.reshape(sequences, TOK_DEV, H, HD), values.reshape(sequences, TOK_DEV, H, HD)))
    branch = low_back(jnp.dot(attended.reshape(token_count, D), w_output, precision=HIGHEST))
    residual = tokens + branch
    normed_ffn = low(rms_scale(residual, gain_ffn))
    router_logits = low_back(jnp.dot(normed_ffn, w_router, precision=HIGHEST))
    router_probs = softmax_rows(router_logits)
    gate_flat = lax.optimization_barrier(jnp.sum(route_onehot * router_probs[:, None, :], axis=-1)).reshape(-1)

    def expert_step(block_in):
        gate_weight, up_weight, down_weight, source_rows, live_rows = block_in
        expert_rows = low_back(jnp.where(live_rows[:, None], normed_ffn[source_rows], 0.0))
        gate_value = low_back(jnp.dot(expert_rows, gate_weight, precision=HIGHEST))
        up_value = low_back(jnp.dot(expert_rows, up_weight, precision=HIGHEST))
        hidden = low(jax.nn.silu(gate_value) * up_value)
        return low(low_back(jnp.dot(hidden, down_weight, precision=HIGHEST)))
    results = lax.map(jax.checkpoint(expert_step), (w_gate, w_up, w_down, sources, slot_live))
    weights = jnp.where(slot_live, gate_flat[pick_index], 0.0)
    mixture = jnp.zeros_like(residual).at[sources.reshape(-1)].add((weights[:, :, None] * results).reshape(-1, D))
    return residual + mixture

def reference(tokens, positions, routes, cotangent, w_query, w_key, w_value, w_output, w_router, gain_attn, gain_query, gain_key, gain_ffn, w_gate, w_up, w_down):
    sources, pick_index, slot_live, expert_counts = expert_tables(routes)
    route_onehot = (routes[:, :, None] == jnp.arange(E, dtype=jnp.int32)[None, None, :]).astype(jnp.float32)
    floats = tuple((array_in.astype(jnp.float32) for array_in in (tokens, w_query, w_key, w_value, w_output, w_router, gain_attn, gain_query, gain_key, gain_ffn, w_gate, w_up, w_down)))

    def forward_part(*params):
        return forward(*params, positions, route_onehot, sources, pick_index, slot_live)
    output, pullback = jax.vjp(forward_part, *floats)
    gradients = pullback(cotangent.astype(jnp.float32))
    return (output.astype(jnp.bfloat16), gradients[0].astype(jnp.bfloat16), gradients[1], gradients[2], gradients[3], gradients[4], gradients[5], gradients[6], gradients[7], gradients[8], gradients[9], gradients[10], gradients[11], gradients[12], expert_counts)
```

```python
import functools

import jax
import jax.numpy as jnp
from jax import lax
from jax.experimental import pallas as pl
from jax.experimental.pallas import tpu as pltpu
from jax.sharding import PartitionSpec as P

D = 2048
H = 16
HD = 128
E = 64
TOPK = 8
CAP = 24
FF = 1024
LANES = 128
EPSILON = 1e-05
THETA_BASE = 10000.0
CHUNKS = 4

BF = jnp.bfloat16
F32 = jnp.float32
VMEM_BYTES = 56 * 1024 * 1024


def matmul(a, b, dims):
    return lax.dot_general(a, b, (dims, ((), ())), preferred_element_type=F32)


def dispatch_body(pieces, rows_each, *refs):
    picks = refs[0]
    sources = refs[1 : 1 + pieces]
    out = refs[-1]
    experts = out.shape[0]
    for q in range(pieces):
        rows = matmul(picks[q, 0], sources[q][...], ((1,), (0,))).astype(BF)
        out[:, q * rows_each : (q + 1) * rows_each, :] = rows.reshape(
            experts, rows_each, rows.shape[-1]
        )


def dispatch(picks, sources, half, total_rows, buffer=None):
    pieces, pairs, slots, span = picks.shape
    width = sources[0].shape[1]
    rows_each = 2 * CAP
    experts = slots // rows_each
    in_specs = [pl.BlockSpec((pieces, 1, slots, span), lambda j: (0, j, 0, 0))]
    in_specs += [pl.BlockSpec((span, width), lambda j: (j, 0))] * pieces
    args = [picks, *sources]
    aliases = {}
    if buffer is not None:
        in_specs.append(pl.BlockSpec(memory_space=pl.ANY))
        aliases = {len(args): 0}
        args.append(buffer)
    block = pieces * rows_each
    return pl.pallas_call(
        functools.partial(dispatch_body, pieces, rows_each),
        grid=(pairs,),
        in_specs=in_specs,
        out_specs=pl.BlockSpec((experts, block, width), lambda j: (0, half * pairs + j, 0)),
        out_shape=jax.ShapeDtypeStruct((experts, total_rows, width), BF),
        input_output_aliases=aliases,
        compiler_params=pltpu.CompilerParams(vmem_limit_bytes=VMEM_BYTES),
        cost_estimate=pl.CostEstimate(
            flops=2 * pieces * pairs * slots * span * width,
            bytes_accessed=2 * pieces * pairs * (slots + span) * width,
            transcendentals=0,
        ),
        name="dispatch",
    )(*args)


def combine_body(pieces, rows_each, chunks, *refs):
    picks = refs[0]
    rows = refs[1 : 1 + chunks]
    outs = refs[1 + chunks :]
    for q in range(pieces):
        total = None
        at = 0
        for chunk in rows:
            experts = chunk.shape[0]
            part = chunk[:, q * rows_each : (q + 1) * rows_each, :].reshape(
                experts * rows_each, chunk.shape[-1]
            )
            term = matmul(picks[q, 0, at : at + experts * rows_each, :], part, ((0,), (0,)))
            total = term if total is None else total + term
            at += experts * rows_each
        outs[q][...] = total.astype(BF)


def combine(picks, rows, half):
    pieces, pairs, slots, span = picks.shape
    rows_each = 2 * CAP
    width = rows[0].shape[-1]
    block = pieces * rows_each
    in_specs = [pl.BlockSpec((pieces, 1, slots, span), lambda j: (0, j, 0, 0))]
    for chunk in rows:
        in_specs.append(
            pl.BlockSpec((chunk.shape[0], block, width), lambda j: (0, half * pairs + j, 0))
        )
    return pl.pallas_call(
        functools.partial(combine_body, pieces, rows_each, len(rows)),
        grid=(pairs,),
        in_specs=in_specs,
        out_specs=[pl.BlockSpec((span, width), lambda j: (j, 0))] * pieces,
        out_shape=[jax.ShapeDtypeStruct((pairs * span, width), BF)] * pieces,
        compiler_params=pltpu.CompilerParams(vmem_limit_bytes=VMEM_BYTES),
        cost_estimate=pl.CostEstimate(
            flops=2 * pieces * pairs * slots * span * width,
            bytes_accessed=2 * pieces * pairs * (slots + span) * width,
            transcendentals=0,
        ),
        name="combine",
    )(picks, *rows)


def expert_body(parts, tiles, start, first, *refs):
    where = refs[0]
    rows_ref, ups_ref = refs[1], refs[2]
    weights = refs[3 : 3 + parts]
    down_ref = refs[3 + parts]
    rest = refs[4 + parts + (0 if first else 1) :]
    results_ref, row_grads_ref = rest[0], rest[1]
    weight_grads = rest[2 : 2 + parts]
    down_grad_ref = rest[2 + parts]
    sums = rest[3 + parts]
    down_sum = rest[4 + parts]
    mine = where[0]
    tile = pl.program_id(1)
    depth = D // parts
    width = FF // parts
    at = [pl.multiple_of((mine ^ s) * depth, depth) for s in range(parts)]

    both = None
    for s in range(parts):
        term = matmul(rows_ref[0, :, pl.ds(at[s], depth)], weights[s][0], ((1,), (0,)))
        both = term if both is None else both + term
    gate_value = both[:, :width]
    up_value = both[:, width:]
    sigma = 1.0 / (1.0 + jnp.exp(-gate_value))
    silu = gate_value * sigma
    hidden = (silu * up_value).astype(BF)
    down = down_ref[0]
    results = matmul(hidden, down, ((1,), (0,)))

    expert = where[1] + start + pl.program_id(0)
    lane = lax.broadcasted_iota(jnp.int32, (rows_ref.shape[1], LANES), 1)
    high = lane == expert
    low = lane == expert + E
    probs = rows_ref[0, :, D:].astype(F32)
    weight = jnp.sum(jnp.where(high | low, probs, 0.0), axis=1, keepdims=True)
    upstream = ups_ref[0].astype(F32)
    gate_grad = jnp.sum(upstream * results, axis=1, keepdims=True)
    results_ref[0] = (weight * results).astype(BF)
    result_grads = (weight * upstream).astype(BF)

    hidden_grads = matmul(result_grads, down, ((1,), (1,)))
    gate_value_grads = (
        hidden_grads * up_value * (sigma * (1.0 + gate_value * (1.0 - sigma)))
    ).astype(BF)
    up_value_grads = (hidden_grads * silu).astype(BF)
    both_grads = jnp.concatenate([gate_value_grads, up_value_grads], axis=1)
    down_term = matmul(hidden, result_grads, ((0,), (0,)))
    for s in range(parts):
        row_grads_ref[0, :, pl.ds(at[s], depth)] = matmul(
            both_grads, weights[s][0], ((1,), (1,))
        ).astype(BF)
    top = gate_grad.astype(BF)
    bottom = (gate_grad - top.astype(F32)).astype(BF)
    row_grads_ref[0, :, D:] = jnp.where(
        high, top.astype(F32), jnp.where(low, bottom.astype(F32), 0.0)
    ).astype(BF)

    terms = [
        matmul(rows_ref[0, :, pl.ds(at[s], depth)], both_grads, ((0,), (0,)))
        for s in range(parts)
    ]

    @pl.when(tile == 0)
    def _():
        for s in range(parts):
            sums[s] = terms[s]
        down_sum[...] = down_term

    @pl.when(tile > 0)
    def _():
        for s in range(parts):
            sums[s] += terms[s]
        down_sum[...] += down_term

    @pl.when(tile == tiles - 1)
    def _():
        for s in range(parts):
            weight_grads[s][0] = sums[s].astype(BF)
        down_grad_ref[0] = down_sum[...]


def expert_chunk(where, rows, ups, weights, down, start, down_grad):
    parts = len(weights)
    experts, depth, width2 = weights[0].shape
    local, total_rows, wide_row = rows.shape
    tile = 384
    tiles = total_rows // tile
    slice_ff = down.shape[1]
    first = down_grad is None
    in_specs = [
        pl.BlockSpec((1, tile, wide_row), lambda e, i, c: (start + e, i, 0)),
        pl.BlockSpec((1, tile, D), lambda e, i, c: (start + e, i, 0)),
    ]
    in_specs += [pl.BlockSpec((1, depth, width2), lambda e, i, c: (e, 0, 0))] * parts
    in_specs.append(pl.BlockSpec((1, slice_ff, D), lambda e, i, c: (start + e, 0, 0)))
    args = [where, rows, ups, *weights, down]
    aliases = {}
    if not first:
        in_specs.append(pl.BlockSpec(memory_space=pl.ANY))
        aliases = {len(args): 2 + parts}
        args.append(down_grad)
    out_specs = [
        pl.BlockSpec((1, tile, D), lambda e, i, c: (e, i, 0)),
        pl.BlockSpec((1, tile, wide_row), lambda e, i, c: (e, i, 0)),
    ]
    out_specs += [pl.BlockSpec((1, depth, width2), lambda e, i, c: (e, 0, 0))] * parts
    out_specs.append(pl.BlockSpec((1, slice_ff, D), lambda e, i, c: (start + e, 0, 0)))
    out_shape = [
        jax.ShapeDtypeStruct((experts, total_rows, D), BF),
        jax.ShapeDtypeStruct((experts, total_rows, wide_row), BF),
    ]
    out_shape += [jax.ShapeDtypeStruct((experts, depth, width2), BF)] * parts
    out_shape.append(jax.ShapeDtypeStruct((local, slice_ff, D), F32))
    out = pl.pallas_call(
        functools.partial(expert_body, parts, tiles, start, first),
        grid_spec=pltpu.PrefetchScalarGridSpec(
            num_scalar_prefetch=1,
            grid=(experts, tiles),
            in_specs=in_specs,
            out_specs=out_specs,
            scratch_shapes=[
                pltpu.VMEM((parts, depth, width2), F32),
                pltpu.VMEM((slice_ff, D), F32),
            ],
        ),
        out_shape=out_shape,
        input_output_aliases=aliases,
        compiler_params=pltpu.CompilerParams(vmem_limit_bytes=VMEM_BYTES),
        cost_estimate=pl.CostEstimate(
            flops=18 * experts * total_rows * D * slice_ff,
            bytes_accessed=8 * experts * total_rows * D + 18 * experts * D * slice_ff,
            transcendentals=experts * total_rows * slice_ff,
        ),
        name="experts",
    )(*args)
    return out[0], out[1], out[2 : 2 + parts], out[2 + parts]


def assemble_body(parts, width, *refs):
    where = refs[0]
    sources = refs[1 : 1 + parts]
    gate_ref, up_ref = refs[-2], refs[-1]
    for s in range(parts):
        columns = pl.ds(pl.multiple_of((where[0] ^ s) * width, width), width)
        gate_ref[0, :, columns] = sources[s][0, :, :width].astype(F32)
        up_ref[0, :, columns] = sources[s][0, :, width:].astype(F32)


def assemble(where, sources, start, local, buffers):
    parts = len(sources)
    experts, depth, width2 = sources[0].shape
    in_specs = [pl.BlockSpec((1, depth, width2), lambda e, c: (e, 0, 0))] * parts
    args = [where, *sources]
    aliases = {}
    if buffers is not None:
        in_specs = in_specs + [pl.BlockSpec(memory_space=pl.ANY)] * 2
        aliases = {len(args): 0, len(args) + 1: 1}
        args += list(buffers)
    spec = pl.BlockSpec((1, depth, FF), lambda e, c: (start + e, 0, 0))
    return pl.pallas_call(
        functools.partial(assemble_body, parts, width2 // 2),
        grid_spec=pltpu.PrefetchScalarGridSpec(
            num_scalar_prefetch=1,
            grid=(experts,),
            in_specs=in_specs,
            out_specs=[spec, spec],
        ),
        out_shape=[jax.ShapeDtypeStruct((local, depth, FF), F32)] * 2,
        input_output_aliases=aliases,
        compiler_params=pltpu.CompilerParams(vmem_limit_bytes=VMEM_BYTES),
        cost_estimate=pl.CostEstimate(
            flops=0, bytes_accessed=6 * experts * depth * FF * 2, transcendentals=0
        ),
        name="assemble",
    )(*args)


def make_on_device(wide, narrow):
    planes = wide // 2
    local = E // wide
    heads = H // wide
    features = heads * HD
    chunks = min(CHUNKS, local)
    per_chunk = local // chunks

    def swap(x, axis, r):
        size = wide if axis == "wide" else narrow
        return lax.ppermute(x, axis, [(i, i ^ r) for i in range(size)])

    def gather_narrow(x):
        return [x] + [swap(x, "narrow", s) for s in range(1, narrow)]

    def gather_wide(x):
        own = [x] + [swap(x, "wide", 2 * q) for q in range(1, planes)]
        other = [swap(piece, "wide", 1) for piece in own]
        return own, other

    def interleave(own, other):
        return [piece for pair in zip(own, other) for piece in pair]

    def exchange(parts, axis):
        return [parts[0]] + [swap(parts[r], axis, r) for r in range(1, len(parts))]

    def add_up(parts):
        total = parts[0].astype(F32)
        for part in parts[1:]:
            total = total + part.astype(F32)
        return total

    def scatter_wide(own, other):
        sums = []
        for q in range(planes):
            sums.append(own[q].astype(F32) + swap(other[q], "wide", 1).astype(F32))
        total = sums[0]
        for q in range(1, planes):
            total = total + swap(sums[q].astype(BF), "wide", 2 * q).astype(F32)
        return total

    def on_device(
        tokens, positions, routes, cotangent,
        w_query, w_key, w_value, w_output, w_router,
        gain_attn, gain_query, gain_key, gain_ffn,
        w_gate, w_up, w_down,
    ):
        count = tokens.shape[0]
        rows = w_query.shape[0]
        w = lax.axis_index("wide")
        n = lax.axis_index("narrow")
        where = jnp.stack([n, w * local]).astype(jnp.int32)
        wide_order = jnp.arange(wide) ^ w
        narrow_order = jnp.arange(narrow) ^ n
        shard_order = (wide_order[:, None] * narrow + narrow_order[None, :]).reshape(-1)

        routed = jnp.any(
            routes[:, :, None] == jnp.arange(E, dtype=jnp.int32)[None, None, :], axis=1
        )
        earlier = matmul(
            jnp.tril(jnp.ones((count, count), BF), -1), routed.astype(BF), ((1,), (0,))
        )
        slots = jnp.where(routed, earlier, -1.0).astype(BF).T

        small = jnp.concatenate(
            [
                w_router.reshape(-1), gain_attn, gain_query, gain_key, gain_ffn,
                positions.astype(BF),
            ]
        )
        small_rows = -(-small.shape[0] // LANES)
        bundle_rows = -(-(E + small_rows) // 16) * 16
        small = jnp.pad(small, (0, (bundle_rows - E) * LANES - small.shape[0]))
        bundle = jnp.concatenate([slots, small.reshape(-1, LANES)], axis=0)
        bundle_z = jnp.stack(gather_narrow(bundle))
        bundles = jnp.stack([bundle_z] + [swap(bundle_z, "wide", r) for r in range(1, wide)])
        all_slots = bundles[:, :, :E, :]
        all_small = bundles[:, :, E:, :].reshape(wide * narrow, -1)
        plane_positions = all_small.reshape(wide, narrow, -1)[
            :, 0, rows * E + 4 * rows : rows * E + 4 * rows + count
        ].reshape(wide * count)
        all_small = jnp.take(all_small, shard_order, axis=0)
        router_full = all_small[:, : rows * E].reshape(D, E)
        gains = [
            all_small[:, rows * E + i * rows : rows * E + (i + 1) * rows]
            .reshape(D)
            .astype(F32)
            for i in range(4)
        ]
        attn_gain, query_gain, key_gain, ffn_gain = gains
        query_gain = lax.dynamic_slice_in_dim(query_gain, w * features, features)
        key_gain = lax.dynamic_slice_in_dim(key_gain, w * features, features)
        expert_counts = jnp.sum((all_slots >= 0).astype(jnp.int32), axis=(0, 1, 3))

        own, other = gather_wide(tokens)
        plane_tokens = jnp.concatenate(interleave(own, other), axis=0).astype(F32)
        plane_count = plane_tokens.shape[0]

        stacked = jnp.concatenate(
            [x.reshape(rows, wide, features) for x in (w_query, w_key, w_value)], axis=-1
        ).transpose(1, 0, 2)
        stacked = jnp.take(stacked, wide_order, axis=0)
        columns = jnp.stack(exchange([stacked[r] for r in range(wide)], "wide"))
        columns = jnp.stack(gather_narrow(columns), axis=1)
        qkv = jnp.take(
            columns.reshape(wide * narrow, rows, 3 * features), shard_order, axis=0
        ).reshape(D, 3 * features)
        output_rows = jnp.take(
            jnp.stack(gather_narrow(w_output)), narrow_order, axis=0
        ).reshape(features, D)

        cot_z = jnp.concatenate(gather_narrow(cotangent), axis=0)
        cot_own, cot_other = gather_wide(cot_z)

        expert_weights = []
        slice_ff = FF // narrow
        for c in range(chunks):
            lo, hi = c * per_chunk, (c + 1) * per_chunk
            mine = []
            for s in range(narrow):
                at = (n ^ s) * slice_ff
                mine.append(
                    jnp.concatenate(
                        [
                            lax.dynamic_slice_in_dim(w_gate[lo:hi], at, slice_ff, axis=2),
                            lax.dynamic_slice_in_dim(w_up[lo:hi], at, slice_ff, axis=2),
                        ],
                        axis=2,
                    )
                )
            expert_weights.append(exchange(mine, "narrow"))

        inverse = lax.rsqrt(jnp.mean(plane_tokens * plane_tokens, axis=-1, keepdims=True) + EPSILON)
        normed = (plane_tokens * inverse * attn_gain).astype(BF)
        raw = matmul(normed, qkv, ((1,), (0,)))
        query_raw = raw[:, :features]
        key_raw = raw[:, features : 2 * features]
        values = raw[:, 2 * features :].astype(BF).reshape(wide, count, heads, HD)

        def sum_wide(x):
            return add_up([x] + [swap(x, "wide", r) for r in range(1, wide)])

        def row_sums(a, b):
            sums = jnp.stack([jnp.sum(a, axis=-1), jnp.sum(b, axis=-1)])
            blocks = sums.reshape(2, wide, count)
            total = blocks
            for r in range(1, wide):
                came = swap(blocks, "wide", r)
                total = total + jnp.stack([came[:, x ^ r] for x in range(wide)], axis=1)
            total = total.reshape(2, plane_count)
            return total[0][:, None], total[1][:, None]

        query_square, key_square = row_sums(query_raw * query_raw, key_raw * key_raw)
        query_r = lax.rsqrt(query_square / D + EPSILON)
        key_r = lax.rsqrt(key_square / D + EPSILON)
        frequency = THETA_BASE ** (-2.0 * jnp.arange(HD // 2, dtype=F32) / HD)
        angles = plane_positions.astype(F32)[:, None] * frequency[None, :]
        cosine = jnp.cos(angles)[:, None, :]
        sine = jnp.sin(angles)[:, None, :]

        def turn(x, sign):
            x = x.reshape(plane_count, heads, HD)
            a, b = x[..., : HD // 2], x[..., HD // 2 :]
            return jnp.concatenate(
                [a * cosine - sign * b * sine, b * cosine + sign * a * sine], axis=-1
            )

        shape = (wide, count, heads, HD)
        queries = turn(query_raw * query_r * query_gain, 1.0).astype(BF).reshape(shape)
        key_rows = turn(key_raw * key_r * key_gain, 1.0).astype(BF).reshape(shape)
        scale = HD ** (-0.5)
        causal = (jnp.arange(count)[:, None] >= jnp.arange(count)[None, :])[None, None]
        scores = (
            jnp.einsum("bqhd,bkhd->bhqk", queries, key_rows, preferred_element_type=F32) * scale
        )
        scores = jnp.where(causal, scores, -1e30)
        powers = jnp.exp(scores - jnp.max(scores, axis=-1, keepdims=True))
        attn_probs = powers / jnp.sum(powers, axis=-1, keepdims=True)
        probs_low = attn_probs.astype(BF)
        attended = (
            jnp.einsum("bhqk,bkhd->bqhd", probs_low, values, preferred_element_type=F32)
            .astype(BF)
            .reshape(plane_count, features)
        )
        branch = matmul(attended, output_rows, ((1,), (0,))).astype(BF)
        branch = branch.reshape(planes, 2, count, D)
        branch = scatter_wide(
            [branch[q, 0] for q in range(planes)], [branch[q, 1] for q in range(planes)]
        )

        residual = tokens.astype(F32) + branch
        ffn_r = lax.rsqrt(jnp.mean(residual * residual, axis=-1, keepdims=True) + EPSILON)
        normed_ffn = (residual * ffn_r * ffn_gain).astype(BF)
        logits = matmul(normed_ffn, router_full, ((1,), (0,)))
        router_powers = jnp.exp(logits - jnp.max(logits, axis=-1, keepdims=True))
        router_probs = router_powers / jnp.sum(router_powers, axis=-1, keepdims=True)
        probs_top = router_probs.astype(BF)
        probs_rest = (router_probs - probs_top.astype(F32)).astype(BF)

        message = jnp.concatenate([normed_ffn, probs_top, probs_rest], axis=1)
        message_z = jnp.concatenate(gather_narrow(message), axis=0)
        token_own, token_other = gather_wide(message_z)

        local_slots = lax.dynamic_slice_in_dim(all_slots, w * local, local, axis=2)
        pairs = narrow // 2
        local_slots = (
            local_slots.reshape(planes, 2, pairs, 2, local, count)
            .transpose(1, 0, 2, 4, 3, 5)
            .reshape(2, planes, pairs, local, 1, 2 * count)
        )
        row = jnp.arange(2 * CAP)[:, None]
        lane = jnp.arange(2 * count)[None, :]
        picks = (
            ((local_slots == (row % CAP).astype(BF)) & (row // CAP == lane // count))
            .astype(BF)
            .reshape(2, planes, pairs, local * 2 * CAP, 2 * count)
        )
        total_rows = wide * narrow * CAP
        ups = dispatch(picks[0], cot_own, 0, total_rows)
        ups = dispatch(picks[1], cot_other, 1, total_rows, ups)
        expert_rows = dispatch(picks[0], token_own, 0, total_rows)
        expert_rows = dispatch(picks[1], token_other, 1, total_rows, expert_rows)

        results, row_grads, came = [], [], []
        down_grad = None
        for c in range(chunks):
            result, row_grad, weight_grads, down_grad = expert_chunk(
                where, expert_rows, ups, expert_weights[c], w_down, c * per_chunk, down_grad
            )
            results.append(result)
            row_grads.append(row_grad)
            came.append(exchange(weight_grads, "narrow"))
        grads_own = combine(picks[0], row_grads, 0)
        grads_other = combine(picks[1], row_grads, 1)
        mix_own = combine(picks[0], results, 0)
        mix_other = combine(picks[1], results, 1)

        def scatter_tokens(own_terms, other_terms):
            plane_sum = scatter_wide(own_terms, other_terms).astype(BF)
            blocks = plane_sum.reshape(narrow, count, plane_sum.shape[-1])
            return add_up(exchange([blocks[s] for s in range(narrow)], "narrow"))

        ffn_message = scatter_tokens(grads_own, grads_other)
        mixture = scatter_tokens(mix_own, mix_other)
        block_out = (residual + mixture).astype(BF)

        upstream = cotangent.astype(F32)
        prob_grads = ffn_message[:, D : D + E] + ffn_message[:, D + E : D + 2 * E]
        logit_grads = (
            router_probs
            * (prob_grads - jnp.sum(router_probs * prob_grads, axis=-1, keepdims=True))
        ).astype(BF)
        ffn_grads = ffn_message[:, :D] + matmul(logit_grads, router_full, ((1,), (1,)))

        def norm_back(v, r, gain, dy):
            u = dy * gain
            return r * u - v * (r * r * r) * jnp.mean(u * v, axis=-1, keepdims=True)

        residual_grads = upstream + norm_back(residual, ffn_r, ffn_gain, ffn_grads)
        ffn_gain_part = jnp.sum(ffn_grads * residual * ffn_r, axis=0)
        branch_grads = residual_grads.astype(BF)

        logit_z = jnp.concatenate(gather_narrow(logit_grads), axis=0)
        logit_own, logit_other = gather_wide(logit_z)
        shard = (w * narrow + n) * rows
        grad_router = None
        for tokens_in, grads_in in zip(token_own + token_other, logit_own + logit_other):
            part = lax.dynamic_slice_in_dim(tokens_in, shard, rows, axis=1)
            term = matmul(part, grads_in, ((0,), (0,)))
            grad_router = term if grad_router is None else grad_router + term

        own, other = gather_wide(branch_grads)
        plane_grads = jnp.concatenate(interleave(own, other), axis=0)
        attended_grads = (
            matmul(plane_grads, output_rows, ((1,), (1,))).astype(BF).reshape(shape)
        )
        grad_output = matmul(attended, plane_grads, ((0,), (0,)))
        prob_grads_attn = jnp.einsum(
            "bqhd,bkhd->bhqk", attended_grads, values, preferred_element_type=F32
        )
        value_grads = (
            jnp.einsum("bhqk,bqhd->bkhd", probs_low, attended_grads, preferred_element_type=F32)
            .astype(BF)
            .reshape(plane_count, features)
        )
        score_grads = attn_probs * (
            prob_grads_attn - jnp.sum(attn_probs * prob_grads_attn, axis=-1, keepdims=True)
        )
        score_grads = jnp.where(causal, score_grads, 0.0).astype(BF)
        query_grads = (
            jnp.einsum("bhqk,bkhd->bqhd", score_grads, key_rows, preferred_element_type=F32)
            * scale
        )
        key_grads = (
            jnp.einsum("bhqk,bqhd->bkhd", score_grads, queries, preferred_element_type=F32)
            * scale
        )
        query_dy = turn(query_grads, -1.0).reshape(plane_count, features)
        key_dy = turn(key_grads, -1.0).reshape(plane_count, features)
        query_u = query_dy * query_gain
        key_u = key_dy * key_gain
        query_dot, key_dot = row_sums(query_u * query_raw, key_u * key_raw)
        query_raw_grads = query_r * query_u - query_raw * (query_r**3) * (query_dot / D)
        key_raw_grads = key_r * key_u - key_raw * (key_r**3) * (key_dot / D)
        raw_grads = jnp.concatenate(
            [query_raw_grads.astype(BF), key_raw_grads.astype(BF), value_grads], axis=1
        )
        qk_gain_parts = jnp.stack(
            [
                jnp.sum(query_dy * query_raw * query_r, axis=0),
                jnp.sum(key_dy * key_raw * key_r, axis=0),
            ]
        )
        normed_grads = matmul(raw_grads, qkv, ((1,), (1,))).astype(BF)
        normed_grads = normed_grads.reshape(planes, 2, count, D)
        normed_grads = scatter_wide(
            [normed_grads[q, 0] for q in range(planes)],
            [normed_grads[q, 1] for q in range(planes)],
        )
        own_inputs = tokens.astype(F32)
        own_r = inverse[:count]
        input_grad = (
            residual_grads + norm_back(own_inputs, own_r, attn_gain, normed_grads)
        ).astype(BF)
        attn_gain_part = jnp.sum(normed_grads * own_inputs * own_r, axis=0)

        grad_qkv = matmul(normed, raw_grads, ((0,), (0,))).astype(BF)
        grad_qkv = jnp.take(
            grad_qkv.reshape(wide, narrow, rows, 3 * features), narrow_order, axis=1
        )
        grad_qkv = add_up(exchange([grad_qkv[:, s] for s in range(narrow)], "narrow"))
        grad_qkv = jnp.take(grad_qkv, wide_order, axis=0)
        grad_qkv = jnp.stack(exchange([grad_qkv[r] for r in range(wide)], "wide"))
        grad_qkv = jnp.take(grad_qkv, wide_order, axis=0).transpose(1, 0, 2)
        grad_query, grad_key, grad_value = [
            grad_qkv[..., i * features : (i + 1) * features].reshape(rows, D) for i in range(3)
        ]
        grad_output = jnp.take(
            grad_output.astype(BF).reshape(narrow, rows, D), narrow_order, axis=0
        )
        grad_output = add_up(exchange([grad_output[s] for s in range(narrow)], "narrow"))

        gain_parts = jnp.stack([attn_gain_part, ffn_gain_part])
        gain_parts = jnp.take(gain_parts.reshape(2, wide, features), wide_order, axis=1)
        gain_parts = add_up(exchange([gain_parts[:, r] for r in range(wide)], "wide"))
        gain_parts = jnp.concatenate([gain_parts, qk_gain_parts], axis=0)
        gain_parts = jnp.take(gain_parts.reshape(4, narrow, rows), narrow_order, axis=1)
        gain_parts = add_up(exchange([gain_parts[:, s] for s in range(narrow)], "narrow"))

        buffers = None
        for c in range(chunks):
            buffers = assemble(where, came[c], c * per_chunk, local, buffers)
        grad_gate, grad_up = buffers

        return (
            block_out, input_grad, grad_query, grad_key, grad_value, grad_output, grad_router,
            gain_parts[0], gain_parts[2], gain_parts[3], gain_parts[1],
            grad_gate, grad_up, down_grad, expert_counts,
        )

    return on_device


def solution(mesh):
    both = ("wide", "narrow")
    in_specs = (P(both, None), P(both), P(both, None), P(both, None))
    in_specs += (P(both, None),) * 5 + (P(both),) * 4 + (P("wide", "narrow", None),) * 3
    out_specs = (P(both, None),) * 7 + (P(both),) * 4 + (P("wide", "narrow", None),) * 3 + (P(),)
    return jax.shard_map(
        make_on_device(mesh.shape["wide"], mesh.shape["narrow"]),
        mesh=mesh,
        in_specs=in_specs,
        out_specs=out_specs,
        check_vma=False,
    )
```

```python
import functools

import jax
import jax.numpy as jnp
from jax import lax
from jax.experimental import pallas as pl
from jax.experimental.pallas import tpu as pltpu
from jax.sharding import PartitionSpec as P

D = 2048
H = 16
HD = 128
E = 64
TOPK = 8
CAP = 24
FF = 1024
LANES = 128
EPSILON = 1e-05
THETA_BASE = 10000.0

BF = jnp.bfloat16
F32 = jnp.float32
VMEM_BYTES = 56 * 1024 * 1024


def matmul(a, b, dims):
    return lax.dot_general(a, b, (dims, ((), ())), preferred_element_type=F32)


def dispatch_body(pieces, each, *refs):
    picks = refs[0]
    sources = refs[1 : 1 + pieces]
    out = refs[-1]
    for q in range(pieces):
        rows = matmul(picks[q, 0], sources[q][...], ((1,), (0,))).astype(BF)
        out[:, q * each : (q + 1) * each, :] = rows.reshape(-1, each, rows.shape[-1])


def dispatch(picks, sources, half, buffer=None):
    pieces, pairs, slots, span = picks.shape
    width = sources[0].shape[1]
    each = 2 * CAP
    block = pieces * each
    in_specs = [pl.BlockSpec((pieces, 1, slots, span), lambda j: (0, j, 0, 0))]
    in_specs += [pl.BlockSpec((span, width), lambda j: (j, 0))] * pieces
    args = [picks, *sources]
    aliases = {}
    if buffer is not None:
        in_specs.append(pl.BlockSpec(memory_space=pl.ANY))
        aliases = {len(args): 0}
        args.append(buffer)
    return pl.pallas_call(
        functools.partial(dispatch_body, pieces, each),
        grid=(pairs,),
        in_specs=in_specs,
        out_specs=pl.BlockSpec(
            (slots // each, block, width), lambda j: (0, half * pairs + j, 0)
        ),
        out_shape=jax.ShapeDtypeStruct((slots // each, 2 * pairs * block, width), BF),
        input_output_aliases=aliases,
        compiler_params=pltpu.CompilerParams(vmem_limit_bytes=VMEM_BYTES),
        cost_estimate=pl.CostEstimate(
            flops=2 * pieces * pairs * slots * span * width,
            bytes_accessed=2 * pieces * pairs * (slots + span) * width,
            transcendentals=0,
        ),
        name="dispatch",
    )(*args)


def combine_body(pieces, each, chunks, *refs):
    picks = refs[0]
    rows = refs[1 : 1 + chunks]
    outs = refs[1 + chunks :]
    for q in range(pieces):
        total = None
        at = 0
        for chunk in rows:
            part = chunk[:, q * each : (q + 1) * each, :].reshape(-1, chunk.shape[-1])
            size = part.shape[0]
            term = matmul(picks[q, 0, at : at + size, :], part, ((0,), (0,)))
            total = term if total is None else total + term
            at += size
        outs[q][...] = total.astype(BF)


def combine(picks, rows, half):
    pieces, pairs, slots, span = picks.shape
    each = 2 * CAP
    width = rows[0].shape[-1]
    in_specs = [pl.BlockSpec((pieces, 1, slots, span), lambda j: (0, j, 0, 0))]
    for chunk in rows:
        in_specs.append(
            pl.BlockSpec(
                (chunk.shape[0], pieces * each, width), lambda j: (0, half * pairs + j, 0)
            )
        )
    return pl.pallas_call(
        functools.partial(combine_body, pieces, each, len(rows)),
        grid=(pairs,),
        in_specs=in_specs,
        out_specs=[pl.BlockSpec((span, width), lambda j: (j, 0))] * pieces,
        out_shape=[jax.ShapeDtypeStruct((pairs * span, width), BF)] * pieces,
        compiler_params=pltpu.CompilerParams(vmem_limit_bytes=VMEM_BYTES),
        cost_estimate=pl.CostEstimate(
            flops=2 * pieces * pairs * slots * span * width,
            bytes_accessed=2 * pieces * pairs * (slots + span) * width,
            transcendentals=0,
        ),
        name="combine",
    )(picks, *rows)


def expert_body(parts, tiles, start, aliased, *refs):
    where, rows_ref, ups_ref, weights_ref, down_ref = refs[:5]
    rest = refs[5 + aliased :]
    results_ref, row_grads_ref, weight_grads_ref, down_grad_ref, sums, down_sum = rest
    tile = pl.program_id(1)
    width = FF // parts

    weights = weights_ref[...].reshape(D, 2 * width)
    tokens = rows_ref[0, :, :D]
    both = matmul(tokens, weights, ((1,), (0,)))
    gate_value = both[:, :width]
    up_value = both[:, width:]
    sigma = 1.0 / (1.0 + jnp.exp(-gate_value))
    silu = gate_value * sigma
    hidden = (silu * up_value).astype(BF)
    down = down_ref[0]
    results = matmul(hidden, down, ((1,), (0,)))

    expert = where[1] + start + pl.program_id(0)
    lane = lax.broadcasted_iota(jnp.int32, (rows_ref.shape[1], LANES), 1)
    high = lane == expert
    low = lane == expert + E
    probs = rows_ref[0, :, D:].astype(F32)
    weight = jnp.sum(jnp.where(high | low, probs, 0.0), axis=1, keepdims=True)
    upstream = ups_ref[0].astype(F32)
    gate_grad = jnp.sum(upstream * results, axis=1, keepdims=True)
    results_ref[0] = (weight * results).astype(BF)
    result_grads = (weight * upstream).astype(BF)

    hidden_grads = matmul(result_grads, down, ((1,), (1,)))
    gate_value_grads = (
        hidden_grads * up_value * (sigma * (1.0 + gate_value * (1.0 - sigma)))
    ).astype(BF)
    up_value_grads = (hidden_grads * silu).astype(BF)
    both_grads = jnp.concatenate([gate_value_grads, up_value_grads], axis=1)
    row_grads_ref[0, :, :D] = matmul(both_grads, weights, ((1,), (1,))).astype(BF)
    top = gate_grad.astype(BF)
    bottom = (gate_grad - top.astype(F32)).astype(BF)
    row_grads_ref[0, :, D:] = jnp.where(
        high, top.astype(F32), jnp.where(low, bottom.astype(F32), 0.0)
    ).astype(BF)

    term = matmul(tokens, both_grads, ((0,), (0,)))
    down_term = matmul(hidden, result_grads, ((0,), (0,)))

    @pl.when(tile == 0)
    def _():
        sums[...] = term
        down_sum[...] = down_term

    @pl.when(tile > 0)
    def _():
        sums[...] += term
        down_sum[...] += down_term

    @pl.when(tile == tiles - 1)
    def _():
        weight_grads_ref[...] = sums[...].astype(BF).reshape(weight_grads_ref.shape)
        down_grad_ref[0] = down_sum[...]


def expert_chunk(where, rows, ups, weights, down, start, down_grad, group, at, grads):
    parts, experts, depth, width2 = weights.shape
    local, total_rows, wide_row = rows.shape
    tile = 384
    tiles = total_rows // tile
    slice_ff = down.shape[1]
    weight_spec = pl.BlockSpec((parts, 1, depth, width2), lambda e, i, c: (0, e, 0, 0))
    down_spec = pl.BlockSpec((1, slice_ff, D), lambda e, i, c: (start + e, 0, 0))
    in_specs = [
        pl.BlockSpec((1, tile, wide_row), lambda e, i, c: (start + e, i, 0)),
        pl.BlockSpec((1, tile, D), lambda e, i, c: (start + e, i, 0)),
        weight_spec,
        down_spec,
    ]
    args = [where, rows, ups, weights, down]
    aliases = {}
    for buffer, index in ((down_grad, 3), (grads, 2)):
        if buffer is not None:
            in_specs.append(pl.BlockSpec(memory_space=pl.ANY))
            aliases[len(args)] = index
            args.append(buffer)
    return pl.pallas_call(
        functools.partial(expert_body, parts, tiles, start, len(aliases)),
        grid_spec=pltpu.PrefetchScalarGridSpec(
            num_scalar_prefetch=1,
            grid=(experts, tiles),
            in_specs=in_specs,
            out_specs=[
                pl.BlockSpec((1, tile, D), lambda e, i, c: (e, i, 0)),
                pl.BlockSpec((1, tile, wide_row), lambda e, i, c: (e, i, 0)),
                pl.BlockSpec((parts, 1, depth, width2), lambda e, i, c: (0, at + e, 0, 0)),
                down_spec,
            ],
            scratch_shapes=[
                pltpu.VMEM((parts * depth, width2), F32),
                pltpu.VMEM((slice_ff, D), F32),
            ],
        ),
        out_shape=[
            jax.ShapeDtypeStruct((experts, total_rows, D), BF),
            jax.ShapeDtypeStruct((experts, total_rows, wide_row), BF),
            jax.ShapeDtypeStruct((parts, group, depth, width2), BF),
            jax.ShapeDtypeStruct((local, slice_ff, D), F32),
        ],
        input_output_aliases=aliases,
        compiler_params=pltpu.CompilerParams(vmem_limit_bytes=VMEM_BYTES),
        cost_estimate=pl.CostEstimate(
            flops=18 * experts * total_rows * D * slice_ff,
            bytes_accessed=8 * experts * total_rows * D + 18 * experts * D * slice_ff,
            transcendentals=experts * total_rows * slice_ff,
        ),
        name="experts",
    )(*args)


def slice_body(parts, width, gate_ref, up_ref, out):
    for s in range(parts):
        columns = slice(s * width, (s + 1) * width)
        out[s, 0, :, :width] = gate_ref[0, :, columns]
        out[s, 0, :, width:] = up_ref[0, :, columns]


def slice_weights(gate, up, start, experts, parts):
    depth = gate.shape[1]
    width = FF // parts
    spec = pl.BlockSpec((1, depth, FF), lambda e: (start + e, 0, 0))
    return pl.pallas_call(
        functools.partial(slice_body, parts, width),
        grid=(experts,),
        in_specs=[spec, spec],
        out_specs=pl.BlockSpec((parts, 1, depth, 2 * width), lambda e: (0, e, 0, 0)),
        out_shape=jax.ShapeDtypeStruct((parts, experts, depth, 2 * width), BF),
        compiler_params=pltpu.CompilerParams(vmem_limit_bytes=VMEM_BYTES),
        cost_estimate=pl.CostEstimate(
            flops=0, bytes_accessed=8 * experts * depth * FF, transcendentals=0
        ),
        name="slice_weights",
    )(gate, up)


def assemble_body(parts, width, *refs):
    source = refs[0]
    gate_ref, up_ref = refs[-2], refs[-1]
    for s in range(parts):
        columns = slice(s * width, (s + 1) * width)
        gate_ref[0, :, columns] = source[s, 0, :, :width].astype(F32)
        up_ref[0, :, columns] = source[s, 0, :, width:].astype(F32)


def assemble(source, start, local, buffers):
    parts, experts, depth, width2 = source.shape
    in_specs = [pl.BlockSpec((parts, 1, depth, width2), lambda e: (0, e, 0, 0))]
    args = [source]
    aliases = {}
    if buffers is not None:
        in_specs += [pl.BlockSpec(memory_space=pl.ANY)] * 2
        aliases = {1: 0, 2: 1}
        args += list(buffers)
    spec = pl.BlockSpec((1, depth, FF), lambda e: (start + e, 0, 0))
    return pl.pallas_call(
        functools.partial(assemble_body, parts, width2 // 2),
        grid=(experts,),
        in_specs=in_specs,
        out_specs=[spec, spec],
        out_shape=[jax.ShapeDtypeStruct((local, depth, FF), F32)] * 2,
        input_output_aliases=aliases,
        compiler_params=pltpu.CompilerParams(vmem_limit_bytes=VMEM_BYTES),
        cost_estimate=pl.CostEstimate(
            flops=0, bytes_accessed=6 * experts * depth * FF * 2, transcendentals=0
        ),
        name="assemble",
    )(*args)


def pick_body(where, *refs):
    out = refs[-1]
    for i, source in enumerate(refs[:-1]):
        at = 0 if i == 0 else out.shape[1] - 1
        out[0, at : at + source.shape[0]] = source[:, 0]


def pick_blocks(order, *sources):
    _, _, rows, width = sources[0].shape
    count = order.shape[0]
    outer = sum(x.shape[0] for x in sources)
    return pl.pallas_call(
        pick_body,
        grid_spec=pltpu.PrefetchScalarGridSpec(
            num_scalar_prefetch=1,
            grid=(count,),
            in_specs=[
                pl.BlockSpec((x.shape[0], 1, rows, width), lambda k, c: (0, c[k], 0, 0))
                for x in sources
            ],
            out_specs=pl.BlockSpec((1, outer, rows, width), lambda k, c: (k, 0, 0, 0)),
        ),
        out_shape=jax.ShapeDtypeStruct((count, outer, rows, width), BF),
        compiler_params=pltpu.CompilerParams(vmem_limit_bytes=VMEM_BYTES),
        cost_estimate=pl.CostEstimate(
            flops=0, bytes_accessed=4 * count * outer * rows * width, transcendentals=0
        ),
        name="pick_blocks",
    )(order, *sources)


def tie(value, *after):
    return lax.optimization_barrier((value, *after))[0]


def split_low(x):
    top = x.astype(BF)
    return top, (x - top.astype(F32)).astype(BF)


def add_up(parts):
    total = parts[0].astype(F32)
    for part in parts[1:]:
        total = total + part.astype(F32)
    return total


def make_on_device(wide, narrow):
    planes = wide // 2
    local = E // wide
    heads = H // wide
    features = heads * HD
    if local == 8:
        sizes, early, groups = [2, 1, 1, 2, 2], 3, [[0], [1, 2, 3], [4]]
    else:
        sizes = [1] * local
        early, groups = min(2, local), [[c] for c in range(local)]
    calls = len(sizes)
    starts = [sum(sizes[:c]) for c in range(calls)]
    slice_ff = FF // narrow
    both_axes = ("wide", "narrow")

    def swap(x, axis, r):
        size = wide if axis == "wide" else narrow
        return lax.ppermute(x, axis, [(i, i ^ r) for i in range(size)])

    bits = [1 << i for i in reversed(range(narrow.bit_length() - 1))]
    near = [0]
    for bit in bits:
        near = near + [r ^ bit for r in near]

    def gather_narrow(x, *after):
        for i, bit in enumerate(bits):
            if i and after:
                x = tie(x, *after)
            x = jnp.concatenate([x, swap(x, "narrow", bit)], axis=0)
        return x

    def scatter_narrow(keep, send, *after):
        first = None
        for bit in reversed(bits):
            total = keep.astype(F32) + swap(send, "narrow", bit).astype(F32)
            first = total if first is None else first
            half = total.shape[0] // 2
            keep, send = total[:half], total[half:].astype(BF)
            if after:
                send = tie(send, *after)
        return total[0], first

    def gather_planes(x):
        return [x] + [swap(x, "wide", 2 * q) for q in range(1, planes)]

    def cross(pieces):
        return [swap(piece, "wide", 1) for piece in pieces]

    def gather_wide(x):
        own = gather_planes(x)
        return own, cross(own)

    def join(own, other):
        return jnp.concatenate([piece for pair in zip(own, other) for piece in pair], axis=0)

    def scatter_wide(own, other):
        return scatter_plane(own, swap(other, "wide", 1))[0]

    def scatter_plane(own, came, *after):
        sums = [own[q].astype(F32) + came[q].astype(F32) for q in range(planes)]
        sent = [x.astype(BF) for x in sums[1:]]
        if after:
            sent = list(lax.optimization_barrier((*sent, *after))[: planes - 1])
        total = sums[0]
        for q in range(1, planes):
            total = total + swap(sent[q - 1], "wide", 2 * q).astype(F32)
        return total, sent

    def on_device(
        tokens, positions, routes, cotangent,
        w_query, w_key, w_value, w_output, w_router,
        gain_attn, gain_query, gain_key, gain_ffn,
        w_gate, w_up, w_down,
    ):
        count = tokens.shape[0]
        rows = w_query.shape[0]
        w = lax.axis_index("wide")
        n = lax.axis_index("narrow")
        where = jnp.stack([n, w * local, w]).astype(jnp.int32)
        wide_order = jnp.arange(wide) ^ w
        near_order = jnp.array(near) ^ n
        narrow_order = jnp.array([near.index(r) for r in range(narrow)])[jnp.arange(narrow) ^ n]

        def by_narrow(*x):
            half = narrow // 2
            send = pick_blocks(near_order[half:], *x)
            return pick_blocks(near_order[:half], *x), send

        routed = jnp.any(
            routes[:, :, None] == jnp.arange(E, dtype=jnp.int32)[None, None, :], axis=1
        )
        earlier = matmul(
            jnp.tril(jnp.ones((count, count), BF), -1), routed.astype(BF), ((1,), (0,))
        )
        slots = jnp.where(routed, earlier, -1.0).astype(BF).T

        small = jnp.concatenate(
            [
                w_router.reshape(-1), gain_attn, gain_query, gain_key, gain_ffn,
                positions.astype(BF),
            ]
        )
        small_rows = -(-small.shape[0] // LANES)
        bundle_rows = -(-(E + small_rows) // 16) * 16
        small = jnp.pad(small, (0, (bundle_rows - E) * LANES - small.shape[0]))
        bundle = jnp.concatenate([slots, small.reshape(-1, LANES)], axis=0)
        bundle_z = lax.all_gather(bundle, "narrow")
        stacked = jnp.concatenate(
            [x.reshape(rows, wide, features) for x in (w_query, w_key, w_value)], axis=-1
        ).transpose(1, 0, 2)
        columns = lax.all_to_all(stacked, "wide", 0, 0, tiled=True)
        bundles = lax.all_gather(bundle_z, "wide")
        all_slots = bundles[:, :, :E, :]
        all_small = bundles[:, :, E:, :].reshape(wide, narrow, -1)
        base = rows * E
        plane_positions = lax.dynamic_index_in_dim(
            all_small[:, :, base + 4 * rows : base + 4 * rows + count], n, 1, keepdims=False
        )
        plane_positions = jnp.take(plane_positions, wide_order, axis=0).reshape(wide * count)
        router_full = all_small[:, :, :base].reshape(D, E)
        gains = [
            all_small[:, :, base + i * rows : base + (i + 1) * rows].reshape(D).astype(F32)
            for i in range(4)
        ]
        attn_gain, query_gain, key_gain, ffn_gain = gains
        query_gain = lax.dynamic_slice_in_dim(query_gain, w * features, features)
        key_gain = lax.dynamic_slice_in_dim(key_gain, w * features, features)
        expert_counts = jnp.sum((all_slots >= 0).astype(jnp.int32), axis=(0, 1, 3))

        tokens_near = gather_wide(tokens)
        plane_tokens = join(*tokens_near).astype(F32)
        plane_count = plane_tokens.shape[0]

        sliced = [
            slice_weights(w_gate, w_up, starts[c], sizes[c], narrow) for c in range(calls)
        ]
        expert_weights = []

        def send_weights(*after):
            part = tie(sliced[len(expert_weights)], *after)
            expert_weights.append(lax.all_to_all(part, "narrow", 0, 0, tiled=True))

        ups_z = gather_narrow(cotangent, bundle_z)
        send_weights(columns, bundles, ups_z)
        ups_own = gather_planes(tie(ups_z, *tokens_near[0], *tokens_near[1]))
        columns, w_output = lax.optimization_barrier(
            (columns, w_output, expert_weights[0], *tokens_near[0], *tokens_near[1], *ups_own[:3])
        )[:2]
        columns = gather_narrow(columns[None])
        columns = jnp.take(columns, narrow_order, axis=0)
        qkv = columns.transpose(1, 0, 2, 3).reshape(D, 3 * features)
        output_rows = gather_narrow(w_output[None])
        output_rows = jnp.take(output_rows, narrow_order, axis=0).reshape(features, D)
        while len(expert_weights) < early:
            send_weights(qkv, output_rows, *expert_weights[1:])

        local_slots = lax.dynamic_slice_in_dim(all_slots, w * local, local, axis=2)
        local_slots = jnp.take(jnp.take(local_slots, wide_order, axis=0), near_order, axis=1)
        pairs = narrow // 2
        local_slots = (
            local_slots.reshape(planes, 2, pairs, 2, local, count)
            .transpose(1, 0, 2, 4, 3, 5)
            .reshape(2, planes, pairs, local, 1, 2 * count)
        )
        row = jnp.arange(2 * CAP)[:, None]
        lane = jnp.arange(2 * count)[None, :]
        picks = (
            ((local_slots == (row % CAP).astype(BF)) & (row // CAP == lane // count))
            .astype(BF)
            .reshape(2, planes, pairs, local * 2 * CAP, 2 * count)
        )
        picks_own, picks_other = picks[0], picks[1]
        inverse = lax.rsqrt(jnp.mean(plane_tokens * plane_tokens, axis=-1, keepdims=True) + EPSILON)
        normed = (plane_tokens * inverse * attn_gain).astype(BF)
        raw = matmul(normed, tie(qkv, *ups_own), ((1,), (0,)))
        query_raw = raw[:, :features]
        key_raw = raw[:, features : 2 * features]
        values = raw[:, 2 * features :].astype(BF).reshape(wide, count, heads, HD)

        def row_sums(a, b):
            sums = jnp.stack([jnp.sum(a, axis=-1), jnp.sum(b, axis=-1)])
            sums = jnp.take(sums.reshape(2, wide, count), wide_order, axis=1)
            sums = jnp.sum(lax.all_gather(sums, "wide"), axis=0)
            sums = jnp.take(sums, wide_order, axis=1).reshape(2, plane_count)
            return sums[0][:, None], sums[1][:, None]

        query_square, key_square = row_sums(query_raw * query_raw, key_raw * key_raw)
        query_r = lax.rsqrt(query_square / D + EPSILON)
        key_r = lax.rsqrt(key_square / D + EPSILON)
        frequency = THETA_BASE ** (-2.0 * jnp.arange(HD // 2, dtype=F32) / HD)
        angles = plane_positions.astype(F32)[:, None] * frequency[None, :]
        cosine = jnp.cos(angles)[:, None, :]
        sine = jnp.sin(angles)[:, None, :]

        def turn(x, sign):
            x = x.reshape(plane_count, heads, HD)
            a, b = x[..., : HD // 2], x[..., HD // 2 :]
            return jnp.concatenate(
                [a * cosine - sign * b * sine, b * cosine + sign * a * sine], axis=-1
            )

        shape = (wide, count, heads, HD)
        queries = turn(query_raw * query_r * query_gain, 1.0).astype(BF).reshape(shape)
        key_rows = turn(key_raw * key_r * key_gain, 1.0).astype(BF).reshape(shape)
        if early > 2:
            queries = tie(queries, expert_weights[1])
        scale = HD ** (-0.5)
        causal = (jnp.arange(count)[:, None] >= jnp.arange(count)[None, :])[None, None]
        scores = (
            jnp.einsum("bqhd,bkhd->bhqk", queries, key_rows, preferred_element_type=F32) * scale
        )
        scores = jnp.where(causal, scores, -1e30)
        powers = jnp.exp(scores - jnp.max(scores, axis=-1, keepdims=True))
        attn_probs = powers / jnp.sum(powers, axis=-1, keepdims=True)
        probs_low = attn_probs.astype(BF)
        attended = (
            jnp.einsum("bhqk,bkhd->bqhd", probs_low, values, preferred_element_type=F32)
            .astype(BF)
            .reshape(plane_count, features)
        )
        branch = matmul(attended, output_rows, ((1,), (0,))).astype(BF)
        branch = branch.reshape(planes, 2, count, D)
        branch = scatter_wide(branch[:, 0], branch[:, 1])

        residual = tokens.astype(F32) + branch
        ffn_r = lax.rsqrt(jnp.mean(residual * residual, axis=-1, keepdims=True) + EPSILON)
        normed_ffn = (residual * ffn_r * ffn_gain).astype(BF)
        logits = matmul(normed_ffn, router_full, ((1,), (0,)))
        router_powers = jnp.exp(logits - jnp.max(logits, axis=-1, keepdims=True))
        router_probs = router_powers / jnp.sum(router_powers, axis=-1, keepdims=True)

        message = jnp.concatenate([normed_ffn, *split_low(router_probs)], axis=1)
        ups = dispatch(picks_own, ups_own, 0)
        ups = dispatch(picks_other, cross(ups_own), 1, ups)
        message = gather_narrow(tie(message, ups, expert_weights[-1]))
        if calls > early:
            send_weights(message)
        tokens_own = gather_planes(message)
        while len(expert_weights) < calls:
            send_weights(*tokens_own)
        tokens_own[0] = tie(tokens_own[0], expert_weights[min(early, calls - 1)])
        tokens_other = cross(tokens_own)
        expert_rows = dispatch(picks_own, tokens_own, 0)
        expert_rows = dispatch(picks_other, tokens_other, 1, expert_rows)

        results, row_grads, came = [], [], []
        down_grad = None
        for c in range(calls):
            if c == 1:
                expert_rows = tie(expert_rows, expert_weights[-1])
            group = next(g for g in groups if c in g)
            grads = came[-1] if c != group[0] else None
            result, row_grad, grads, down_grad = expert_chunk(
                where, expert_rows, ups, expert_weights[c], w_down, starts[c], down_grad,
                sum(sizes[g] for g in group), starts[c] - starts[group[0]], grads,
            )
            results.append(result)
            row_grads.append(row_grad)
            if c == group[0]:
                came.append(grads)
            else:
                came[-1] = grads
        buffers, arrived = [None], []

        def send_grads(*after):
            g = len(buffers) - 1
            part = tie(came[g], *after) if after else came[g]
            part = lax.all_to_all(part, "narrow", 0, 0, tiled=True)
            arrived.append(part)
            buffers.append(assemble(part, starts[groups[g][0]], local, buffers[-1]))

        for g in range(len(groups) - 1):
            send_grads(*([row_grads[-1]] if g else []))

        def combine_tokens(terms, *after):
            terms = [tie(terms[0], *after), *terms[1:]] if after else terms
            other = combine(picks_other, terms, 1)
            other = [swap(x, "wide", 1) for x in other]
            return list(combine(picks_own, terms, 0)), other

        def scatter_rest(plane_sum):
            blocks = plane_sum.reshape(narrow, count, plane_sum.shape[-1])
            return scatter_narrow(blocks[: narrow // 2], blocks[narrow // 2 :])[0]

        own, other = combine_tokens(row_grads)
        plane_sum, sent = scatter_plane(own, other)
        mix_own, mix_other = combine_tokens(results, *sent)
        mix_sums = [mix_own[q].astype(F32) + mix_other[q].astype(F32) for q in range(planes)]
        mix_sent = [x.astype(BF) for x in mix_sums[1:]]
        plane_sum = tie(plane_sum.astype(BF), *arrived, *mix_sent)
        ffn_message = scatter_rest(plane_sum)
        send_grads(ffn_message)

        upstream = cotangent.astype(F32)
        prob_grads = ffn_message[:, D : D + E] + ffn_message[:, D + E : D + 2 * E]
        logit_grads = (
            router_probs
            * (prob_grads - jnp.sum(router_probs * prob_grads, axis=-1, keepdims=True))
        ).astype(BF)
        ffn_grads = ffn_message[:, :D] + matmul(logit_grads, router_full, ((1,), (1,)))

        def norm_back(v, r, gain, dy):
            u = dy * gain
            return r * u - v * (r * r * r) * jnp.mean(u * v, axis=-1, keepdims=True)

        residual_grads = upstream + norm_back(residual, ffn_r, ffn_gain, ffn_grads)
        ffn_gain_part = jnp.sum(ffn_grads * residual * ffn_r, axis=0)
        message = jnp.concatenate(
            [residual_grads.astype(BF), logit_grads, jnp.zeros_like(logit_grads)], axis=1
        )

        plane_message = join(*gather_wide(message))
        mix_came = [swap(tie(mix_sent[0], plane_message), "wide", 2)]
        plane_grads = plane_message[:, :D]
        attended_grads = (
            matmul(plane_grads, output_rows, ((1,), (1,))).astype(BF).reshape(shape)
        )
        plane_rows = lax.dynamic_slice_in_dim(
            join([x[:count] for x in tokens_own], [x[:count] for x in tokens_other]),
            w * features,
            features,
            axis=1,
        )
        prob_grads_attn = jnp.einsum(
            "bqhd,bkhd->bhqk", attended_grads, values, preferred_element_type=F32
        )
        value_grads = (
            jnp.einsum("bhqk,bqhd->bkhd", probs_low, attended_grads, preferred_element_type=F32)
            .astype(BF)
            .reshape(plane_count, features)
        )
        score_grads = attn_probs * (
            prob_grads_attn - jnp.sum(attn_probs * prob_grads_attn, axis=-1, keepdims=True)
        )
        score_grads = jnp.where(causal, score_grads, 0.0).astype(BF)
        query_grads = (
            jnp.einsum("bhqk,bkhd->bqhd", score_grads, key_rows, preferred_element_type=F32)
            * scale
        )
        key_grads = (
            jnp.einsum("bhqk,bqhd->bkhd", score_grads, queries, preferred_element_type=F32)
            * scale
        )
        query_dy = turn(query_grads, -1.0).reshape(plane_count, features)
        key_dy = turn(key_grads, -1.0).reshape(plane_count, features)
        query_u = tie(query_dy, *mix_came) * query_gain
        key_u = key_dy * key_gain
        query_dot, key_dot = row_sums(query_u * query_raw, key_u * key_raw)
        query_raw_grads = query_r * query_u - query_raw * (query_r**3) * (query_dot / D)
        key_raw_grads = key_r * key_u - key_raw * (key_r**3) * (key_dot / D)
        mix_came += [
            swap(tie(mix_sent[q - 1], query_dot), "wide", 2 * q) for q in range(2, planes)
        ]
        raw_grads = jnp.concatenate(
            [query_raw_grads.astype(BF), key_raw_grads.astype(BF), value_grads], axis=1
        )
        normed_grads = matmul(raw_grads, qkv, ((1,), (1,))).astype(BF)
        raw_grads = tie(raw_grads, arrived[-1])

        grad_output = jnp.concatenate(
            [
                matmul(attended, plane_grads, ((0,), (0,))).astype(BF),
                matmul(plane_rows, plane_message[:, D:], ((0,), (0,))).astype(BF),
            ],
            axis=1,
        )
        grad_output, _ = scatter_narrow(
            *by_narrow(tie(grad_output, query_dot).reshape(1, narrow, rows, D + LANES))
        )
        grad_output = grad_output[0]

        attn_gain_part = jnp.sum(normed_grads.astype(F32) * plane_tokens * inverse, axis=0)
        grad_qkv = matmul(normed, raw_grads, ((0,), (0,))).astype(BF)
        grad_qkv = grad_qkv.reshape(wide, narrow, rows, 3 * features)
        gain_parts = jnp.concatenate(
            [
                jnp.stack([attn_gain_part, ffn_gain_part]).reshape(2 * wide, narrow, rows),
                jnp.stack(
                    [
                        jnp.sum(query_dy * query_raw * query_r, axis=0),
                        jnp.sum(key_dy * key_raw * key_r, axis=0),
                    ]
                ).reshape(2, narrow, rows),
            ]
        ).transpose(1, 2, 0)
        columns_each = 2 * wide + 2
        gain_parts = jnp.concatenate(split_low(gain_parts), axis=-1)
        gain_parts = jnp.pad(
            gain_parts, ((0, 0), (0, 0), (0, 3 * features - 2 * columns_each))
        )
        grad_qkv, first_sums = scatter_narrow(*by_narrow(grad_qkv, gain_parts[None]))
        gain_parts = grad_qkv[wide, :, :columns_each] + grad_qkv[wide, :, columns_each : 2 * columns_each]
        gain_parts = gain_parts.T
        grad_qkv = grad_qkv[:wide]
        grad_gain_query, grad_gain_key = gain_parts[2 * wide], gain_parts[2 * wide + 1]
        mix_came = list(lax.optimization_barrier((*mix_came, first_sums))[:-1])
        mixture = scatter_rest(add_up([mix_sums[0], *mix_came]).astype(BF))
        block_out = (residual + mixture).astype(BF)
        gain_rows = jnp.concatenate(
            [*split_low(gain_parts[:wide]), *split_low(gain_parts[wide : 2 * wide])], axis=1
        )
        gain_rows = jnp.pad(
            gain_rows[:, None, :], ((0, 0), (0, 15), (0, 3 * features - 4 * rows))
        )
        grad_qkv = jnp.concatenate([grad_qkv.astype(BF), gain_rows], axis=1)
        grad_qkv = lax.all_to_all(grad_qkv, "wide", 0, 0, tiled=True)
        gain_rows = jnp.sum(grad_qkv[:, rows, : 4 * rows].astype(F32), axis=0).reshape(4, rows)
        gain_sums = [gain_rows[0] + gain_rows[1], gain_rows[2] + gain_rows[3]]
        grad_qkv = grad_qkv[:, :rows].transpose(1, 0, 2).astype(F32)
        grad_query, grad_key, grad_value = [
            grad_qkv[..., i * features : (i + 1) * features].reshape(rows, D) for i in range(3)
        ]

        normed_grads = normed_grads.reshape(planes, 2, count, D)
        normed_grads, _ = scatter_plane(
            normed_grads[:, 0], swap(normed_grads[:, 1], "wide", 1), first_sums
        )
        input_grad = (
            residual_grads
            + norm_back(tokens.astype(F32), inverse[:count], attn_gain, normed_grads)
        ).astype(BF)

        grad_gate, grad_up = buffers[-1]

        return (
            block_out, input_grad, grad_query, grad_key, grad_value,
            grad_output[:, :D], grad_output[:, D : D + E],
            gain_sums[0], grad_gain_query, grad_gain_key, gain_sums[1],
            grad_gate, grad_up, down_grad, expert_counts,
        )

    return on_device


def solution(mesh):
    both = ("wide", "narrow")
    in_specs = (P(both, None), P(both), P(both, None), P(both, None))
    in_specs += (P(both, None),) * 5 + (P(both),) * 4 + (P("wide", "narrow", None),) * 3
    out_specs = (P(both, None),) * 7 + (P(both),) * 4 + (P("wide", "narrow", None),) * 3 + (P(),)
    return jax.shard_map(
        make_on_device(mesh.shape["wide"], mesh.shape["narrow"]),
        mesh=mesh,
        in_specs=in_specs,
        out_specs=out_specs,
        check_vma=False,
    )
```

```python
import functools

import jax
import jax.numpy as jnp
from jax import lax
from jax.experimental import pallas as pl
from jax.experimental.pallas import tpu as pltpu
from jax.sharding import PartitionSpec as P

D = 2048
H = 16
HD = 128
E = 64
TOPK = 8
CAP = 24
FF = 1024
LANES = 128
EPSILON = 1e-05
THETA_BASE = 10000.0

BF = jnp.bfloat16
F32 = jnp.float32
VMEM_BYTES = 56 * 1024 * 1024


def matmul(a, b, dims):
    return lax.dot_general(a, b, (dims, ((), ())), preferred_element_type=F32)


def dispatch_body(pieces, each, *refs):
    picks = refs[0]
    sources = refs[1 : 1 + pieces]
    out = refs[-1]
    for q in range(pieces):
        rows = matmul(picks[q, 0], sources[q][...], ((1,), (0,))).astype(BF)
        out[:, q * each : (q + 1) * each, :] = rows.reshape(-1, each, rows.shape[-1])


def dispatch(picks, sources, half, buffer=None):
    pieces, pairs, slots, span = picks.shape
    width = sources[0].shape[1]
    each = 2 * CAP
    block = pieces * each
    in_specs = [pl.BlockSpec((pieces, 1, slots, span), lambda j: (0, j, 0, 0))]
    in_specs += [pl.BlockSpec((span, width), lambda j: (j, 0))] * pieces
    args = [picks, *sources]
    aliases = {}
    if buffer is not None:
        in_specs.append(pl.BlockSpec(memory_space=pl.ANY))
        aliases = {len(args): 0}
        args.append(buffer)
    return pl.pallas_call(
        functools.partial(dispatch_body, pieces, each),
        grid=(pairs,),
        in_specs=in_specs,
        out_specs=pl.BlockSpec(
            (slots // each, block, width), lambda j: (0, half * pairs + j, 0)
        ),
        out_shape=jax.ShapeDtypeStruct((slots // each, 2 * pairs * block, width), BF),
        input_output_aliases=aliases,
        compiler_params=pltpu.CompilerParams(vmem_limit_bytes=VMEM_BYTES),
        cost_estimate=pl.CostEstimate(
            flops=2 * pieces * pairs * slots * span * width,
            bytes_accessed=2 * pieces * pairs * (slots + span) * width,
            transcendentals=0,
        ),
        name="dispatch",
    )(*args)


def combine_body(pieces, each, chunks, *refs):
    picks = refs[0]
    rows = refs[1 : 1 + chunks]
    outs = refs[1 + chunks :]
    for q in range(pieces):
        total = None
        at = 0
        for chunk in rows:
            part = chunk[:, q * each : (q + 1) * each, :].reshape(-1, chunk.shape[-1])
            size = part.shape[0]
            term = matmul(picks[q, 0, at : at + size, :], part, ((0,), (0,)))
            total = term if total is None else total + term
            at += size
        outs[q][...] = total.astype(BF)


def combine(picks, rows, half):
    pieces, pairs, slots, span = picks.shape
    each = 2 * CAP
    width = rows[0].shape[-1]
    in_specs = [pl.BlockSpec((pieces, 1, slots, span), lambda j: (0, j, 0, 0))]
    for chunk in rows:
        in_specs.append(
            pl.BlockSpec(
                (chunk.shape[0], pieces * each, width), lambda j: (0, half * pairs + j, 0)
            )
        )
    return pl.pallas_call(
        functools.partial(combine_body, pieces, each, len(rows)),
        grid=(pairs,),
        in_specs=in_specs,
        out_specs=[pl.BlockSpec((span, width), lambda j: (j, 0))] * pieces,
        out_shape=[jax.ShapeDtypeStruct((pairs * span, width), BF)] * pieces,
        compiler_params=pltpu.CompilerParams(vmem_limit_bytes=VMEM_BYTES),
        cost_estimate=pl.CostEstimate(
            flops=2 * pieces * pairs * slots * span * width,
            bytes_accessed=2 * pieces * pairs * (slots + span) * width,
            transcendentals=0,
        ),
        name="combine",
    )(picks, *rows)


def expert_body(parts, tiles, start, aliased, *refs):
    where, rows_ref, ups_ref, weights_ref, down_ref = refs[:5]
    rest = refs[5 + aliased :]
    results_ref, row_grads_ref, weight_grads_ref, down_grad_ref, sums, down_sum = rest
    tile = pl.program_id(1)
    width = FF // parts

    weights = weights_ref[...].reshape(D, 2 * width)
    tokens = rows_ref[0, :, :D]
    both = matmul(tokens, weights, ((1,), (0,)))
    gate_value = both[:, :width]
    up_value = both[:, width:]
    sigma = 1.0 / (1.0 + jnp.exp(-gate_value))
    silu = gate_value * sigma
    hidden = (silu * up_value).astype(BF)
    down = down_ref[0]
    results = matmul(hidden, down, ((1,), (0,)))

    expert = where[1] + start + pl.program_id(0)
    lane = lax.broadcasted_iota(jnp.int32, (rows_ref.shape[1], LANES), 1)
    high = lane == expert
    low = lane == expert + E
    probs = rows_ref[0, :, D:].astype(F32)
    weight = jnp.sum(jnp.where(high | low, probs, 0.0), axis=1, keepdims=True)
    upstream = ups_ref[0].astype(F32)
    gate_grad = jnp.sum(upstream * results, axis=1, keepdims=True)
    results_ref[0] = (weight * results).astype(BF)
    result_grads = (weight * upstream).astype(BF)

    hidden_grads = matmul(result_grads, down, ((1,), (1,)))
    gate_value_grads = (
        hidden_grads * up_value * (sigma * (1.0 + gate_value * (1.0 - sigma)))
    ).astype(BF)
    up_value_grads = (hidden_grads * silu).astype(BF)
    both_grads = jnp.concatenate([gate_value_grads, up_value_grads], axis=1)
    row_grads_ref[0, :, :D] = matmul(both_grads, weights, ((1,), (1,))).astype(BF)
    top = gate_grad.astype(BF)
    bottom = (gate_grad - top.astype(F32)).astype(BF)
    row_grads_ref[0, :, D:] = jnp.where(
        high, top.astype(F32), jnp.where(low, bottom.astype(F32), 0.0)
    ).astype(BF)

    term = matmul(tokens, both_grads, ((0,), (0,)))
    down_term = matmul(hidden, result_grads, ((0,), (0,)))

    @pl.when(tile == 0)
    def _():
        sums[...] = term
        down_sum[...] = down_term

    @pl.when(tile > 0)
    def _():
        sums[...] += term
        down_sum[...] += down_term

    @pl.when(tile == tiles - 1)
    def _():
        weight_grads_ref[...] = sums[...].astype(BF).reshape(weight_grads_ref.shape)
        down_grad_ref[0] = down_sum[...]


def expert_chunk(where, rows, ups, weights, down, start, down_grad, group, at, grads):
    parts, experts, depth, width2 = weights.shape
    local, total_rows, wide_row = rows.shape
    tile = 384
    tiles = total_rows // tile
    slice_ff = down.shape[1]
    weight_spec = pl.BlockSpec((parts, 1, depth, width2), lambda e, i, c: (0, e, 0, 0))
    down_spec = pl.BlockSpec((1, slice_ff, D), lambda e, i, c: (start + e, 0, 0))
    in_specs = [
        pl.BlockSpec((1, tile, wide_row), lambda e, i, c: (start + e, i, 0)),
        pl.BlockSpec((1, tile, D), lambda e, i, c: (start + e, i, 0)),
        weight_spec,
        down_spec,
    ]
    args = [where, rows, ups, weights, down]
    aliases = {}
    for buffer, index in ((down_grad, 3), (grads, 2)):
        if buffer is not None:
            in_specs.append(pl.BlockSpec(memory_space=pl.ANY))
            aliases[len(args)] = index
            args.append(buffer)
    return pl.pallas_call(
        functools.partial(expert_body, parts, tiles, start, len(aliases)),
        grid_spec=pltpu.PrefetchScalarGridSpec(
            num_scalar_prefetch=1,
            grid=(experts, tiles),
            in_specs=in_specs,
            out_specs=[
                pl.BlockSpec((1, tile, D), lambda e, i, c: (e, i, 0)),
                pl.BlockSpec((1, tile, wide_row), lambda e, i, c: (e, i, 0)),
                pl.BlockSpec((parts, 1, depth, width2), lambda e, i, c: (0, at + e, 0, 0)),
                down_spec,
            ],
            scratch_shapes=[
                pltpu.VMEM((parts * depth, width2), F32),
                pltpu.VMEM((slice_ff, D), F32),
            ],
        ),
        out_shape=[
            jax.ShapeDtypeStruct((experts, total_rows, D), BF),
            jax.ShapeDtypeStruct((experts, total_rows, wide_row), BF),
            jax.ShapeDtypeStruct((parts, group, depth, width2), BF),
            jax.ShapeDtypeStruct((local, slice_ff, D), F32),
        ],
        input_output_aliases=aliases,
        compiler_params=pltpu.CompilerParams(vmem_limit_bytes=VMEM_BYTES),
        cost_estimate=pl.CostEstimate(
            flops=18 * experts * total_rows * D * slice_ff,
            bytes_accessed=8 * experts * total_rows * D + 18 * experts * D * slice_ff,
            transcendentals=experts * total_rows * slice_ff,
        ),
        name="experts",
    )(*args)


def slice_body(parts, width, gate_ref, up_ref, out):
    for s in range(parts):
        columns = slice(s * width, (s + 1) * width)
        out[s, 0, :, :width] = gate_ref[0, :, columns]
        out[s, 0, :, width:] = up_ref[0, :, columns]


def slice_weights(gate, up, start, experts, parts):
    depth = gate.shape[1]
    width = FF // parts
    spec = pl.BlockSpec((1, depth, FF), lambda e: (start + e, 0, 0))
    return pl.pallas_call(
        functools.partial(slice_body, parts, width),
        grid=(experts,),
        in_specs=[spec, spec],
        out_specs=pl.BlockSpec((parts, 1, depth, 2 * width), lambda e: (0, e, 0, 0)),
        out_shape=jax.ShapeDtypeStruct((parts, experts, depth, 2 * width), BF),
        compiler_params=pltpu.CompilerParams(vmem_limit_bytes=VMEM_BYTES),
        cost_estimate=pl.CostEstimate(
            flops=0, bytes_accessed=8 * experts * depth * FF, transcendentals=0
        ),
        name="slice_weights",
    )(gate, up)


def assemble_body(parts, width, *refs):
    source = refs[0]
    gate_ref, up_ref = refs[-2], refs[-1]
    for s in range(parts):
        columns = slice(s * width, (s + 1) * width)
        gate_ref[0, :, columns] = source[s, 0, :, :width].astype(F32)
        up_ref[0, :, columns] = source[s, 0, :, width:].astype(F32)


def assemble(source, start, local, buffers):
    parts, experts, depth, width2 = source.shape
    in_specs = [pl.BlockSpec((parts, 1, depth, width2), lambda e: (0, e, 0, 0))]
    args = [source]
    aliases = {}
    if buffers is not None:
        in_specs += [pl.BlockSpec(memory_space=pl.ANY)] * 2
        aliases = {1: 0, 2: 1}
        args += list(buffers)
    spec = pl.BlockSpec((1, depth, FF), lambda e: (start + e, 0, 0))
    return pl.pallas_call(
        functools.partial(assemble_body, parts, width2 // 2),
        grid=(experts,),
        in_specs=in_specs,
        out_specs=[spec, spec],
        out_shape=[jax.ShapeDtypeStruct((local, depth, FF), F32)] * 2,
        input_output_aliases=aliases,
        compiler_params=pltpu.CompilerParams(vmem_limit_bytes=VMEM_BYTES),
        cost_estimate=pl.CostEstimate(
            flops=0, bytes_accessed=6 * experts * depth * FF * 2, transcendentals=0
        ),
        name="assemble",
    )(*args)


def turn(x, cosine, sine):
    return x * cosine + pltpu.roll(x, HD // 2, 1) * sine


def probabilities(query, key):
    scores = matmul(query, key, ((1,), (1,))) * HD ** (-0.5)
    row = lax.broadcasted_iota(jnp.int32, scores.shape, 0)
    column = lax.broadcasted_iota(jnp.int32, scores.shape, 1)
    causal = row >= column
    scores = jnp.where(causal, scores, -1e30)
    powers = jnp.exp(scores - jnp.max(scores, axis=-1, keepdims=True))
    return powers / jnp.sum(powers, axis=-1, keepdims=True), causal


def attend_body(raw, scales, cosine, sine, gains, turned, attended):
    features = attended.shape[1]
    for part in range(2):
        scale = scales[:, part : part + 1]
        for at in range(0, features, HD):
            columns = slice(part * features + at, part * features + at + HD)
            x = raw[:, columns] * scale * gains[part : part + 1, at : at + HD]
            turned[:, columns] = turn(x, cosine[...], sine[...]).astype(BF)
    turned[:, 2 * features :] = raw[:, 2 * features :].astype(BF)
    for at in range(0, features, HD):
        query = turned[:, at : at + HD]
        key = turned[:, features + at : features + at + HD]
        value = turned[:, 2 * features + at : 2 * features + at + HD]
        probs, _ = probabilities(query, key)
        attended[:, at : at + HD] = matmul(probs.astype(BF), value, ((1,), (0,))).astype(BF)


def attend(raw, scales, cosine, sine, gains, count):
    total, features = raw.shape[0], raw.shape[1] // 3

    def block(x):
        return pl.BlockSpec((count, x.shape[1]), lambda i: (i, 0))

    return pl.pallas_call(
        attend_body,
        grid=(total // count,),
        in_specs=[block(x) for x in (raw, scales, cosine, sine)]
        + [pl.BlockSpec(gains.shape, lambda i: (0, 0))],
        out_specs=[
            pl.BlockSpec((count, 3 * features), lambda i: (i, 0)),
            pl.BlockSpec((count, features), lambda i: (i, 0)),
        ],
        out_shape=[
            jax.ShapeDtypeStruct((total, 3 * features), BF),
            jax.ShapeDtypeStruct((total, features), BF),
        ],
        compiler_params=pltpu.CompilerParams(vmem_limit_bytes=VMEM_BYTES),
        cost_estimate=pl.CostEstimate(
            flops=4 * total * count * features,
            bytes_accessed=20 * total * features,
            transcendentals=total * count,
        ),
        name="attend",
    )(raw, scales, cosine, sine, gains)


def attend_back_body(turned, grads, raw, scales, cosine, sine, gains, scaled, value_grads, sums, gain_grads):
    features = grads.shape[1]
    scale = HD ** (-0.5)
    dots = [0.0, 0.0]
    first = pl.program_id(0) == 0
    for at in range(0, features, HD):
        query = turned[:, at : at + HD]
        key = turned[:, features + at : features + at + HD]
        value = turned[:, 2 * features + at : 2 * features + at + HD]
        grad = grads[:, at : at + HD]
        probs, causal = probabilities(query, key)
        value_grads[:, at : at + HD] = matmul(probs.astype(BF), grad, ((0,), (0,))).astype(BF)
        prob_grads = matmul(grad, value, ((1,), (1,)))
        score_grads = probs * (prob_grads - jnp.sum(probs * prob_grads, axis=-1, keepdims=True))
        score_grads = jnp.where(causal, score_grads, 0.0).astype(BF)
        turned_grads = (
            matmul(score_grads, key, ((1,), (0,))) * scale,
            matmul(score_grads, query, ((0,), (0,))) * scale,
        )
        for part in range(2):
            columns = slice(part * features + at, part * features + at + HD)
            x = raw[:, columns]
            dy = turn(turned_grads[part], cosine[...], -sine[...])
            u = dy * gains[part : part + 1, at : at + HD]
            scaled[:, columns] = u
            dots[part] = dots[part] + jnp.sum(u * x, axis=-1, keepdims=True)
            gain_grad = jnp.sum(dy * x * scales[:, part : part + 1], axis=0, keepdims=True)
            old = gain_grads[part : part + 1, at : at + HD]
            gain_grads[part : part + 1, at : at + HD] = gain_grad + jnp.where(first, 0.0, old)
    sums[...] = jnp.concatenate(dots, axis=1)


def attend_back(turned, grads, raw, scales, cosine, sine, gains, count):
    total, features = grads.shape

    def block(x):
        return pl.BlockSpec((count, x.shape[1]), lambda i: (i, 0))

    out_shape = [
        jax.ShapeDtypeStruct((total, 2 * features), F32),
        jax.ShapeDtypeStruct((total, features), BF),
        jax.ShapeDtypeStruct((total, 2), F32),
    ]
    return pl.pallas_call(
        attend_back_body,
        grid=(total // count,),
        in_specs=[block(x) for x in (turned, grads, raw, scales, cosine, sine)]
        + [pl.BlockSpec(gains.shape, lambda i: (0, 0))],
        out_specs=[block(x) for x in out_shape] + [pl.BlockSpec(gains.shape, lambda i: (0, 0))],
        out_shape=[*out_shape, jax.ShapeDtypeStruct(gains.shape, F32)],
        compiler_params=pltpu.CompilerParams(vmem_limit_bytes=VMEM_BYTES),
        cost_estimate=pl.CostEstimate(
            flops=12 * total * count * features,
            bytes_accessed=30 * total * features,
            transcendentals=total * count,
        ),
        name="attend_back",
    )(turned, grads, raw, scales, cosine, sine, gains)


def pick_body(where, *refs):
    out = refs[-1]
    width = out.shape[-1]
    at = 0
    for source in refs[:-1]:
        outer, _, _, own = source.shape
        if own >= width:
            for i in range(outer):
                for column in range(0, own, width):
                    out[0, at] = source[i, 0, :, column : column + width]
                    at += 1
        else:
            for i in range(0, outer, width // own):
                for k in range(width // own):
                    out[0, at, :, k * own : (k + 1) * own] = source[i + k, 0]
                at += 1


def pick_blocks(order, width, *sources):
    rows = sources[0].shape[2]
    count = order.shape[0]
    outer = sum(x.shape[0] * x.shape[3] for x in sources) // width
    return pl.pallas_call(
        pick_body,
        grid_spec=pltpu.PrefetchScalarGridSpec(
            num_scalar_prefetch=1,
            grid=(count,),
            in_specs=[
                pl.BlockSpec((x.shape[0], 1, *x.shape[2:]), lambda k, c: (0, c[k], 0, 0))
                for x in sources
            ],
            out_specs=pl.BlockSpec((1, outer, rows, width), lambda k, c: (k, 0, 0, 0)),
        ),
        out_shape=jax.ShapeDtypeStruct((count, outer, rows, width), BF),
        compiler_params=pltpu.CompilerParams(vmem_limit_bytes=VMEM_BYTES),
        cost_estimate=pl.CostEstimate(
            flops=0, bytes_accessed=4 * count * outer * rows * width, transcendentals=0
        ),
        name="pick_blocks",
    )(order, *sources)


def tie(value, *after):
    return lax.optimization_barrier((value, *after))[0]


def split_low(x):
    top = x.astype(BF)
    return top, (x - top.astype(F32)).astype(BF)


def add_up(parts):
    total = parts[0].astype(F32)
    for part in parts[1:]:
        total = total + part.astype(F32)
    return total


def make_on_device(wide, narrow):
    planes = wide // 2
    local = E // wide
    heads = H // wide
    features = heads * HD
    if local == 8:
        sizes, early, groups = [2, 1, 1, 2, 2], 3, [[0], [1, 2, 3], [4]]
    else:
        sizes = [1] * local
        early, groups = min(2, local), [[c] for c in range(local)]
    calls = len(sizes)
    starts = [sum(sizes[:c]) for c in range(calls)]
    slice_ff = FF // narrow
    both_axes = ("wide", "narrow")

    def swap(x, axis, r):
        size = wide if axis == "wide" else narrow
        return lax.ppermute(x, axis, [(i, i ^ r) for i in range(size)])

    bits = [1 << i for i in reversed(range(narrow.bit_length() - 1))]
    near = [0]
    for bit in bits:
        near = near + [r ^ bit for r in near]

    def gather_narrow(x, *after):
        for i, bit in enumerate(bits):
            if i and after:
                x = tie(x, *after)
            x = jnp.concatenate([x, swap(x, "narrow", bit)], axis=0)
        return x

    def scatter_narrow(keep, send, step=(), last=()):
        arrivals = []
        for bit in reversed(bits):
            came = swap(send, "narrow", bit)
            if last and bit == bits[0]:
                came = tie(came, *last)
            arrivals.append(came)
            total = keep.astype(F32) + came.astype(F32)
            half = total.shape[0] // 2
            keep, send = total[:half], total[half:].astype(BF)
            if step:
                send = tie(send, *step)
        return total[0], arrivals

    def gather_planes(x):
        return [x] + [swap(x, "wide", 2 * q) for q in range(1, planes)]

    def cross(pieces):
        return [swap(piece, "wide", 1) for piece in pieces]

    def gather_wide(x):
        own = gather_planes(x)
        return own, cross(own)

    def join(own, other):
        return jnp.concatenate([piece for pair in zip(own, other) for piece in pair], axis=0)

    def scatter_wide(own, other):
        return scatter_plane(own, swap(other, "wide", 1))[0]

    def scatter_plane(own, came, *after):
        sums = [own[q].astype(F32) + came[q].astype(F32) for q in range(planes)]
        sent = [x.astype(BF) for x in sums[1:]]
        if after:
            sent = list(lax.optimization_barrier((*sent, *after))[: planes - 1])
        total = sums[0]
        for q in range(1, planes):
            total = total + swap(sent[q - 1], "wide", 2 * q).astype(F32)
        return total, sent

    def on_device(
        tokens, positions, routes, cotangent,
        w_query, w_key, w_value, w_output, w_router,
        gain_attn, gain_query, gain_key, gain_ffn,
        w_gate, w_up, w_down,
    ):
        count = tokens.shape[0]
        rows = w_query.shape[0]
        w = lax.axis_index("wide")
        n = lax.axis_index("narrow")
        where = jnp.stack([n, w * local, w]).astype(jnp.int32)
        wide_order = jnp.arange(wide) ^ w
        near_order = jnp.array(near) ^ n
        narrow_order = jnp.array([near.index(r) for r in range(narrow)])[jnp.arange(narrow) ^ n]

        def by_narrow(*x):
            half = narrow // 2
            send = pick_blocks(near_order[half:], 2 * features, *x)
            return pick_blocks(near_order[:half], 2 * features, *x), send

        routed = jnp.any(
            routes[:, :, None] == jnp.arange(E, dtype=jnp.int32)[None, None, :], axis=1
        )
        earlier = matmul(
            jnp.tril(jnp.ones((count, count), BF), -1), routed.astype(BF), ((1,), (0,))
        )
        slots = jnp.where(routed, earlier, -1.0).astype(BF).T

        small = jnp.concatenate(
            [
                w_router.reshape(-1), gain_attn, gain_query, gain_key, gain_ffn,
                positions.astype(BF),
            ]
        )
        small_rows = -(-small.shape[0] // LANES)
        bundle_rows = -(-(E + small_rows) // 16) * 16
        small = jnp.pad(small, (0, (bundle_rows - E) * LANES - small.shape[0]))
        bundle = jnp.concatenate([slots, small.reshape(-1, LANES)], axis=0)
        bundle_z = lax.all_gather(bundle, "narrow")
        stacked = jnp.concatenate(
            [x.reshape(rows, wide, features) for x in (w_query, w_key, w_value)], axis=-1
        ).transpose(1, 0, 2)
        columns = lax.all_to_all(stacked, "wide", 0, 0, tiled=True)
        bundles = lax.all_gather(bundle_z, "wide")
        all_slots = bundles[:, :, :E, :]
        all_small = bundles[:, :, E:, :].reshape(wide, narrow, -1)
        base = rows * E
        plane_positions = lax.dynamic_index_in_dim(
            all_small[:, :, base + 4 * rows : base + 4 * rows + count], n, 1, keepdims=False
        )
        plane_positions = jnp.take(plane_positions, wide_order, axis=0).reshape(wide * count)
        router_full = all_small[:, :, :base].reshape(D, E)
        gains = [
            all_small[:, :, base + i * rows : base + (i + 1) * rows].reshape(D).astype(F32)
            for i in range(4)
        ]
        attn_gain, query_gain, key_gain, ffn_gain = gains
        query_gain = lax.dynamic_slice_in_dim(query_gain, w * features, features)
        key_gain = lax.dynamic_slice_in_dim(key_gain, w * features, features)
        expert_counts = jnp.sum((all_slots >= 0).astype(jnp.int32), axis=(0, 1, 3))

        tokens_near = gather_wide(tokens)
        plane_tokens = join(*tokens_near).astype(F32)
        plane_count = plane_tokens.shape[0]

        sliced = [
            slice_weights(w_gate, w_up, starts[c], sizes[c], narrow) for c in range(calls)
        ]
        expert_weights = []

        def send_weights(*after):
            part = tie(sliced[len(expert_weights)], *after)
            expert_weights.append(lax.all_to_all(part, "narrow", 0, 0, tiled=True))

        ups_z = gather_narrow(cotangent, bundle_z)
        send_weights(columns, bundles, ups_z)
        ups_own = gather_planes(tie(ups_z, *tokens_near[0], *tokens_near[1]))
        columns, w_output = lax.optimization_barrier(
            (columns, w_output, expert_weights[0], *tokens_near[0], *tokens_near[1], *ups_own[:3])
        )[:2]
        columns = gather_narrow(columns[None])
        columns = jnp.take(columns, narrow_order, axis=0)
        qkv = columns.transpose(1, 0, 2, 3).reshape(D, 3 * features)
        output_rows = gather_narrow(w_output[None])
        output_rows = jnp.take(output_rows, narrow_order, axis=0).reshape(features, D)
        while len(expert_weights) < early:
            send_weights(qkv, output_rows, *expert_weights[1:])

        local_slots = lax.dynamic_slice_in_dim(all_slots, w * local, local, axis=2)
        local_slots = jnp.take(jnp.take(local_slots, wide_order, axis=0), near_order, axis=1)
        pairs = narrow // 2
        local_slots = (
            local_slots.reshape(planes, 2, pairs, 2, local, count)
            .transpose(1, 0, 2, 4, 3, 5)
            .reshape(2, planes, pairs, local, 1, 2 * count)
        )
        row = jnp.arange(2 * CAP)[:, None]
        lane = jnp.arange(2 * count)[None, :]
        picks = (
            ((local_slots == (row % CAP).astype(BF)) & (row // CAP == lane // count))
            .astype(BF)
            .reshape(2, planes, pairs, local * 2 * CAP, 2 * count)
        )
        picks_own, picks_other = picks[0], picks[1]
        inverse = lax.rsqrt(jnp.mean(plane_tokens * plane_tokens, axis=-1, keepdims=True) + EPSILON)
        normed = (plane_tokens * inverse * attn_gain).astype(BF)
        raw = matmul(normed, tie(qkv, *ups_own), ((1,), (0,)))

        def row_sums(sums):
            sums = jnp.take(sums.reshape(2, wide, count), wide_order, axis=1)
            gathered = lax.all_gather(sums, "wide")
            sums = jnp.sum(gathered, axis=0)
            return jnp.take(sums, wide_order, axis=1).reshape(2, plane_count), gathered

        squares = jnp.stack(
            [
                jnp.sum(x * x, axis=-1)
                for x in (raw[:, :features], raw[:, features : 2 * features])
            ]
        )
        scales = lax.rsqrt(row_sums(squares)[0] / D + EPSILON).T
        frequency = THETA_BASE ** (-2.0 * jnp.arange(HD // 2, dtype=F32) / HD)
        angles = plane_positions.astype(F32)[:, None] * frequency[None, :]
        cosine, sine = jnp.cos(angles), jnp.sin(angles)
        cosine = jnp.concatenate([cosine, cosine], axis=1)
        sine = jnp.concatenate([-sine, sine], axis=1)
        head_gains = jnp.stack([query_gain, key_gain])
        turned, attended = attend(raw, scales, cosine, sine, head_gains, count)
        if early > 2:
            attended = tie(attended, expert_weights[1])
        branch = matmul(attended, output_rows, ((1,), (0,))).astype(BF)
        branch = branch.reshape(planes, 2, count, D)
        branch = scatter_wide(branch[:, 0], branch[:, 1])

        residual = tokens.astype(F32) + branch
        ffn_r = lax.rsqrt(jnp.mean(residual * residual, axis=-1, keepdims=True) + EPSILON)
        normed_ffn = (residual * ffn_r * ffn_gain).astype(BF)
        logits = matmul(normed_ffn, router_full, ((1,), (0,)))
        router_powers = jnp.exp(logits - jnp.max(logits, axis=-1, keepdims=True))
        router_probs = router_powers / jnp.sum(router_powers, axis=-1, keepdims=True)

        message = jnp.concatenate([normed_ffn, *split_low(router_probs)], axis=1)
        ups = dispatch(picks_own, ups_own, 0)
        ups = dispatch(picks_other, cross(ups_own), 1, ups)
        message = gather_narrow(tie(message, ups, expert_weights[-1]))
        if calls > early:
            send_weights(message)
        tokens_own = gather_planes(message)
        while len(expert_weights) < calls:
            send_weights(*tokens_own)
        tokens_own[0] = tie(tokens_own[0], expert_weights[min(early, calls - 1)])
        tokens_other = cross(tokens_own)
        expert_rows = dispatch(picks_own, tokens_own, 0)
        expert_rows = dispatch(picks_other, tokens_other, 1, expert_rows)

        results, row_grads, came = [], [], []
        down_grad = None
        for c in range(calls):
            if c == 1:
                expert_rows = tie(expert_rows, expert_weights[-1])
            group = next(g for g in groups if c in g)
            grads = came[-1] if c != group[0] else None
            result, row_grad, grads, down_grad = expert_chunk(
                where, expert_rows, ups, expert_weights[c], w_down, starts[c], down_grad,
                sum(sizes[g] for g in group), starts[c] - starts[group[0]], grads,
            )
            results.append(result)
            row_grads.append(row_grad)
            if c == group[0]:
                came.append(grads)
            else:
                came[-1] = grads
        arrived = []

        def send_grads(*after):
            part = came[len(arrived)]
            part = tie(part, *after) if after else part
            arrived.append(lax.all_to_all(part, "narrow", 0, 0, tiled=True))

        grad_starts = [starts[group[0]] for group in groups]
        sent_early = len(groups) - 1
        for g in range(sent_early):
            send_grads(*([row_grads[-1]] if g else []))

        def combine_tokens(terms, *after):
            terms = [tie(terms[0], *after), *terms[1:]] if after else terms
            other = combine(picks_other, terms, 1)
            other = [swap(x, "wide", 1) for x in other]
            return list(combine(picks_own, terms, 0)), other

        def scatter_rest(plane_sum, *after):
            blocks = plane_sum.reshape(narrow, count, plane_sum.shape[-1])
            return scatter_narrow(blocks[: narrow // 2], blocks[narrow // 2 :], (), after)[0]

        own, other = combine_tokens(row_grads)
        plane_sum, sent = scatter_plane(own, other)
        mix_own, mix_other = combine_tokens(results, *sent)
        mix_sums = [mix_own[q].astype(F32) + mix_other[q].astype(F32) for q in range(planes)]
        mix_sent = [x.astype(BF) for x in mix_sums[1:]]
        plane_done = plane_sum.astype(BF)
        plane_sum = tie(plane_done, *arrived, *mix_other)
        mix_came = [
            swap(tie(mix_sent[q - 1], plane_done), "wide", 2 * q) for q in range(1, planes)[:2]
        ]
        ffn_message = scatter_rest(plane_sum, *mix_came)
        send_grads(ffn_message)
        buffers = None
        for start, part in zip(grad_starts, arrived[:sent_early]):
            buffers = assemble(part, start, local, buffers)
        ffn_message = tie(ffn_message, *buffers)

        upstream = cotangent.astype(F32)
        prob_grads = ffn_message[:, D : D + E] + ffn_message[:, D + E : D + 2 * E]
        logit_grads = (
            router_probs
            * (prob_grads - jnp.sum(router_probs * prob_grads, axis=-1, keepdims=True))
        ).astype(BF)
        ffn_grads = ffn_message[:, :D] + matmul(logit_grads, router_full, ((1,), (1,)))

        def norm_back(v, r, gain, dy):
            u = dy * gain
            return r * u - v * (r * r * r) * jnp.mean(u * v, axis=-1, keepdims=True)

        residual_grads = upstream + norm_back(residual, ffn_r, ffn_gain, ffn_grads)
        ffn_gain_part = jnp.sum(ffn_grads * residual * ffn_r, axis=0)
        message = jnp.concatenate(
            [residual_grads.astype(BF), logit_grads, jnp.zeros_like(logit_grads)], axis=1
        )

        plane_message = join(*gather_wide(message))
        plane_grads = plane_message[:, :D]
        attended_grads = matmul(plane_grads, output_rows, ((1,), (1,))).astype(BF)
        plane_rows = lax.dynamic_slice_in_dim(
            join([x[:count] for x in tokens_own], [x[:count] for x in tokens_other]),
            w * features,
            features,
            axis=1,
        )
        scaled, value_grads, dots, head_gain_parts = attend_back(
            turned, attended_grads, raw, scales, cosine, sine, head_gains, count
        )

        grad_output = matmul(attended, plane_grads, ((0,), (0,))).astype(BF)
        grad_value = matmul(normed, value_grads, ((0,), (0,))).astype(BF)
        early_parts = by_narrow(
            grad_output.reshape(1, narrow, rows, D),
            grad_value.reshape(wide, narrow, rows, features),
        )

        dots, dots_gathered = row_sums(dots.T)
        dots = dots.T / D
        shrink = scales * scales * scales * dots
        raw_grads = (
            scaled.reshape(plane_count, 2, features) * scales[:, :, None]
            - raw[:, : 2 * features].reshape(plane_count, 2, features) * shrink[:, :, None]
        ).astype(BF)
        raw_grads = jnp.concatenate([raw_grads.reshape(plane_count, 2 * features), value_grads], axis=1)
        mix_came += [
            swap(tie(mix_sent[q - 1], dots_gathered), "wide", 2 * q) for q in range(3, planes)
        ]
        grad_early, early_came = scatter_narrow(*early_parts)
        raw_grads = tie(raw_grads, arrived[-1], early_came[0])
        normed_grads = matmul(raw_grads, qkv, ((1,), (1,))).astype(BF)

        attn_gain_part = jnp.sum(normed_grads.astype(F32) * plane_tokens * inverse, axis=0)
        gain_parts = jnp.concatenate(
            [
                jnp.stack([attn_gain_part, ffn_gain_part]).reshape(2 * wide, features),
                head_gain_parts,
            ]
        ).T
        gain_columns = 2 * wide + 2
        router_part = matmul(plane_rows, plane_message[:, D : D + E], ((0,), (0,)))
        small_parts = jnp.concatenate([router_part.astype(BF), *split_low(gain_parts)], axis=1)
        small_parts = jnp.pad(
            small_parts, ((0, 0), (0, 2 * features - E - 2 * gain_columns))
        )
        plane_normed = normed_grads.reshape(planes, 2, count, D)
        normed_other = swap(plane_normed[:, 1], "wide", 1)
        normed_sums = [add_up([plane_normed[q, 0], normed_other[q]]) for q in range(planes)]
        normed_came = [
            swap(normed_sums[q].astype(BF), "wide", 2 * q)
            for q in range(1, planes)
        ]
        grad_raw = matmul(normed, raw_grads[:, : 2 * features], ((0,), (0,))).astype(BF)
        grad_raw, raw_came = scatter_narrow(
            *by_narrow(
                grad_raw.reshape(wide, narrow, rows, 2 * features),
                small_parts.reshape(1, narrow, rows, 2 * features),
            ),
            (),
            normed_came,
        )
        small_parts = grad_raw[wide]
        grad_router = small_parts[:, :E]
        gain_parts = small_parts[:, E : E + 2 * gain_columns]
        gain_parts = (gain_parts[:, :gain_columns] + gain_parts[:, gain_columns:]).T
        grad_gain_query, grad_gain_key = gain_parts[2 * wide], gain_parts[2 * wide + 1]
        blocks = D // (2 * features)
        grad_output = jnp.concatenate([grad_early[i] for i in range(blocks)], axis=1)
        grad_value = (
            grad_early[blocks:]
            .reshape(wide // 2, rows, 2, features)
            .transpose(0, 2, 1, 3)
            .reshape(wide, rows, features)
        )
        grad_qkv = jnp.concatenate([grad_raw[:wide], grad_value], axis=-1)
        mix_came[-1] = tie(mix_came[-1], raw_came[0])
        mixture = add_up([mix_sums[0], *mix_came]).astype(BF)
        block_out = (residual + scatter_rest(mixture)).astype(BF)
        gain_rows = jnp.concatenate(
            [*split_low(gain_parts[:wide]), *split_low(gain_parts[wide : 2 * wide])], axis=1
        )
        gain_rows = jnp.pad(
            gain_rows[:, None, :], ((0, 0), (0, 15), (0, 3 * features - 4 * rows))
        )
        grad_qkv = jnp.concatenate([grad_qkv.astype(BF), gain_rows], axis=1)
        grad_qkv = lax.all_to_all(grad_qkv, "wide", 0, 0, tiled=True)
        gain_rows = jnp.sum(grad_qkv[:, rows, : 4 * rows].astype(F32), axis=0).reshape(4, rows)
        gain_sums = [gain_rows[0] + gain_rows[1], gain_rows[2] + gain_rows[3]]
        grad_qkv = grad_qkv[:, :rows].transpose(1, 0, 2).astype(F32)
        grad_query, grad_key, grad_value = [
            grad_qkv[..., i * features : (i + 1) * features].reshape(rows, D) for i in range(3)
        ]

        normed_grads = add_up([normed_sums[0], *normed_came])
        input_grad = (
            residual_grads
            + norm_back(tokens.astype(F32), inverse[:count], attn_gain, normed_grads)
        ).astype(BF)

        for start, part in zip(grad_starts[sent_early:], arrived[sent_early:]):
            buffers = assemble(tie(part, raw_came[0]), start, local, buffers)
        grad_gate, grad_up = buffers

        return (
            block_out, input_grad, grad_query, grad_key, grad_value,
            grad_output, grad_router,
            gain_sums[0], grad_gain_query, grad_gain_key, gain_sums[1],
            grad_gate, grad_up, down_grad, expert_counts,
        )

    return on_device


def solution(mesh):
    both = ("wide", "narrow")
    in_specs = (P(both, None), P(both), P(both, None), P(both, None))
    in_specs += (P(both, None),) * 5 + (P(both),) * 4 + (P("wide", "narrow", None),) * 3
    out_specs = (P(both, None),) * 7 + (P(both),) * 4 + (P("wide", "narrow", None),) * 3 + (P(),)
    return jax.shard_map(
        make_on_device(mesh.shape["wide"], mesh.shape["narrow"]),
        mesh=mesh,
        in_specs=in_specs,
        out_specs=out_specs,
        check_vma=False,
    )
```

```python
import functools

import jax
import jax.numpy as jnp
from jax import lax
from jax.experimental import pallas as pl
from jax.experimental.pallas import tpu as pltpu
from jax.sharding import PartitionSpec as P

D = 2048
H = 16
HD = 128
E = 64
TOPK = 8
CAP = 24
FF = 1024
LANES = 128
EXPERT_TILE = 768
EPSILON = 1e-05
THETA_BASE = 10000.0

BF = jnp.bfloat16
F32 = jnp.float32
VMEM_BYTES = 56 * 1024 * 1024


def matmul(a, b, dims):
    return lax.dot_general(a, b, (dims, ((), ())), preferred_element_type=F32)


def dispatch_body(pieces, each, *refs):
    picks = refs[0]
    sources = refs[1 : 1 + pieces]
    out = refs[-1]
    for q in range(pieces):
        rows = matmul(picks[q, 0], sources[q][...], ((1,), (0,))).astype(BF)
        out[:, q * each : (q + 1) * each, :] = rows.reshape(-1, each, rows.shape[-1])


def dispatch(picks, sources, half, buffer=None):
    pieces, pairs, slots, span = picks.shape
    width = sources[0].shape[1]
    each = 2 * CAP
    block = pieces * each
    in_specs = [pl.BlockSpec((pieces, 1, slots, span), lambda j: (0, j, 0, 0))]
    in_specs += [pl.BlockSpec((span, width), lambda j: (j, 0))] * pieces
    args = [picks, *sources]
    aliases = {}
    if buffer is not None:
        in_specs.append(pl.BlockSpec(memory_space=pl.ANY))
        aliases = {len(args): 0}
        args.append(buffer)
    return pl.pallas_call(
        functools.partial(dispatch_body, pieces, each),
        grid=(pairs,),
        in_specs=in_specs,
        out_specs=pl.BlockSpec(
            (slots // each, block, width), lambda j: (0, half * pairs + j, 0)
        ),
        out_shape=jax.ShapeDtypeStruct((slots // each, 2 * pairs * block, width), BF),
        input_output_aliases=aliases,
        compiler_params=pltpu.CompilerParams(vmem_limit_bytes=VMEM_BYTES),
        cost_estimate=pl.CostEstimate(
            flops=2 * pieces * pairs * slots * span * width,
            bytes_accessed=2 * pieces * pairs * (slots + span) * width,
            transcendentals=0,
        ),
        name="dispatch",
    )(*args)


def combine_body(pieces, each, picks, rows, *outs):
    for q in range(pieces):
        part = rows[:, q * each : (q + 1) * each, :].reshape(-1, rows.shape[-1])
        outs[q][...] = matmul(picks[q, 0], part, ((0,), (0,))).astype(BF)


def combine(picks, rows, half):
    pieces, pairs, slots, span = picks.shape
    each = 2 * CAP
    local, _, width = rows.shape
    return pl.pallas_call(
        functools.partial(combine_body, pieces, each),
        grid=(pairs,),
        in_specs=[
            pl.BlockSpec((pieces, 1, slots, span), lambda j: (0, j, 0, 0)),
            pl.BlockSpec((local, pieces * each, width), lambda j: (0, half * pairs + j, 0)),
        ],
        out_specs=[pl.BlockSpec((span, width), lambda j: (j, 0))] * pieces,
        out_shape=[jax.ShapeDtypeStruct((pairs * span, width), BF)] * pieces,
        compiler_params=pltpu.CompilerParams(vmem_limit_bytes=VMEM_BYTES),
        cost_estimate=pl.CostEstimate(
            flops=2 * pieces * pairs * slots * span * width,
            bytes_accessed=2 * pieces * pairs * (slots + span) * width,
            transcendentals=0,
        ),
        name="combine",
    )(picks, rows)


def expert_body(parts, tiles, start, aliased, *refs):
    where, rows_ref, ups_ref, weights_ref, down_ref = refs[:5]
    rest = refs[5 + aliased :]
    results_ref, row_grads_ref, weight_grads_ref, down_grad_ref, result_grads, *sums = rest
    tile = pl.program_id(1)
    width = FF // parts
    depth = D // parts
    slices = [slice(s * depth, (s + 1) * depth) for s in range(parts)]

    both = None
    for s in range(parts):
        term = matmul(rows_ref[0, :, slices[s]], weights_ref[s, 0], ((1,), (0,)))
        both = term if both is None else both + term
    gate_value = both[:, :width]
    up_value = both[:, width:]
    sigma = 1.0 / (1.0 + jnp.exp(-gate_value))
    silu = gate_value * sigma
    hidden = (silu * up_value).astype(BF)

    expert = where[1] + start + pl.program_id(0)
    lane = lax.broadcasted_iota(jnp.int32, (rows_ref.shape[1], LANES), 1)
    high = lane == expert
    low = lane == expert + E
    probs = rows_ref[0, :, D:].astype(F32)
    weight = jnp.sum(jnp.where(high | low, probs, 0.0), axis=1, keepdims=True)

    gate_grad = None
    hidden_grads = None
    for columns in slices:
        down = down_ref[0, :, columns]
        results = matmul(hidden, down, ((1,), (0,)))
        upstream = ups_ref[0, :, columns].astype(F32)
        dot = jnp.sum(upstream * results, axis=1, keepdims=True)
        gate_grad = dot if gate_grad is None else gate_grad + dot
        results_ref[0, :, columns] = (weight * results).astype(BF)
        part = (weight * upstream).astype(BF)
        result_grads[:, columns] = part
        term = matmul(part, down, ((1,), (1,)))
        hidden_grads = term if hidden_grads is None else hidden_grads + term

    gate_value_grads = (
        hidden_grads * up_value * (sigma * (1.0 + gate_value * (1.0 - sigma)))
    ).astype(BF)
    up_value_grads = (hidden_grads * silu).astype(BF)
    both_grads = jnp.concatenate([gate_value_grads, up_value_grads], axis=1)
    top = gate_grad.astype(BF)
    bottom = (gate_grad - top.astype(F32)).astype(BF)
    row_grads_ref[0, :, D:] = jnp.where(
        high, top.astype(F32), jnp.where(low, bottom.astype(F32), 0.0)
    ).astype(BF)
    for s in range(parts):
        row_grads_ref[0, :, slices[s]] = matmul(
            both_grads, weights_ref[s, 0], ((1,), (1,))
        ).astype(BF)

    def weight_term(s):
        return matmul(rows_ref[0, :, slices[s]], both_grads, ((0,), (0,)))

    def down_term(columns):
        return matmul(hidden, result_grads[:, columns], ((0,), (0,)))

    if tiles == 1:
        for s in range(parts):
            weight_grads_ref[s, 0] = weight_term(s).astype(BF)
            down_grad_ref[0, :, slices[s]] = down_term(slices[s])
        return
    weight_sums = sums[0]
    first = tile == 0

    @pl.when(first)
    def _():
        for s in range(parts):
            weight_sums[s] = weight_term(s)
            down_grad_ref[0, :, slices[s]] = down_term(slices[s])

    @pl.when(jnp.logical_not(first))
    def _():
        for s in range(parts):
            weight_sums[s] += weight_term(s)
            down_grad_ref[0, :, slices[s]] += down_term(slices[s])

    @pl.when(tile == tiles - 1)
    def _():
        for s in range(parts):
            weight_grads_ref[s, 0] = weight_sums[s].astype(BF)


def expert_chunk(where, rows, ups, weights, down, start, group, at, buffers):
    parts, experts, depth, width2 = weights.shape
    local, total_rows, wide_row = rows.shape
    tile = EXPERT_TILE
    tiles = total_rows // tile
    slice_ff = down.shape[1]
    weight_spec = pl.BlockSpec((parts, 1, depth, width2), lambda e, i, c: (0, e, 0, 0))
    down_spec = pl.BlockSpec((1, slice_ff, D), lambda e, i, c: (start + e, 0, 0))
    in_specs = [
        pl.BlockSpec((1, tile, wide_row), lambda e, i, c: (start + e, i, 0)),
        pl.BlockSpec((1, tile, D), lambda e, i, c: (start + e, i, 0)),
        weight_spec,
        down_spec,
    ]
    args = [where, rows, ups, weights, down]
    aliases = {}
    for index, buffer in enumerate(buffers):
        if buffer is not None:
            in_specs.append(pl.BlockSpec(memory_space=pl.ANY))
            aliases[len(args)] = index
            args.append(buffer)
    return pl.pallas_call(
        functools.partial(expert_body, parts, tiles, start, len(aliases)),
        grid_spec=pltpu.PrefetchScalarGridSpec(
            num_scalar_prefetch=1,
            grid=(experts, tiles),
            in_specs=in_specs,
            out_specs=[
                pl.BlockSpec((1, tile, D), lambda e, i, c: (start + e, i, 0)),
                pl.BlockSpec((1, tile, wide_row), lambda e, i, c: (start + e, i, 0)),
                pl.BlockSpec((parts, 1, depth, width2), lambda e, i, c: (0, at + e, 0, 0)),
                down_spec,
            ],
            scratch_shapes=[pltpu.VMEM((tile, D), BF)]
            + ([pltpu.VMEM((parts, depth, width2), F32)] if tiles > 1 else []),
        ),
        out_shape=[
            jax.ShapeDtypeStruct((local, total_rows, D), BF),
            jax.ShapeDtypeStruct((local, total_rows, wide_row), BF),
            jax.ShapeDtypeStruct((parts, group, depth, width2), BF),
            jax.ShapeDtypeStruct((local, slice_ff, D), F32),
        ],
        input_output_aliases=aliases,
        compiler_params=pltpu.CompilerParams(vmem_limit_bytes=VMEM_BYTES),
        cost_estimate=pl.CostEstimate(
            flops=18 * experts * total_rows * D * slice_ff,
            bytes_accessed=8 * experts * total_rows * D + 18 * experts * D * slice_ff,
            transcendentals=experts * total_rows * slice_ff,
        ),
        name="experts",
    )(*args)


def slice_body(parts, width, gate_ref, up_ref, out):
    for s in range(parts):
        columns = slice(s * width, (s + 1) * width)
        out[s, 0, :, :width] = gate_ref[0, :, columns]
        out[s, 0, :, width:] = up_ref[0, :, columns]


def slice_weights(gate, up, start, experts, parts):
    depth = gate.shape[1]
    width = FF // parts
    spec = pl.BlockSpec((1, depth, FF), lambda e: (start + e, 0, 0))
    return pl.pallas_call(
        functools.partial(slice_body, parts, width),
        grid=(experts,),
        in_specs=[spec, spec],
        out_specs=pl.BlockSpec((parts, 1, depth, 2 * width), lambda e: (0, e, 0, 0)),
        out_shape=jax.ShapeDtypeStruct((parts, experts, depth, 2 * width), BF),
        compiler_params=pltpu.CompilerParams(vmem_limit_bytes=VMEM_BYTES),
        cost_estimate=pl.CostEstimate(
            flops=0, bytes_accessed=8 * experts * depth * FF, transcendentals=0
        ),
        name="slice_weights",
    )(gate, up)


def assemble_body(parts, width, *refs):
    source = refs[0]
    gate_ref, up_ref = refs[-2], refs[-1]
    for s in range(parts):
        columns = slice(s * width, (s + 1) * width)
        gate_ref[0, :, columns] = source[s, 0, :, :width].astype(F32)
        up_ref[0, :, columns] = source[s, 0, :, width:].astype(F32)


def assemble(source, start, local, buffers):
    parts, experts, depth, width2 = source.shape
    in_specs = [pl.BlockSpec((parts, 1, depth, width2), lambda e: (0, e, 0, 0))]
    args = [source]
    aliases = {}
    if buffers is not None:
        in_specs += [pl.BlockSpec(memory_space=pl.ANY)] * 2
        aliases = {1: 0, 2: 1}
        args += list(buffers)
    spec = pl.BlockSpec((1, depth, FF), lambda e: (start + e, 0, 0))
    return pl.pallas_call(
        functools.partial(assemble_body, parts, width2 // 2),
        grid=(experts,),
        in_specs=in_specs,
        out_specs=[spec, spec],
        out_shape=[jax.ShapeDtypeStruct((local, depth, FF), F32)] * 2,
        input_output_aliases=aliases,
        compiler_params=pltpu.CompilerParams(vmem_limit_bytes=VMEM_BYTES),
        cost_estimate=pl.CostEstimate(
            flops=0, bytes_accessed=6 * experts * depth * FF * 2, transcendentals=0
        ),
        name="assemble",
    )(*args)


def turn(x, cosine, sine):
    return x * cosine + pltpu.roll(x, HD // 2, 1) * sine


def probabilities(query, key):
    scores = matmul(query, key, ((1,), (1,))) * HD ** (-0.5)
    row = lax.broadcasted_iota(jnp.int32, scores.shape, 0)
    column = lax.broadcasted_iota(jnp.int32, scores.shape, 1)
    causal = row >= column
    scores = jnp.where(causal, scores, -1e30)
    powers = jnp.exp(scores - jnp.max(scores, axis=-1, keepdims=True))
    return powers / jnp.sum(powers, axis=-1, keepdims=True), causal


def attend_body(raw, scales, cosine, sine, gains, turned, attended):
    features = attended.shape[1]
    for part in range(2):
        scale = scales[:, part : part + 1]
        for at in range(0, features, HD):
            columns = slice(part * features + at, part * features + at + HD)
            x = raw[:, columns] * scale * gains[part : part + 1, at : at + HD]
            turned[:, columns] = turn(x, cosine[...], sine[...]).astype(BF)
    turned[:, 2 * features :] = raw[:, 2 * features :].astype(BF)
    for at in range(0, features, HD):
        query = turned[:, at : at + HD]
        key = turned[:, features + at : features + at + HD]
        value = turned[:, 2 * features + at : 2 * features + at + HD]
        probs, _ = probabilities(query, key)
        attended[:, at : at + HD] = matmul(probs.astype(BF), value, ((1,), (0,))).astype(BF)


def attend(raw, scales, cosine, sine, gains, count):
    total, features = raw.shape[0], raw.shape[1] // 3

    def block(x):
        return pl.BlockSpec((count, x.shape[1]), lambda i: (i, 0))

    return pl.pallas_call(
        attend_body,
        grid=(total // count,),
        in_specs=[block(x) for x in (raw, scales, cosine, sine)]
        + [pl.BlockSpec(gains.shape, lambda i: (0, 0))],
        out_specs=[
            pl.BlockSpec((count, 3 * features), lambda i: (i, 0)),
            pl.BlockSpec((count, features), lambda i: (i, 0)),
        ],
        out_shape=[
            jax.ShapeDtypeStruct((total, 3 * features), BF),
            jax.ShapeDtypeStruct((total, features), BF),
        ],
        compiler_params=pltpu.CompilerParams(vmem_limit_bytes=VMEM_BYTES),
        cost_estimate=pl.CostEstimate(
            flops=4 * total * count * features,
            bytes_accessed=20 * total * features,
            transcendentals=total * count,
        ),
        name="attend",
    )(raw, scales, cosine, sine, gains)


def attend_back_body(turned, grads, raw, scales, cosine, sine, gains, scaled, value_grads, sums, gain_grads):
    features = grads.shape[1]
    scale = HD ** (-0.5)
    dots = [0.0, 0.0]
    first = pl.program_id(0) == 0
    for at in range(0, features, HD):
        query = turned[:, at : at + HD]
        key = turned[:, features + at : features + at + HD]
        value = turned[:, 2 * features + at : 2 * features + at + HD]
        grad = grads[:, at : at + HD]
        probs, causal = probabilities(query, key)
        value_grads[:, at : at + HD] = matmul(probs.astype(BF), grad, ((0,), (0,))).astype(BF)
        prob_grads = matmul(grad, value, ((1,), (1,)))
        score_grads = probs * (prob_grads - jnp.sum(probs * prob_grads, axis=-1, keepdims=True))
        score_grads = jnp.where(causal, score_grads, 0.0).astype(BF)
        turned_grads = (
            matmul(score_grads, key, ((1,), (0,))) * scale,
            matmul(score_grads, query, ((0,), (0,))) * scale,
        )
        for part in range(2):
            columns = slice(part * features + at, part * features + at + HD)
            x = raw[:, columns]
            dy = turn(turned_grads[part], cosine[...], -sine[...])
            u = dy * gains[part : part + 1, at : at + HD]
            scaled[:, columns] = u
            dots[part] = dots[part] + jnp.sum(u * x, axis=-1, keepdims=True)
            gain_grad = jnp.sum(dy * x * scales[:, part : part + 1], axis=0, keepdims=True)
            old = gain_grads[part : part + 1, at : at + HD]
            gain_grads[part : part + 1, at : at + HD] = gain_grad + jnp.where(first, 0.0, old)
    sums[...] = jnp.concatenate(dots, axis=1)


def attend_back(turned, grads, raw, scales, cosine, sine, gains, count):
    total, features = grads.shape

    def block(x):
        return pl.BlockSpec((count, x.shape[1]), lambda i: (i, 0))

    out_shape = [
        jax.ShapeDtypeStruct((total, 2 * features), F32),
        jax.ShapeDtypeStruct((total, features), BF),
        jax.ShapeDtypeStruct((total, 2), F32),
    ]
    return pl.pallas_call(
        attend_back_body,
        grid=(total // count,),
        in_specs=[block(x) for x in (turned, grads, raw, scales, cosine, sine)]
        + [pl.BlockSpec(gains.shape, lambda i: (0, 0))],
        out_specs=[block(x) for x in out_shape] + [pl.BlockSpec(gains.shape, lambda i: (0, 0))],
        out_shape=[*out_shape, jax.ShapeDtypeStruct(gains.shape, F32)],
        compiler_params=pltpu.CompilerParams(vmem_limit_bytes=VMEM_BYTES),
        cost_estimate=pl.CostEstimate(
            flops=12 * total * count * features,
            bytes_accessed=30 * total * features,
            transcendentals=total * count,
        ),
        name="attend_back",
    )(turned, grads, raw, scales, cosine, sine, gains)


def pick_body(where, *refs):
    half = pl.num_programs(0) // 2

    def fill(out):
        width = out.shape[-1]
        at = 0
        for source in refs[:-2]:
            outer, _, _, own = source.shape
            if own >= width:
                for i in range(outer):
                    for column in range(0, own, width):
                        out[0, at] = source[i, 0, :, column : column + width]
                        at += 1
            else:
                for i in range(0, outer, width // own):
                    for k in range(width // own):
                        out[0, at, :, k * own : (k + 1) * own] = source[i + k, 0]
                    at += 1

    @pl.when(pl.program_id(0) < half)
    def _():
        fill(refs[-2])

    @pl.when(pl.program_id(0) >= half)
    def _():
        fill(refs[-1])


def pick_blocks(order, width, *sources):
    rows = sources[0].shape[2]
    half = order.shape[0] // 2
    outer = sum(x.shape[0] * x.shape[3] for x in sources) // width
    shape = (1, outer, rows, width)
    return pl.pallas_call(
        pick_body,
        grid_spec=pltpu.PrefetchScalarGridSpec(
            num_scalar_prefetch=1,
            grid=(2 * half,),
            in_specs=[
                pl.BlockSpec((x.shape[0], 1, *x.shape[2:]), lambda k, c: (0, c[k], 0, 0))
                for x in sources
            ],
            out_specs=[
                pl.BlockSpec(shape, lambda k, c: (jnp.minimum(k, half - 1), 0, 0, 0)),
                pl.BlockSpec(shape, lambda k, c: (jnp.maximum(k - half, 0), 0, 0, 0)),
            ],
        ),
        out_shape=[jax.ShapeDtypeStruct((half, *shape[1:]), BF)] * 2,
        compiler_params=pltpu.CompilerParams(vmem_limit_bytes=VMEM_BYTES),
        cost_estimate=pl.CostEstimate(
            flops=0, bytes_accessed=8 * half * outer * rows * width, transcendentals=0
        ),
        name="pick_blocks",
    )(order, *sources)


def tie(value, *after):
    return lax.optimization_barrier((value, *after))[0]


def split_low(x):
    top = x.astype(BF)
    return top, (x - top.astype(F32)).astype(BF)


def add_up(parts):
    total = parts[0].astype(F32)
    for part in parts[1:]:
        total = total + part.astype(F32)
    return total


def make_on_device(wide, narrow):
    planes = wide // 2
    local = E // wide
    heads = H // wide
    features = heads * HD
    if local == 8:
        sizes, early, groups = [2, 1, 1, 2, 2], 3, [[0], [1, 2, 3], [4]]
    else:
        sizes = [1] * local
        early, groups = min(2, local), [[c] for c in range(local)]
    calls = len(sizes)
    starts = [sum(sizes[:c]) for c in range(calls)]
    slice_ff = FF // narrow
    both_axes = ("wide", "narrow")

    def swap(x, axis, r):
        size = wide if axis == "wide" else narrow
        return lax.ppermute(x, axis, [(i, i ^ r) for i in range(size)])

    bits = [1 << i for i in reversed(range(narrow.bit_length() - 1))]
    near = [0]
    for bit in bits:
        near = near + [r ^ bit for r in near]

    def swap_marked(x, bit, small):
        rest = swap(x[:-small], "narrow", bit)
        marker = swap(x[-small:], "narrow", bit)
        return jnp.concatenate([rest, marker], axis=0), marker

    def gather_narrow(x, *after):
        for i, bit in enumerate(bits):
            if i and after:
                x = tie(x, *after)
            x = jnp.concatenate([x, swap(x, "narrow", bit)], axis=0)
        return x

    def scatter_narrow(keep, send, step=(), last=(), small=0):
        arrivals = []
        for bit in reversed(bits):
            marker = None
            if small and bit == bits[0]:
                came, marker = swap_marked(send[0], bit, small)
                came = came[None]
            else:
                came = swap(send, "narrow", bit)
            if last and bit == bits[0]:
                came = tie(came, *last)
            arrivals.append(came)
            if marker is not None:
                arrivals.append(marker)
            total = keep.astype(F32) + came.astype(F32)
            half = total.shape[0] // 2
            keep, send = total[:half], total[half:].astype(BF)
            if step:
                send = tie(send, *step)
        return total[0], arrivals

    def gather_planes(x):
        return [x] + [swap(x, "wide", 2 * q) for q in range(1, planes)]

    def cross(pieces):
        return [swap(piece, "wide", 1) for piece in pieces]

    def gather_wide(x):
        own = gather_planes(x)
        return own, cross(own)

    def join(own, other):
        return jnp.concatenate([piece for pair in zip(own, other) for piece in pair], axis=0)

    def scatter_wide(own, other):
        return scatter_plane(own, swap(other, "wide", 1))[0]

    def scatter_plane(own, came, *after):
        sums = [own[q].astype(F32) + came[q].astype(F32) for q in range(planes)]
        sent = [x.astype(BF) for x in sums[1:]]
        if after:
            sent = list(lax.optimization_barrier((*sent, *after))[: planes - 1])
        total = sums[0]
        for q in range(1, planes):
            total = total + swap(sent[q - 1], "wide", 2 * q).astype(F32)
        return total, sent

    def on_device(
        tokens, positions, routes, cotangent,
        w_query, w_key, w_value, w_output, w_router,
        gain_attn, gain_query, gain_key, gain_ffn,
        w_gate, w_up, w_down,
    ):
        count = tokens.shape[0]
        rows = w_query.shape[0]
        w = lax.axis_index("wide")
        n = lax.axis_index("narrow")
        where = jnp.stack([n, w * local, w]).astype(jnp.int32)
        wide_order = jnp.arange(wide) ^ w
        near_order = jnp.array(near) ^ n
        narrow_order = jnp.array([near.index(r) for r in range(narrow)])[jnp.arange(narrow) ^ n]

        def by_narrow(*x):
            return pick_blocks(near_order, 2 * features, *x)

        routed = jnp.any(
            routes[:, :, None] == jnp.arange(E, dtype=jnp.int32)[None, None, :], axis=1
        )
        earlier = matmul(
            jnp.tril(jnp.ones((count, count), BF), -1), routed.astype(BF), ((1,), (0,))
        )
        slots = jnp.where(routed, earlier, -1.0).astype(BF).T

        small = jnp.concatenate(
            [
                w_router.reshape(-1), gain_attn, gain_query, gain_key, gain_ffn,
                positions.astype(BF),
            ]
        )
        small_rows = -(-small.shape[0] // LANES)
        bundle_rows = -(-(E + small_rows) // 16) * 16
        small = jnp.pad(small, (0, (bundle_rows - E) * LANES - small.shape[0]))
        bundle = jnp.concatenate([slots, small.reshape(-1, LANES)], axis=0)
        bundle_z = lax.all_gather(bundle, "narrow")
        stacked = jnp.concatenate(
            [x.reshape(rows, wide, features) for x in (w_query, w_key, w_value)], axis=-1
        ).transpose(1, 0, 2)
        columns = lax.all_to_all(stacked, "wide", 0, 0, tiled=True)
        bundles = lax.all_gather(bundle_z, "wide")
        all_slots = bundles[:, :, :E, :]
        all_small = bundles[:, :, E:, :].reshape(wide, narrow, -1)
        base = rows * E
        plane_positions = lax.dynamic_index_in_dim(
            all_small[:, :, base + 4 * rows : base + 4 * rows + count], n, 1, keepdims=False
        )
        plane_positions = jnp.take(plane_positions, wide_order, axis=0).reshape(wide * count)
        router_full = all_small[:, :, :base].reshape(D, E)
        gains = [
            all_small[:, :, base + i * rows : base + (i + 1) * rows].reshape(D).astype(F32)
            for i in range(4)
        ]
        attn_gain, query_gain, key_gain, ffn_gain = gains
        query_gain = lax.dynamic_slice_in_dim(query_gain, w * features, features)
        key_gain = lax.dynamic_slice_in_dim(key_gain, w * features, features)
        expert_counts = jnp.sum((all_slots >= 0).astype(jnp.int32), axis=(0, 1, 3))

        tokens_near = gather_wide(tokens)
        plane_tokens = join(*tokens_near).astype(F32)
        plane_count = plane_tokens.shape[0]

        sliced = [
            slice_weights(w_gate, w_up, starts[c], sizes[c], narrow) for c in range(calls)
        ]
        expert_weights = []

        def send_weights(*after):
            part = tie(sliced[len(expert_weights)], *after)
            expert_weights.append(lax.all_to_all(part, "narrow", 0, 0, tiled=True))

        ups_z = gather_narrow(cotangent, bundle_z)
        send_weights(columns, bundles, ups_z)
        ups_own = gather_planes(tie(ups_z, *tokens_near[0], *tokens_near[1]))
        columns, w_output = lax.optimization_barrier(
            (columns, w_output, expert_weights[0], *tokens_near[0], *tokens_near[1], *ups_own[:3])
        )[:2]
        columns = gather_narrow(columns[None])
        columns = jnp.take(columns, narrow_order, axis=0)
        qkv = columns.transpose(1, 0, 2, 3).reshape(D, 3 * features)
        output_rows = gather_narrow(w_output[None])
        output_rows = jnp.take(output_rows, narrow_order, axis=0).reshape(features, D)
        while len(expert_weights) < early:
            send_weights(qkv, output_rows, *expert_weights[1:])

        local_slots = lax.dynamic_slice_in_dim(all_slots, w * local, local, axis=2)
        local_slots = jnp.take(jnp.take(local_slots, wide_order, axis=0), near_order, axis=1)
        pairs = narrow // 2
        local_slots = (
            local_slots.reshape(planes, 2, pairs, 2, local, count)
            .transpose(1, 0, 2, 4, 3, 5)
            .reshape(2, planes, pairs, local, 1, 2 * count)
        )
        row = jnp.arange(2 * CAP)[:, None]
        lane = jnp.arange(2 * count)[None, :]
        picks = (
            ((local_slots == (row % CAP).astype(BF)) & (row // CAP == lane // count))
            .astype(BF)
            .reshape(2, planes, pairs, local * 2 * CAP, 2 * count)
        )
        picks_own, picks_other = picks[0], picks[1]
        inverse = lax.rsqrt(jnp.mean(plane_tokens * plane_tokens, axis=-1, keepdims=True) + EPSILON)
        normed = (plane_tokens * inverse * attn_gain).astype(BF)
        raw = matmul(normed, tie(qkv, *ups_own), ((1,), (0,)))

        def row_sums(sums):
            sums = jnp.take(sums.reshape(2, wide, count), wide_order, axis=1)
            gathered = lax.all_gather(sums, "wide")
            sums = jnp.sum(gathered, axis=0)
            return jnp.take(sums, wide_order, axis=1).reshape(2, plane_count), gathered

        squares = jnp.stack(
            [
                jnp.sum(x * x, axis=-1)
                for x in (raw[:, :features], raw[:, features : 2 * features])
            ]
        )
        scales = lax.rsqrt(row_sums(squares)[0] / D + EPSILON).T
        frequency = THETA_BASE ** (-2.0 * jnp.arange(HD // 2, dtype=F32) / HD)
        angles = plane_positions.astype(F32)[:, None] * frequency[None, :]
        cosine, sine = jnp.cos(angles), jnp.sin(angles)
        cosine = jnp.concatenate([cosine, cosine], axis=1)
        sine = jnp.concatenate([-sine, sine], axis=1)
        head_gains = jnp.stack([query_gain, key_gain])
        turned, attended = attend(raw, scales, cosine, sine, head_gains, count)
        if early > 2:
            attended = tie(attended, expert_weights[1])
        branch = matmul(attended, output_rows, ((1,), (0,))).astype(BF)
        branch = branch.reshape(planes, 2, count, D)
        branch = scatter_wide(branch[:, 0], branch[:, 1])

        residual = tokens.astype(F32) + branch
        ffn_r = lax.rsqrt(jnp.mean(residual * residual, axis=-1, keepdims=True) + EPSILON)
        normed_ffn = (residual * ffn_r * ffn_gain).astype(BF)
        logits = matmul(normed_ffn, router_full, ((1,), (0,)))
        router_powers = jnp.exp(logits - jnp.max(logits, axis=-1, keepdims=True))
        router_probs = router_powers / jnp.sum(router_powers, axis=-1, keepdims=True)

        message = jnp.concatenate([normed_ffn, *split_low(router_probs)], axis=1)
        ups = dispatch(picks_own, ups_own, 0)
        ups = dispatch(picks_other, cross(ups_own), 1, ups)
        message = gather_narrow(tie(message, ups, expert_weights[-1]))
        if calls > early:
            send_weights(message)
        tokens_own = gather_planes(message)
        while len(expert_weights) < calls:
            send_weights(*tokens_own)
        tokens_own[0] = tie(tokens_own[0], expert_weights[min(early, calls - 1)])
        tokens_other = cross(tokens_own)
        expert_rows = dispatch(picks_own, tokens_own, 0)
        expert_rows = dispatch(picks_other, tokens_other, 1, expert_rows)

        came = []
        held = [None] * 4
        for c in range(calls):
            if c == 1:
                expert_rows = tie(expert_rows, expert_weights[-1])
            group = next(g for g in groups if c in g)
            if c == group[0]:
                held[2] = None
            held = [*expert_chunk(
                where, expert_rows, ups, expert_weights[c], w_down, starts[c],
                sum(sizes[g] for g in group), starts[c] - starts[group[0]], held,
            )]
            if c == group[-1]:
                came.append(held[2])
        results, row_grads, _, down_grad = held
        arrived = []

        def send_grads(*after):
            part = came[len(arrived)]
            part = tie(part, *after) if after else part
            arrived.append(lax.all_to_all(part, "narrow", 0, 0, tiled=True))

        grad_starts = [starts[group[0]] for group in groups]
        sent_early = len(groups) - 1
        for g in range(sent_early):
            send_grads(*([row_grads] if g else []))

        def combine_tokens(terms, *after):
            terms = tie(terms, *after) if after else terms
            other = cross(combine(picks_other, terms, 1))
            return list(combine(picks_own, terms, 0)), other

        def scatter_rest(plane_sum, last=(), small=0):
            blocks = plane_sum.reshape(narrow, count, plane_sum.shape[-1])
            return scatter_narrow(
                blocks[: narrow // 2], blocks[narrow // 2 :], (), last, small
            )

        own, other = combine_tokens(row_grads)
        plane_sum, sent = scatter_plane(own, other)
        mix_own, mix_other = combine_tokens(results, *sent)
        mix_sums = [mix_own[q].astype(F32) + mix_other[q].astype(F32) for q in range(planes)]
        mix_sent = [x.astype(BF) for x in mix_sums[1:]]
        plane_done = plane_sum.astype(BF)
        plane_sum = tie(plane_done, *arrived, *mix_other)
        mix_came = [
            swap(tie(mix_sent[q - 1], plane_done), "wide", 2 * q) for q in range(1, planes)[:2]
        ]
        ffn_message, ffn_came = scatter_rest(plane_sum, mix_came, 16)
        send_grads(ffn_came[-1])
        buffers = None
        for start, part in zip(grad_starts, arrived[:sent_early]):
            buffers = assemble(tie(part, ffn_came[-1]), start, local, buffers)
        ffn_message = tie(ffn_message, *buffers)

        upstream = cotangent.astype(F32)
        prob_grads = ffn_message[:, D : D + E] + ffn_message[:, D + E : D + 2 * E]
        logit_grads = (
            router_probs
            * (prob_grads - jnp.sum(router_probs * prob_grads, axis=-1, keepdims=True))
        ).astype(BF)
        ffn_grads = ffn_message[:, :D] + matmul(logit_grads, router_full, ((1,), (1,)))

        def norm_back(v, r, gain, dy):
            u = dy * gain
            return r * u - v * (r * r * r) * jnp.mean(u * v, axis=-1, keepdims=True)

        residual_grads = upstream + norm_back(residual, ffn_r, ffn_gain, ffn_grads)
        ffn_gain_part = jnp.sum(ffn_grads * residual * ffn_r, axis=0)
        message = jnp.concatenate(
            [residual_grads.astype(BF), logit_grads, jnp.zeros_like(logit_grads)], axis=1
        )

        plane_message = join(*gather_wide(message))
        plane_grads = plane_message[:, :D]
        attended_grads = matmul(plane_grads, output_rows, ((1,), (1,))).astype(BF)
        plane_rows = lax.dynamic_slice_in_dim(
            join([x[:count] for x in tokens_own], [x[:count] for x in tokens_other]),
            w * features,
            features,
            axis=1,
        )
        scaled, value_grads, dots, head_gain_parts = attend_back(
            turned, attended_grads, raw, scales, cosine, sine, head_gains, count
        )

        grad_output = matmul(attended, plane_grads, ((0,), (0,))).astype(BF)
        grad_value = matmul(normed, value_grads, ((0,), (0,))).astype(BF)
        early_parts = by_narrow(
            grad_output.reshape(1, narrow, rows, D),
            grad_value.reshape(wide, narrow, rows, features),
        )

        dots, dots_gathered = row_sums(dots.T)
        dots = dots.T / D
        shrink = scales * scales * scales * dots
        raw_grads = (
            scaled.reshape(plane_count, 2, features) * scales[:, :, None]
            - raw[:, : 2 * features].reshape(plane_count, 2, features) * shrink[:, :, None]
        ).astype(BF)
        raw_grads = jnp.concatenate([raw_grads.reshape(plane_count, 2 * features), value_grads], axis=1)
        mix_came += [
            swap(tie(mix_sent[q - 1], dots_gathered), "wide", 2 * q) for q in range(3, planes)
        ]
        grad_early, early_came = scatter_narrow(*early_parts)
        raw_grads = tie(raw_grads, arrived[-1], early_came[0])
        normed_grads = matmul(raw_grads, qkv, ((1,), (1,))).astype(BF)

        attn_gain_part = jnp.sum(normed_grads.astype(F32) * plane_tokens * inverse, axis=0)
        gain_parts = jnp.concatenate(
            [
                jnp.stack([attn_gain_part, ffn_gain_part]).reshape(2 * wide, features),
                head_gain_parts,
            ]
        ).T
        gain_columns = 2 * wide + 2
        router_part = matmul(plane_rows, plane_message[:, D : D + E], ((0,), (0,)))
        small_parts = jnp.concatenate([router_part.astype(BF), *split_low(gain_parts)], axis=1)
        small_parts = jnp.pad(
            small_parts, ((0, 0), (0, 2 * features - E - 2 * gain_columns))
        )
        plane_normed = normed_grads.reshape(planes, 2, count, D)
        normed_other = swap(plane_normed[:, 1], "wide", 1)
        normed_sums = [add_up([plane_normed[q, 0], normed_other[q]]) for q in range(planes)]
        normed_came = [
            swap(normed_sums[q].astype(BF), "wide", 2 * q)
            for q in range(1, planes)
        ]
        grad_raw = matmul(normed, raw_grads[:, : 2 * features], ((0,), (0,))).astype(BF)
        grad_raw, raw_came = scatter_narrow(
            *by_narrow(
                grad_raw.reshape(wide, narrow, rows, 2 * features),
                small_parts.reshape(1, narrow, rows, 2 * features),
            ),
            (),
            normed_came,
        )
        small_parts = grad_raw[wide]
        grad_router = small_parts[:, :E]
        gain_parts = small_parts[:, E : E + 2 * gain_columns]
        gain_parts = (gain_parts[:, :gain_columns] + gain_parts[:, gain_columns:]).T
        grad_gain_query, grad_gain_key = gain_parts[2 * wide], gain_parts[2 * wide + 1]
        blocks = D // (2 * features)
        grad_output = jnp.concatenate([grad_early[i] for i in range(blocks)], axis=1)
        grad_value = (
            grad_early[blocks:]
            .reshape(wide // 2, rows, 2, features)
            .transpose(0, 2, 1, 3)
            .reshape(wide, rows, features)
        )
        grad_qkv = jnp.concatenate([grad_raw[:wide], grad_value], axis=-1)
        mix_came[-1] = tie(mix_came[-1], raw_came[0])
        mixture = add_up([mix_sums[0], *mix_came]).astype(BF)
        block_out = (residual + scatter_rest(mixture)[0]).astype(BF)
        gain_rows = jnp.concatenate(
            [*split_low(gain_parts[:wide]), *split_low(gain_parts[wide : 2 * wide])], axis=1
        )
        gain_rows = jnp.pad(
            gain_rows[:, None, :], ((0, 0), (0, 15), (0, 3 * features - 4 * rows))
        )
        grad_qkv = jnp.concatenate([grad_qkv.astype(BF), gain_rows], axis=1)
        grad_qkv = lax.all_to_all(grad_qkv, "wide", 0, 0, tiled=True)
        gain_rows = jnp.sum(grad_qkv[:, rows, : 4 * rows].astype(F32), axis=0).reshape(4, rows)
        gain_sums = [gain_rows[0] + gain_rows[1], gain_rows[2] + gain_rows[3]]
        grad_qkv = grad_qkv[:, :rows].transpose(1, 0, 2).astype(F32)
        grad_query, grad_key, grad_value = [
            grad_qkv[..., i * features : (i + 1) * features].reshape(rows, D) for i in range(3)
        ]

        normed_grads = add_up([normed_sums[0], *normed_came])
        input_grad = (
            residual_grads
            + norm_back(tokens.astype(F32), inverse[:count], attn_gain, normed_grads)
        ).astype(BF)

        for start, part in zip(grad_starts[sent_early:], arrived[sent_early:]):
            buffers = assemble(tie(part, raw_came[1]), start, local, buffers)
        grad_gate, grad_up = buffers

        return (
            block_out, input_grad, grad_query, grad_key, grad_value,
            grad_output, grad_router,
            gain_sums[0], grad_gain_query, grad_gain_key, gain_sums[1],
            grad_gate, grad_up, down_grad, expert_counts,
        )

    return on_device


def solution(mesh):
    both = ("wide", "narrow")
    in_specs = (P(both, None), P(both), P(both, None), P(both, None))
    in_specs += (P(both, None),) * 5 + (P(both),) * 4 + (P("wide", "narrow", None),) * 3
    out_specs = (P(both, None),) * 7 + (P(both),) * 4 + (P("wide", "narrow", None),) * 3 + (P(),)
    return jax.shard_map(
        make_on_device(mesh.shape["wide"], mesh.shape["narrow"]),
        mesh=mesh,
        in_specs=in_specs,
        out_specs=out_specs,
        check_vma=False,
    )
```

```python
import functools

import jax
import jax.numpy as jnp
from jax import lax
from jax.experimental import pallas as pl
from jax.experimental.pallas import tpu as pltpu
from jax.sharding import PartitionSpec as P

D = 2048
H = 16
HD = 128
E = 64
TOPK = 8
CAP = 24
FF = 1024
LANES = 128
EXPERT_TILE = 768
EPSILON = 1e-05
THETA_BASE = 10000.0

BF = jnp.bfloat16
F32 = jnp.float32
VMEM_BYTES = 56 * 1024 * 1024


def matmul(a, b, dims):
    return lax.dot_general(a, b, (dims, ((), ())), preferred_element_type=F32)


def dispatch_body(pieces, each, *refs):
    picks = refs[0]
    sources = refs[1 : 1 + pieces]
    out = refs[-1]
    for q in range(pieces):
        rows = matmul(picks[q, 0], sources[q][...], ((1,), (0,))).astype(BF)
        out[:, q * each : (q + 1) * each, :] = rows.reshape(-1, each, rows.shape[-1])


def dispatch(picks, sources, half, buffer=None):
    pieces, pairs, slots, span = picks.shape
    width = sources[0].shape[1]
    each = 2 * CAP
    block = pieces * each
    in_specs = [pl.BlockSpec((pieces, 1, slots, span), lambda j: (0, j, 0, 0))]
    in_specs += [pl.BlockSpec((span, width), lambda j: (j, 0))] * pieces
    args = [picks, *sources]
    aliases = {}
    if buffer is not None:
        in_specs.append(pl.BlockSpec(memory_space=pl.ANY))
        aliases = {len(args): 0}
        args.append(buffer)
    return pl.pallas_call(
        functools.partial(dispatch_body, pieces, each),
        grid=(pairs,),
        in_specs=in_specs,
        out_specs=pl.BlockSpec(
            (slots // each, block, width), lambda j: (0, half * pairs + j, 0)
        ),
        out_shape=jax.ShapeDtypeStruct((slots // each, 2 * pairs * block, width), BF),
        input_output_aliases=aliases,
        compiler_params=pltpu.CompilerParams(vmem_limit_bytes=VMEM_BYTES),
        cost_estimate=pl.CostEstimate(
            flops=2 * pieces * pairs * slots * span * width,
            bytes_accessed=2 * pieces * pairs * (slots + span) * width,
            transcendentals=0,
        ),
        name="dispatch",
    )(*args)


def combine_body(pieces, each, picks, rows, *outs):
    for q in range(pieces):
        part = rows[:, q * each : (q + 1) * each, :].reshape(-1, rows.shape[-1])
        outs[q][...] = matmul(picks[q, 0], part, ((0,), (0,))).astype(BF)


def combine(picks, rows, half):
    pieces, pairs, slots, span = picks.shape
    each = 2 * CAP
    local, _, width = rows.shape
    return pl.pallas_call(
        functools.partial(combine_body, pieces, each),
        grid=(pairs,),
        in_specs=[
            pl.BlockSpec((pieces, 1, slots, span), lambda j: (0, j, 0, 0)),
            pl.BlockSpec((local, pieces * each, width), lambda j: (0, half * pairs + j, 0)),
        ],
        out_specs=[pl.BlockSpec((span, width), lambda j: (j, 0))] * pieces,
        out_shape=[jax.ShapeDtypeStruct((pairs * span, width), BF)] * pieces,
        compiler_params=pltpu.CompilerParams(vmem_limit_bytes=VMEM_BYTES),
        cost_estimate=pl.CostEstimate(
            flops=2 * pieces * pairs * slots * span * width,
            bytes_accessed=2 * pieces * pairs * (slots + span) * width,
            transcendentals=0,
        ),
        name="combine",
    )(picks, rows)


def expert_body(parts, tiles, start, aliased, *refs):
    where, rows_ref, ups_ref, weights_ref, down_ref = refs[:5]
    rest = refs[5 + aliased :]
    results_ref, row_grads_ref, weight_grads_ref, down_grad_ref, result_grads, *sums = rest
    tile = pl.program_id(1)
    width = FF // parts
    depth = D // parts
    slices = [slice(s * depth, (s + 1) * depth) for s in range(parts)]

    both = None
    for s in range(parts):
        term = matmul(rows_ref[0, :, slices[s]], weights_ref[s, 0], ((1,), (0,)))
        both = term if both is None else both + term
    gate_value = both[:, :width]
    up_value = both[:, width:]
    sigma = 1.0 / (1.0 + jnp.exp(-gate_value))
    silu = gate_value * sigma
    hidden = (silu * up_value).astype(BF)

    expert = where[1] + start + pl.program_id(0)
    lane = lax.broadcasted_iota(jnp.int32, (rows_ref.shape[1], LANES), 1)
    high = lane == expert
    low = lane == expert + E
    probs = rows_ref[0, :, D:].astype(F32)
    weight = jnp.sum(jnp.where(high | low, probs, 0.0), axis=1, keepdims=True)

    gate_grad = None
    hidden_grads = None
    for columns in slices:
        down = down_ref[0, :, columns]
        results = matmul(hidden, down, ((1,), (0,)))
        upstream = ups_ref[0, :, columns].astype(F32)
        dot = jnp.sum(upstream * results, axis=1, keepdims=True)
        gate_grad = dot if gate_grad is None else gate_grad + dot
        results_ref[0, :, columns] = (weight * results).astype(BF)
        part = (weight * upstream).astype(BF)
        result_grads[:, columns] = part
        term = matmul(part, down, ((1,), (1,)))
        hidden_grads = term if hidden_grads is None else hidden_grads + term

    gate_value_grads = (
        hidden_grads * up_value * (sigma * (1.0 + gate_value * (1.0 - sigma)))
    ).astype(BF)
    up_value_grads = (hidden_grads * silu).astype(BF)
    both_grads = jnp.concatenate([gate_value_grads, up_value_grads], axis=1)
    top = gate_grad.astype(BF)
    bottom = (gate_grad - top.astype(F32)).astype(BF)
    row_grads_ref[0, :, D:] = jnp.where(
        high, top.astype(F32), jnp.where(low, bottom.astype(F32), 0.0)
    ).astype(BF)
    for s in range(parts):
        row_grads_ref[0, :, slices[s]] = matmul(
            both_grads, weights_ref[s, 0], ((1,), (1,))
        ).astype(BF)

    def weight_term(s):
        return matmul(rows_ref[0, :, slices[s]], both_grads, ((0,), (0,)))

    def down_term(columns):
        return matmul(hidden, result_grads[:, columns], ((0,), (0,)))

    if tiles == 1:
        for s in range(parts):
            weight_grads_ref[s, 0] = weight_term(s).astype(BF)
            down_grad_ref[0, :, slices[s]] = down_term(slices[s])
        return
    weight_sums = sums[0]
    first = tile == 0

    @pl.when(first)
    def _():
        for s in range(parts):
            weight_sums[s] = weight_term(s)
            down_grad_ref[0, :, slices[s]] = down_term(slices[s])

    @pl.when(jnp.logical_not(first))
    def _():
        for s in range(parts):
            weight_sums[s] += weight_term(s)
            down_grad_ref[0, :, slices[s]] += down_term(slices[s])

    @pl.when(tile == tiles - 1)
    def _():
        for s in range(parts):
            weight_grads_ref[s, 0] = weight_sums[s].astype(BF)


def expert_chunk(where, rows, ups, weights, down, start, experts, offset, group, at, buffers):
    parts, _, depth, width2 = weights.shape
    local, total_rows, wide_row = rows.shape
    tile = EXPERT_TILE
    tiles = total_rows // tile
    slice_ff = down.shape[1]
    weight_spec = pl.BlockSpec((parts, 1, depth, width2), lambda e, i, c: (0, offset + e, 0, 0))
    down_spec = pl.BlockSpec((1, slice_ff, D), lambda e, i, c: (start + e, 0, 0))
    in_specs = [
        pl.BlockSpec((1, tile, wide_row), lambda e, i, c: (start + e, i, 0)),
        pl.BlockSpec((1, tile, D), lambda e, i, c: (start + e, i, 0)),
        weight_spec,
        down_spec,
    ]
    args = [where, rows, ups, weights, down]
    aliases = {}
    for index, buffer in enumerate(buffers):
        if buffer is not None:
            in_specs.append(pl.BlockSpec(memory_space=pl.ANY))
            aliases[len(args)] = index
            args.append(buffer)
    return pl.pallas_call(
        functools.partial(expert_body, parts, tiles, start, len(aliases)),
        grid_spec=pltpu.PrefetchScalarGridSpec(
            num_scalar_prefetch=1,
            grid=(experts, tiles),
            in_specs=in_specs,
            out_specs=[
                pl.BlockSpec((1, tile, D), lambda e, i, c: (start + e, i, 0)),
                pl.BlockSpec((1, tile, wide_row), lambda e, i, c: (start + e, i, 0)),
                pl.BlockSpec((parts, 1, depth, width2), lambda e, i, c: (0, at + e, 0, 0)),
                down_spec,
            ],
            scratch_shapes=[pltpu.VMEM((tile, D), BF)]
            + ([pltpu.VMEM((parts, depth, width2), F32)] if tiles > 1 else []),
        ),
        out_shape=[
            jax.ShapeDtypeStruct((local, total_rows, D), BF),
            jax.ShapeDtypeStruct((local, total_rows, wide_row), BF),
            jax.ShapeDtypeStruct((parts, group, depth, width2), BF),
            jax.ShapeDtypeStruct((local, slice_ff, D), F32),
        ],
        input_output_aliases=aliases,
        compiler_params=pltpu.CompilerParams(vmem_limit_bytes=VMEM_BYTES),
        cost_estimate=pl.CostEstimate(
            flops=18 * experts * total_rows * D * slice_ff,
            bytes_accessed=8 * experts * total_rows * D + 18 * experts * D * slice_ff,
            transcendentals=experts * total_rows * slice_ff,
        ),
        name="experts",
    )(*args)


def slice_body(parts, width, gate_ref, up_ref, out):
    for s in range(parts):
        columns = slice(s * width, (s + 1) * width)
        out[s, 0, :, :width] = gate_ref[0, :, columns]
        out[s, 0, :, width:] = up_ref[0, :, columns]


def slice_weights(gate, up, start, experts, parts):
    depth = gate.shape[1]
    width = FF // parts
    spec = pl.BlockSpec((1, depth, FF), lambda e: (start + e, 0, 0))
    return pl.pallas_call(
        functools.partial(slice_body, parts, width),
        grid=(experts,),
        in_specs=[spec, spec],
        out_specs=pl.BlockSpec((parts, 1, depth, 2 * width), lambda e: (0, e, 0, 0)),
        out_shape=jax.ShapeDtypeStruct((parts, experts, depth, 2 * width), BF),
        compiler_params=pltpu.CompilerParams(vmem_limit_bytes=VMEM_BYTES),
        cost_estimate=pl.CostEstimate(
            flops=0, bytes_accessed=8 * experts * depth * FF, transcendentals=0
        ),
        name="slice_weights",
    )(gate, up)


def assemble_body(parts, width, *refs):
    source = refs[0]
    gate_ref, up_ref = refs[-2], refs[-1]
    for s in range(parts):
        columns = slice(s * width, (s + 1) * width)
        gate_ref[0, :, columns] = source[s, 0, :, :width].astype(F32)
        up_ref[0, :, columns] = source[s, 0, :, width:].astype(F32)


def assemble(source, start, local, buffers):
    parts, experts, depth, width2 = source.shape
    in_specs = [pl.BlockSpec((parts, 1, depth, width2), lambda e: (0, e, 0, 0))]
    args = [source]
    aliases = {}
    if buffers is not None:
        in_specs += [pl.BlockSpec(memory_space=pl.ANY)] * 2
        aliases = {1: 0, 2: 1}
        args += list(buffers)
    spec = pl.BlockSpec((1, depth, FF), lambda e: (start + e, 0, 0))
    return pl.pallas_call(
        functools.partial(assemble_body, parts, width2 // 2),
        grid=(experts,),
        in_specs=in_specs,
        out_specs=[spec, spec],
        out_shape=[jax.ShapeDtypeStruct((local, depth, FF), F32)] * 2,
        input_output_aliases=aliases,
        compiler_params=pltpu.CompilerParams(vmem_limit_bytes=VMEM_BYTES),
        cost_estimate=pl.CostEstimate(
            flops=0, bytes_accessed=6 * experts * depth * FF * 2, transcendentals=0
        ),
        name="assemble",
    )(*args)


def turn(x, cosine, sine):
    return x * cosine + pltpu.roll(x, HD // 2, 1) * sine


def probabilities(query, key):
    scores = matmul(query, key, ((1,), (1,))) * HD ** (-0.5)
    row = lax.broadcasted_iota(jnp.int32, scores.shape, 0)
    column = lax.broadcasted_iota(jnp.int32, scores.shape, 1)
    causal = row >= column
    scores = jnp.where(causal, scores, -1e30)
    powers = jnp.exp(scores - jnp.max(scores, axis=-1, keepdims=True))
    return powers / jnp.sum(powers, axis=-1, keepdims=True), causal


def attend_body(raw, scales, cosine, sine, gains, turned, attended):
    features = attended.shape[1]
    for part in range(2):
        scale = scales[:, part : part + 1]
        for at in range(0, features, HD):
            columns = slice(part * features + at, part * features + at + HD)
            x = raw[:, columns] * scale * gains[part : part + 1, at : at + HD]
            turned[:, columns] = turn(x, cosine[...], sine[...]).astype(BF)
    turned[:, 2 * features :] = raw[:, 2 * features :].astype(BF)
    for at in range(0, features, HD):
        query = turned[:, at : at + HD]
        key = turned[:, features + at : features + at + HD]
        value = turned[:, 2 * features + at : 2 * features + at + HD]
        probs, _ = probabilities(query, key)
        attended[:, at : at + HD] = matmul(probs.astype(BF), value, ((1,), (0,))).astype(BF)


def attend(raw, scales, cosine, sine, gains, count):
    total, features = raw.shape[0], raw.shape[1] // 3

    def block(x):
        return pl.BlockSpec((count, x.shape[1]), lambda i: (i, 0))

    return pl.pallas_call(
        attend_body,
        grid=(total // count,),
        in_specs=[block(x) for x in (raw, scales, cosine, sine)]
        + [pl.BlockSpec(gains.shape, lambda i: (0, 0))],
        out_specs=[
            pl.BlockSpec((count, 3 * features), lambda i: (i, 0)),
            pl.BlockSpec((count, features), lambda i: (i, 0)),
        ],
        out_shape=[
            jax.ShapeDtypeStruct((total, 3 * features), BF),
            jax.ShapeDtypeStruct((total, features), BF),
        ],
        compiler_params=pltpu.CompilerParams(vmem_limit_bytes=VMEM_BYTES),
        cost_estimate=pl.CostEstimate(
            flops=4 * total * count * features,
            bytes_accessed=20 * total * features,
            transcendentals=total * count,
        ),
        name="attend",
    )(raw, scales, cosine, sine, gains)


def attend_back_body(turned, grads, raw, scales, cosine, sine, gains, scaled, value_grads, sums, gain_grads):
    features = grads.shape[1]
    scale = HD ** (-0.5)
    dots = [0.0, 0.0]
    first = pl.program_id(0) == 0
    for at in range(0, features, HD):
        query = turned[:, at : at + HD]
        key = turned[:, features + at : features + at + HD]
        value = turned[:, 2 * features + at : 2 * features + at + HD]
        grad = grads[:, at : at + HD]
        probs, causal = probabilities(query, key)
        value_grads[:, at : at + HD] = matmul(probs.astype(BF), grad, ((0,), (0,))).astype(BF)
        prob_grads = matmul(grad, value, ((1,), (1,)))
        score_grads = probs * (prob_grads - jnp.sum(probs * prob_grads, axis=-1, keepdims=True))
        score_grads = jnp.where(causal, score_grads, 0.0).astype(BF)
        turned_grads = (
            matmul(score_grads, key, ((1,), (0,))) * scale,
            matmul(score_grads, query, ((0,), (0,))) * scale,
        )
        for part in range(2):
            columns = slice(part * features + at, part * features + at + HD)
            x = raw[:, columns]
            dy = turn(turned_grads[part], cosine[...], -sine[...])
            u = dy * gains[part : part + 1, at : at + HD]
            scaled[:, columns] = u
            dots[part] = dots[part] + jnp.sum(u * x, axis=-1, keepdims=True)
            gain_grad = jnp.sum(dy * x * scales[:, part : part + 1], axis=0, keepdims=True)
            old = gain_grads[part : part + 1, at : at + HD]
            gain_grads[part : part + 1, at : at + HD] = gain_grad + jnp.where(first, 0.0, old)
    sums[...] = jnp.concatenate(dots, axis=1)


def attend_back(turned, grads, raw, scales, cosine, sine, gains, count):
    total, features = grads.shape

    def block(x):
        return pl.BlockSpec((count, x.shape[1]), lambda i: (i, 0))

    out_shape = [
        jax.ShapeDtypeStruct((total, 2 * features), F32),
        jax.ShapeDtypeStruct((total, features), BF),
        jax.ShapeDtypeStruct((total, 2), F32),
    ]
    return pl.pallas_call(
        attend_back_body,
        grid=(total // count,),
        in_specs=[block(x) for x in (turned, grads, raw, scales, cosine, sine)]
        + [pl.BlockSpec(gains.shape, lambda i: (0, 0))],
        out_specs=[block(x) for x in out_shape] + [pl.BlockSpec(gains.shape, lambda i: (0, 0))],
        out_shape=[*out_shape, jax.ShapeDtypeStruct(gains.shape, F32)],
        compiler_params=pltpu.CompilerParams(vmem_limit_bytes=VMEM_BYTES),
        cost_estimate=pl.CostEstimate(
            flops=12 * total * count * features,
            bytes_accessed=30 * total * features,
            transcendentals=total * count,
        ),
        name="attend_back",
    )(turned, grads, raw, scales, cosine, sine, gains)


def pick_body(where, *refs):
    half = pl.num_programs(0) // 2

    def fill(out):
        width = out.shape[-1]
        at = 0
        for source in refs[:-2]:
            outer, _, _, own = source.shape
            if own >= width:
                for i in range(outer):
                    for column in range(0, own, width):
                        out[0, at] = source[i, 0, :, column : column + width]
                        at += 1
            else:
                for i in range(0, outer, width // own):
                    for k in range(width // own):
                        out[0, at, :, k * own : (k + 1) * own] = source[i + k, 0]
                    at += 1

    @pl.when(pl.program_id(0) < half)
    def _():
        fill(refs[-2])

    @pl.when(pl.program_id(0) >= half)
    def _():
        fill(refs[-1])


def pick_blocks(order, width, *sources):
    rows = sources[0].shape[2]
    half = order.shape[0] // 2
    outer = sum(x.shape[0] * x.shape[3] for x in sources) // width
    shape = (1, outer, rows, width)
    return pl.pallas_call(
        pick_body,
        grid_spec=pltpu.PrefetchScalarGridSpec(
            num_scalar_prefetch=1,
            grid=(2 * half,),
            in_specs=[
                pl.BlockSpec((x.shape[0], 1, *x.shape[2:]), lambda k, c: (0, c[k], 0, 0))
                for x in sources
            ],
            out_specs=[
                pl.BlockSpec(shape, lambda k, c: (jnp.minimum(k, half - 1), 0, 0, 0)),
                pl.BlockSpec(shape, lambda k, c: (jnp.maximum(k - half, 0), 0, 0, 0)),
            ],
        ),
        out_shape=[jax.ShapeDtypeStruct((half, *shape[1:]), BF)] * 2,
        compiler_params=pltpu.CompilerParams(vmem_limit_bytes=VMEM_BYTES),
        cost_estimate=pl.CostEstimate(
            flops=0, bytes_accessed=8 * half * outer * rows * width, transcendentals=0
        ),
        name="pick_blocks",
    )(order, *sources)


def tie(value, *after):
    return lax.optimization_barrier((value, *after))[0]


def split_low(x):
    top = x.astype(BF)
    return top, (x - top.astype(F32)).astype(BF)


def add_up(parts):
    total = parts[0].astype(F32)
    for part in parts[1:]:
        total = total + part.astype(F32)
    return total


def make_on_device(wide, narrow):
    planes = wide // 2
    local = E // wide
    heads = H // wide
    features = heads * HD
    if local == 8:
        sizes, early, groups = [2, 1, 1, 1, 1, 2], 3, [[0], [1, 2, 3], [4, 5]]
        parts = [[0], [1], [2], [3, 4], [5]]
    else:
        sizes = [1] * local
        early, groups = min(2, local), [[c] for c in range(local)]
        parts = groups
    calls = len(sizes)
    starts = [sum(sizes[:c]) for c in range(calls)]
    slice_ff = FF // narrow
    both_axes = ("wide", "narrow")

    def swap(x, axis, r):
        size = wide if axis == "wide" else narrow
        return lax.ppermute(x, axis, [(i, i ^ r) for i in range(size)])

    bits = [1 << i for i in reversed(range(narrow.bit_length() - 1))]
    near = [0]
    for bit in bits:
        near = near + [r ^ bit for r in near]

    def swap_marked(x, bit, small):
        rest = swap(x[:-small], "narrow", bit)
        marker = swap(x[-small:], "narrow", bit)
        return jnp.concatenate([rest, marker], axis=0), marker

    def gather_narrow(x, *after):
        for i, bit in enumerate(bits):
            if i and after:
                x = tie(x, *after)
            x = jnp.concatenate([x, swap(x, "narrow", bit)], axis=0)
        return x

    def scatter_narrow(keep, send, step=(), last=(), small=0):
        arrivals = []
        for bit in reversed(bits):
            marker = None
            if small and bit == bits[0]:
                came, marker = swap_marked(send[0], bit, small)
                came = came[None]
            else:
                came = swap(send, "narrow", bit)
            if last and bit == bits[0]:
                came = tie(came, *last)
            arrivals.append(came)
            if marker is not None:
                arrivals.append(marker)
            total = keep.astype(F32) + came.astype(F32)
            half = total.shape[0] // 2
            keep, send = total[:half], total[half:].astype(BF)
            if step:
                send = tie(send, *step)
        return total[0], arrivals

    def gather_planes(x):
        return [x] + [swap(x, "wide", 2 * q) for q in range(1, planes)]

    def cross(pieces):
        return [swap(piece, "wide", 1) for piece in pieces]

    def gather_wide(x):
        own = gather_planes(x)
        return own, cross(own)

    def join(own, other):
        return jnp.concatenate([piece for pair in zip(own, other) for piece in pair], axis=0)

    def scatter_wide(own, other):
        return scatter_plane(own, swap(other, "wide", 1))[0]

    def scatter_plane(own, came, *after):
        sums = [own[q].astype(F32) + came[q].astype(F32) for q in range(planes)]
        sent = [x.astype(BF) for x in sums[1:]]
        if after:
            sent = list(lax.optimization_barrier((*sent, *after))[: planes - 1])
        total = sums[0]
        for q in range(1, planes):
            total = total + swap(sent[q - 1], "wide", 2 * q).astype(F32)
        return total, sent

    def on_device(
        tokens, positions, routes, cotangent,
        w_query, w_key, w_value, w_output, w_router,
        gain_attn, gain_query, gain_key, gain_ffn,
        w_gate, w_up, w_down,
    ):
        count = tokens.shape[0]
        rows = w_query.shape[0]
        w = lax.axis_index("wide")
        n = lax.axis_index("narrow")
        where = jnp.stack([n, w * local, w]).astype(jnp.int32)
        wide_order = jnp.arange(wide) ^ w
        near_order = jnp.array(near) ^ n
        narrow_order = jnp.array([near.index(r) for r in range(narrow)])[jnp.arange(narrow) ^ n]

        def by_narrow(*x):
            return pick_blocks(near_order, 2 * features, *x)

        routed = jnp.any(
            routes[:, :, None] == jnp.arange(E, dtype=jnp.int32)[None, None, :], axis=1
        )
        earlier = matmul(
            jnp.tril(jnp.ones((count, count), BF), -1), routed.astype(BF), ((1,), (0,))
        )
        slots = jnp.where(routed, earlier, -1.0).astype(BF).T

        small = jnp.concatenate(
            [
                w_router.reshape(-1), gain_attn, gain_query, gain_key, gain_ffn,
                positions.astype(BF),
            ]
        )
        small_rows = -(-small.shape[0] // LANES)
        bundle_rows = -(-(E + small_rows) // 16) * 16
        small = jnp.pad(small, (0, (bundle_rows - E) * LANES - small.shape[0]))
        bundle = jnp.concatenate([slots, small.reshape(-1, LANES)], axis=0)
        bundle_z = lax.all_gather(bundle, "narrow")
        stacked = jnp.concatenate(
            [x.reshape(rows, wide, features) for x in (w_query, w_key, w_value)], axis=-1
        ).transpose(1, 0, 2)
        columns = lax.all_to_all(stacked, "wide", 0, 0, tiled=True)
        bundles = lax.all_gather(bundle_z, "wide")
        all_slots = bundles[:, :, :E, :]
        all_small = bundles[:, :, E:, :].reshape(wide, narrow, -1)
        base = rows * E
        plane_positions = lax.dynamic_index_in_dim(
            all_small[:, :, base + 4 * rows : base + 4 * rows + count], n, 1, keepdims=False
        )
        plane_positions = jnp.take(plane_positions, wide_order, axis=0).reshape(wide * count)
        router_full = all_small[:, :, :base].reshape(D, E)
        gains = [
            all_small[:, :, base + i * rows : base + (i + 1) * rows].reshape(D).astype(F32)
            for i in range(4)
        ]
        attn_gain, query_gain, key_gain, ffn_gain = gains
        query_gain = lax.dynamic_slice_in_dim(query_gain, w * features, features)
        key_gain = lax.dynamic_slice_in_dim(key_gain, w * features, features)
        expert_counts = jnp.sum((all_slots >= 0).astype(jnp.int32), axis=(0, 1, 3))

        tokens_near = gather_wide(tokens)
        plane_tokens = join(*tokens_near).astype(F32)
        plane_count = plane_tokens.shape[0]

        sliced = [
            slice_weights(w_gate, w_up, starts[p[0]], sum(sizes[c] for c in p), narrow)
            for p in parts
        ]
        expert_weights = []

        def send_weights(*after):
            part = tie(sliced[len(expert_weights)], *after)
            expert_weights.append(lax.all_to_all(part, "narrow", 0, 0, tiled=True))

        ups_z = gather_narrow(cotangent, bundle_z)
        send_weights(columns, bundles, ups_z)
        ups_own = gather_planes(tie(ups_z, *tokens_near[0], *tokens_near[1]))
        columns, w_output = lax.optimization_barrier(
            (columns, w_output, expert_weights[0], *tokens_near[0], *tokens_near[1], *ups_own[:3])
        )[:2]
        columns = gather_narrow(columns[None])
        columns = jnp.take(columns, narrow_order, axis=0)
        qkv = columns.transpose(1, 0, 2, 3).reshape(D, 3 * features)
        output_rows = gather_narrow(w_output[None])
        output_rows = jnp.take(output_rows, narrow_order, axis=0).reshape(features, D)
        while len(expert_weights) < early:
            send_weights(qkv, output_rows, *expert_weights[1:])

        local_slots = lax.dynamic_slice_in_dim(all_slots, w * local, local, axis=2)
        local_slots = jnp.take(jnp.take(local_slots, wide_order, axis=0), near_order, axis=1)
        pairs = narrow // 2
        local_slots = (
            local_slots.reshape(planes, 2, pairs, 2, local, count)
            .transpose(1, 0, 2, 4, 3, 5)
            .reshape(2, planes, pairs, local, 1, 2 * count)
        )
        row = jnp.arange(2 * CAP)[:, None]
        lane = jnp.arange(2 * count)[None, :]
        picks = (
            ((local_slots == (row % CAP).astype(BF)) & (row // CAP == lane // count))
            .astype(BF)
            .reshape(2, planes, pairs, local * 2 * CAP, 2 * count)
        )
        picks_own, picks_other = picks[0], picks[1]
        inverse = lax.rsqrt(jnp.mean(plane_tokens * plane_tokens, axis=-1, keepdims=True) + EPSILON)
        normed = (plane_tokens * inverse * attn_gain).astype(BF)
        raw = matmul(normed, tie(qkv, *ups_own), ((1,), (0,)))

        def row_sums(sums):
            sums = jnp.take(sums.reshape(2, wide, count), wide_order, axis=1)
            gathered = lax.all_gather(sums, "wide")
            sums = jnp.sum(gathered, axis=0)
            return jnp.take(sums, wide_order, axis=1).reshape(2, plane_count), gathered

        squares = jnp.stack(
            [
                jnp.sum(x * x, axis=-1)
                for x in (raw[:, :features], raw[:, features : 2 * features])
            ]
        )
        scales = lax.rsqrt(row_sums(squares)[0] / D + EPSILON).T
        frequency = THETA_BASE ** (-2.0 * jnp.arange(HD // 2, dtype=F32) / HD)
        angles = plane_positions.astype(F32)[:, None] * frequency[None, :]
        cosine, sine = jnp.cos(angles), jnp.sin(angles)
        cosine = jnp.concatenate([cosine, cosine], axis=1)
        sine = jnp.concatenate([-sine, sine], axis=1)
        head_gains = jnp.stack([query_gain, key_gain])
        turned, attended = attend(raw, scales, cosine, sine, head_gains, count)
        if early > 2:
            attended = tie(attended, expert_weights[1])
        branch = matmul(attended, output_rows, ((1,), (0,))).astype(BF)
        branch = branch.reshape(planes, 2, count, D)
        branch = scatter_wide(branch[:, 0], branch[:, 1])

        residual = tokens.astype(F32) + branch
        ffn_r = lax.rsqrt(jnp.mean(residual * residual, axis=-1, keepdims=True) + EPSILON)
        normed_ffn = (residual * ffn_r * ffn_gain).astype(BF)
        logits = matmul(normed_ffn, router_full, ((1,), (0,)))
        router_powers = jnp.exp(logits - jnp.max(logits, axis=-1, keepdims=True))
        router_probs = router_powers / jnp.sum(router_powers, axis=-1, keepdims=True)

        message = jnp.concatenate([normed_ffn, *split_low(router_probs)], axis=1)
        ups = dispatch(picks_own, ups_own, 0)
        ups = dispatch(picks_other, cross(ups_own), 1, ups)
        message = gather_narrow(tie(message, ups, expert_weights[-1]))
        if len(parts) > early:
            send_weights(message)
        tokens_own = gather_planes(message)
        while len(expert_weights) < len(parts):
            send_weights(*tokens_own)
        tokens_own[0] = tie(tokens_own[0], expert_weights[min(early, len(parts) - 1)])
        tokens_other = cross(tokens_own)
        expert_rows = dispatch(picks_own, tokens_own, 0)
        expert_rows = dispatch(picks_other, tokens_other, 1, expert_rows)

        came = []
        held = [None] * 4
        for c in range(calls):
            if c == 1:
                expert_rows = tie(expert_rows, expert_weights[-1])
            group = next(g for g in groups if c in g)
            part = next(i for i, p in enumerate(parts) if c in p)
            if c == group[0]:
                held[2] = None
            held = [*expert_chunk(
                where, expert_rows, ups, expert_weights[part], w_down, starts[c], sizes[c],
                starts[c] - starts[parts[part][0]], sum(sizes[g] for g in group), starts[c] - starts[group[0]], held,
            )]
            if c == group[-1]:
                came.append(held[2])
        results, row_grads, _, down_grad = held
        arrived = []

        def send_grads(*after):
            part = came[len(arrived)]
            part = tie(part, *after) if after else part
            arrived.append(lax.all_to_all(part, "narrow", 0, 0, tiled=True))

        grad_starts = [starts[group[0]] for group in groups]
        sent_early = len(groups) - 1
        for g in range(sent_early):
            send_grads(*([row_grads] if g else []))

        def combine_tokens(terms, *after):
            terms = tie(terms, *after) if after else terms
            other = cross(combine(picks_other, terms, 1))
            return list(combine(picks_own, terms, 0)), other

        def scatter_rest(plane_sum, last=(), small=0):
            blocks = plane_sum.reshape(narrow, count, plane_sum.shape[-1])
            return scatter_narrow(
                blocks[: narrow // 2], blocks[narrow // 2 :], (), last, small
            )

        own, other = combine_tokens(row_grads)
        plane_sum, sent = scatter_plane(own, other)
        mix_own, mix_other = combine_tokens(results, *sent)
        mix_sums = [mix_own[q].astype(F32) + mix_other[q].astype(F32) for q in range(planes)]
        mix_sent = [x.astype(BF) for x in mix_sums[1:]]
        plane_done = plane_sum.astype(BF)
        plane_sum = tie(plane_done, *arrived, *mix_other)
        mix_came = [
            swap(tie(mix_sent[q - 1], plane_done), "wide", 2 * q) for q in range(1, planes)[:2]
        ]
        ffn_message, ffn_came = scatter_rest(plane_sum, mix_came, 16)
        send_grads(ffn_came[-1])
        buffers = None
        for start, part in zip(grad_starts, arrived[:sent_early]):
            buffers = assemble(tie(part, ffn_came[-1]), start, local, buffers)
        ffn_message = tie(ffn_message, *buffers)

        upstream = cotangent.astype(F32)
        prob_grads = ffn_message[:, D : D + E] + ffn_message[:, D + E : D + 2 * E]
        logit_grads = (
            router_probs
            * (prob_grads - jnp.sum(router_probs * prob_grads, axis=-1, keepdims=True))
        ).astype(BF)
        ffn_grads = ffn_message[:, :D] + matmul(logit_grads, router_full, ((1,), (1,)))

        def norm_back(v, r, gain, dy):
            u = dy * gain
            return r * u - v * (r * r * r) * jnp.mean(u * v, axis=-1, keepdims=True)

        residual_grads = upstream + norm_back(residual, ffn_r, ffn_gain, ffn_grads)
        ffn_gain_part = jnp.sum(ffn_grads * residual * ffn_r, axis=0)
        message = jnp.concatenate(
            [residual_grads.astype(BF), logit_grads, jnp.zeros_like(logit_grads)], axis=1
        )

        plane_message = join(*gather_wide(message))
        plane_grads = plane_message[:, :D]
        attended_grads = matmul(plane_grads, output_rows, ((1,), (1,))).astype(BF)
        plane_rows = lax.dynamic_slice_in_dim(
            join([x[:count] for x in tokens_own], [x[:count] for x in tokens_other]),
            w * features,
            features,
            axis=1,
        )
        scaled, value_grads, dots, head_gain_parts = attend_back(
            turned, attended_grads, raw, scales, cosine, sine, head_gains, count
        )

        grad_output = matmul(attended, plane_grads, ((0,), (0,))).astype(BF)
        grad_value = matmul(normed, value_grads, ((0,), (0,))).astype(BF)
        early_parts = by_narrow(
            grad_output.reshape(1, narrow, rows, D),
            grad_value.reshape(wide, narrow, rows, features),
        )

        dots, dots_gathered = row_sums(dots.T)
        dots = dots.T / D
        shrink = scales * scales * scales * dots
        raw_grads = (
            scaled.reshape(plane_count, 2, features) * scales[:, :, None]
            - raw[:, : 2 * features].reshape(plane_count, 2, features) * shrink[:, :, None]
        ).astype(BF)
        raw_grads = jnp.concatenate([raw_grads.reshape(plane_count, 2 * features), value_grads], axis=1)
        mix_came += [
            swap(tie(mix_sent[q - 1], dots_gathered), "wide", 2 * q) for q in range(3, planes)
        ]
        grad_early, early_came = scatter_narrow(*early_parts)
        raw_grads = tie(raw_grads, arrived[-1], early_came[0])
        normed_grads = matmul(raw_grads, qkv, ((1,), (1,))).astype(BF)

        attn_gain_part = jnp.sum(normed_grads.astype(F32) * plane_tokens * inverse, axis=0)
        gain_parts = jnp.concatenate(
            [
                jnp.stack([attn_gain_part, ffn_gain_part]).reshape(2 * wide, features),
                head_gain_parts,
            ]
        ).T
        gain_columns = 2 * wide + 2
        router_part = matmul(plane_rows, plane_message[:, D : D + E], ((0,), (0,)))
        small_parts = jnp.concatenate([router_part.astype(BF), *split_low(gain_parts)], axis=1)
        small_parts = jnp.pad(
            small_parts, ((0, 0), (0, 2 * features - E - 2 * gain_columns))
        )
        plane_normed = normed_grads.reshape(planes, 2, count, D)
        normed_other = swap(plane_normed[:, 1], "wide", 1)
        normed_sums = [add_up([plane_normed[q, 0], normed_other[q]]) for q in range(planes)]
        normed_came = [
            swap(normed_sums[q].astype(BF), "wide", 2 * q)
            for q in range(1, planes)
        ]
        grad_raw = matmul(normed, raw_grads[:, : 2 * features], ((0,), (0,))).astype(BF)
        grad_raw, raw_came = scatter_narrow(
            *by_narrow(
                grad_raw.reshape(wide, narrow, rows, 2 * features),
                small_parts.reshape(1, narrow, rows, 2 * features),
            ),
            (),
            normed_came,
        )
        small_parts = grad_raw[wide]
        grad_router = small_parts[:, :E]
        gain_parts = small_parts[:, E : E + 2 * gain_columns]
        gain_parts = (gain_parts[:, :gain_columns] + gain_parts[:, gain_columns:]).T
        grad_gain_query, grad_gain_key = gain_parts[2 * wide], gain_parts[2 * wide + 1]
        blocks = D // (2 * features)
        grad_output = jnp.concatenate([grad_early[i] for i in range(blocks)], axis=1)
        grad_value = (
            grad_early[blocks:]
            .reshape(wide // 2, rows, 2, features)
            .transpose(0, 2, 1, 3)
            .reshape(wide, rows, features)
        )
        grad_qkv = jnp.concatenate([grad_raw[:wide], grad_value], axis=-1)
        mix_came[-1] = tie(mix_came[-1], raw_came[0])
        mixture = add_up([mix_sums[0], *mix_came]).astype(BF)
        block_out = (residual + scatter_rest(mixture)[0]).astype(BF)
        gain_rows = jnp.concatenate(
            [*split_low(gain_parts[:wide]), *split_low(gain_parts[wide : 2 * wide])], axis=1
        )
        gain_rows = jnp.pad(
            gain_rows[:, None, :], ((0, 0), (0, 15), (0, 3 * features - 4 * rows))
        )
        grad_qkv = jnp.concatenate([grad_qkv.astype(BF), gain_rows], axis=1)
        grad_qkv = lax.all_to_all(grad_qkv, "wide", 0, 0, tiled=True)
        gain_rows = jnp.sum(grad_qkv[:, rows, : 4 * rows].astype(F32), axis=0).reshape(4, rows)
        gain_sums = [gain_rows[0] + gain_rows[1], gain_rows[2] + gain_rows[3]]
        grad_qkv = grad_qkv[:, :rows].transpose(1, 0, 2).astype(F32)
        grad_query, grad_key, grad_value = [
            grad_qkv[..., i * features : (i + 1) * features].reshape(rows, D) for i in range(3)
        ]

        normed_grads = add_up([normed_sums[0], *normed_came])
        input_grad = (
            residual_grads
            + norm_back(tokens.astype(F32), inverse[:count], attn_gain, normed_grads)
        ).astype(BF)

        for start, part in zip(grad_starts[sent_early:], arrived[sent_early:]):
            buffers = assemble(tie(part, raw_came[1]), start, local, buffers)
        grad_gate, grad_up = buffers

        return (
            block_out, input_grad, grad_query, grad_key, grad_value,
            grad_output, grad_router,
            gain_sums[0], grad_gain_query, grad_gain_key, gain_sums[1],
            grad_gate, grad_up, down_grad, expert_counts,
        )

    return on_device


def solution(mesh):
    both = ("wide", "narrow")
    in_specs = (P(both, None), P(both), P(both, None), P(both, None))
    in_specs += (P(both, None),) * 5 + (P(both),) * 4 + (P("wide", "narrow", None),) * 3
    out_specs = (P(both, None),) * 7 + (P(both),) * 4 + (P("wide", "narrow", None),) * 3 + (P(),)
    return jax.shard_map(
        make_on_device(mesh.shape["wide"], mesh.shape["narrow"]),
        mesh=mesh,
        in_specs=in_specs,
        out_specs=out_specs,
        check_vma=False,
    )
```

```python
import functools

import jax
import jax.numpy as jnp
from jax import lax
from jax.experimental import pallas as pl
from jax.experimental.pallas import tpu as pltpu
from jax.sharding import PartitionSpec as P

D = 2048
H = 16
HD = 128
E = 64
TOPK = 8
CAP = 24
FF = 1024
LANES = 128
EXPERT_TILE = 768
EPSILON = 1e-05
THETA_BASE = 10000.0

BF = jnp.bfloat16
F32 = jnp.float32
VMEM_BYTES = 56 * 1024 * 1024


def matmul(a, b, dims):
    return lax.dot_general(a, b, (dims, ((), ())), preferred_element_type=F32)


def dispatch_body(pieces, each, *refs):
    picks = refs[0]
    sources = refs[1 : 1 + pieces]
    out = refs[-1]
    for q in range(pieces):
        rows = matmul(picks[q, 0], sources[q][...], ((1,), (0,))).astype(BF)
        out[:, q * each : (q + 1) * each, :] = rows.reshape(-1, each, rows.shape[-1])


def dispatch(picks, sources, half, buffer=None):
    pieces, pairs, slots, span = picks.shape
    width = sources[0].shape[1]
    each = 2 * CAP
    block = pieces * each
    in_specs = [pl.BlockSpec((pieces, 1, slots, span), lambda j: (0, j, 0, 0))]
    in_specs += [pl.BlockSpec((span, width), lambda j: (j, 0))] * pieces
    args = [picks, *sources]
    aliases = {}
    if buffer is not None:
        in_specs.append(pl.BlockSpec(memory_space=pl.ANY))
        aliases = {len(args): 0}
        args.append(buffer)
    return pl.pallas_call(
        functools.partial(dispatch_body, pieces, each),
        grid=(pairs,),
        in_specs=in_specs,
        out_specs=pl.BlockSpec(
            (slots // each, block, width), lambda j: (0, half * pairs + j, 0)
        ),
        out_shape=jax.ShapeDtypeStruct((slots // each, 2 * pairs * block, width), BF),
        input_output_aliases=aliases,
        compiler_params=pltpu.CompilerParams(vmem_limit_bytes=VMEM_BYTES),
        cost_estimate=pl.CostEstimate(
            flops=2 * pieces * pairs * slots * span * width,
            bytes_accessed=2 * pieces * pairs * (slots + span) * width,
            transcendentals=0,
        ),
        name="dispatch",
    )(*args)


def combine_body(pieces, each, picks, rows, *outs):
    for q in range(pieces):
        part = rows[:, q * each : (q + 1) * each, :].reshape(-1, rows.shape[-1])
        outs[q][...] = matmul(picks[q, 0], part, ((0,), (0,))).astype(BF)


def combine(picks, rows, half):
    pieces, pairs, slots, span = picks.shape
    each = 2 * CAP
    local, _, width = rows.shape
    return pl.pallas_call(
        functools.partial(combine_body, pieces, each),
        grid=(pairs,),
        in_specs=[
            pl.BlockSpec((pieces, 1, slots, span), lambda j: (0, j, 0, 0)),
            pl.BlockSpec((local, pieces * each, width), lambda j: (0, half * pairs + j, 0)),
        ],
        out_specs=[pl.BlockSpec((span, width), lambda j: (j, 0))] * pieces,
        out_shape=[jax.ShapeDtypeStruct((pairs * span, width), BF)] * pieces,
        compiler_params=pltpu.CompilerParams(vmem_limit_bytes=VMEM_BYTES),
        cost_estimate=pl.CostEstimate(
            flops=2 * pieces * pairs * slots * span * width,
            bytes_accessed=2 * pieces * pairs * (slots + span) * width,
            transcendentals=0,
        ),
        name="combine",
    )(picks, rows)


def expert_body(parts, tiles, start, aliased, *refs):
    where, rows_ref, ups_ref, weights_ref, down_ref = refs[:5]
    rest = refs[5 + aliased :]
    results_ref, row_grads_ref, weight_grads_ref, down_grad_ref, result_grads, *sums = rest
    tile = pl.program_id(1)
    width = FF // parts
    depth = D // parts
    slices = [slice(s * depth, (s + 1) * depth) for s in range(parts)]

    both = None
    for s in range(parts):
        term = matmul(rows_ref[0, :, slices[s]], weights_ref[s, 0], ((1,), (0,)))
        both = term if both is None else both + term
    gate_value = both[:, :width]
    up_value = both[:, width:]
    sigma = 1.0 / (1.0 + jnp.exp(-gate_value))
    silu = gate_value * sigma
    hidden = (silu * up_value).astype(BF)

    expert = where[1] + start + pl.program_id(0)
    lane = lax.broadcasted_iota(jnp.int32, (rows_ref.shape[1], LANES), 1)
    high = lane == expert
    low = lane == expert + E
    probs = rows_ref[0, :, D:].astype(F32)
    weight = jnp.sum(jnp.where(high | low, probs, 0.0), axis=1, keepdims=True)

    gate_grad = None
    hidden_grads = None
    for columns in slices:
        down = down_ref[0, :, columns]
        results = matmul(hidden, down, ((1,), (0,)))
        upstream = ups_ref[0, :, columns].astype(F32)
        dot = jnp.sum(upstream * results, axis=1, keepdims=True)
        gate_grad = dot if gate_grad is None else gate_grad + dot
        results_ref[0, :, columns] = (weight * results).astype(BF)
        part = (weight * upstream).astype(BF)
        result_grads[:, columns] = part
        term = matmul(part, down, ((1,), (1,)))
        hidden_grads = term if hidden_grads is None else hidden_grads + term

    gate_value_grads = (
        hidden_grads * up_value * (sigma * (1.0 + gate_value * (1.0 - sigma)))
    ).astype(BF)
    up_value_grads = (hidden_grads * silu).astype(BF)
    both_grads = jnp.concatenate([gate_value_grads, up_value_grads], axis=1)
    top = gate_grad.astype(BF)
    bottom = (gate_grad - top.astype(F32)).astype(BF)
    row_grads_ref[0, :, D:] = jnp.where(
        high, top.astype(F32), jnp.where(low, bottom.astype(F32), 0.0)
    ).astype(BF)
    for s in range(parts):
        row_grads_ref[0, :, slices[s]] = matmul(
            both_grads, weights_ref[s, 0], ((1,), (1,))
        ).astype(BF)

    def weight_term(s):
        return matmul(rows_ref[0, :, slices[s]], both_grads, ((0,), (0,)))

    def down_term(columns):
        return matmul(hidden, result_grads[:, columns], ((0,), (0,)))

    if tiles == 1:
        for s in range(parts):
            weight_grads_ref[s, 0] = weight_term(s).astype(BF)
            down_grad_ref[0, :, slices[s]] = down_term(slices[s])
        return
    weight_sums = sums[0]
    first = tile == 0

    @pl.when(first)
    def _():
        for s in range(parts):
            weight_sums[s] = weight_term(s)
            down_grad_ref[0, :, slices[s]] = down_term(slices[s])

    @pl.when(jnp.logical_not(first))
    def _():
        for s in range(parts):
            weight_sums[s] += weight_term(s)
            down_grad_ref[0, :, slices[s]] += down_term(slices[s])

    @pl.when(tile == tiles - 1)
    def _():
        for s in range(parts):
            weight_grads_ref[s, 0] = weight_sums[s].astype(BF)


def expert_chunk(where, rows, ups, weights, down, start, experts, offset, group, at, buffers):
    parts, _, depth, width2 = weights.shape
    local, total_rows, wide_row = rows.shape
    tile = EXPERT_TILE
    tiles = total_rows // tile
    slice_ff = down.shape[1]
    weight_spec = pl.BlockSpec((parts, 1, depth, width2), lambda e, i, c: (0, offset + e, 0, 0))
    down_spec = pl.BlockSpec((1, slice_ff, D), lambda e, i, c: (start + e, 0, 0))
    in_specs = [
        pl.BlockSpec((1, tile, wide_row), lambda e, i, c: (start + e, i, 0)),
        pl.BlockSpec((1, tile, D), lambda e, i, c: (start + e, i, 0)),
        weight_spec,
        down_spec,
    ]
    args = [where, rows, ups, weights, down]
    aliases = {}
    for index, buffer in enumerate(buffers):
        if buffer is not None:
            in_specs.append(pl.BlockSpec(memory_space=pl.ANY))
            aliases[len(args)] = index
            args.append(buffer)
    return pl.pallas_call(
        functools.partial(expert_body, parts, tiles, start, len(aliases)),
        grid_spec=pltpu.PrefetchScalarGridSpec(
            num_scalar_prefetch=1,
            grid=(experts, tiles),
            in_specs=in_specs,
            out_specs=[
                pl.BlockSpec((1, tile, D), lambda e, i, c: (start + e, i, 0)),
                pl.BlockSpec((1, tile, wide_row), lambda e, i, c: (start + e, i, 0)),
                pl.BlockSpec((parts, 1, depth, width2), lambda e, i, c: (0, at + e, 0, 0)),
                down_spec,
            ],
            scratch_shapes=[pltpu.VMEM((tile, D), BF)]
            + ([pltpu.VMEM((parts, depth, width2), F32)] if tiles > 1 else []),
        ),
        out_shape=[
            jax.ShapeDtypeStruct((local, total_rows, D), BF),
            jax.ShapeDtypeStruct((local, total_rows, wide_row), BF),
            jax.ShapeDtypeStruct((parts, group, depth, width2), BF),
            jax.ShapeDtypeStruct((local, slice_ff, D), F32),
        ],
        input_output_aliases=aliases,
        compiler_params=pltpu.CompilerParams(vmem_limit_bytes=VMEM_BYTES),
        cost_estimate=pl.CostEstimate(
            flops=18 * experts * total_rows * D * slice_ff,
            bytes_accessed=8 * experts * total_rows * D + 18 * experts * D * slice_ff,
            transcendentals=experts * total_rows * slice_ff,
        ),
        name="experts",
    )(*args)


def slice_body(parts, width, gate_ref, up_ref, out):
    for s in range(parts):
        columns = slice(s * width, (s + 1) * width)
        out[s, 0, :, :width] = gate_ref[0, :, columns]
        out[s, 0, :, width:] = up_ref[0, :, columns]


def slice_weights(gate, up, start, experts, parts):
    depth = gate.shape[1]
    width = FF // parts
    spec = pl.BlockSpec((1, depth, FF), lambda e: (start + e, 0, 0))
    return pl.pallas_call(
        functools.partial(slice_body, parts, width),
        grid=(experts,),
        in_specs=[spec, spec],
        out_specs=pl.BlockSpec((parts, 1, depth, 2 * width), lambda e: (0, e, 0, 0)),
        out_shape=jax.ShapeDtypeStruct((parts, experts, depth, 2 * width), BF),
        compiler_params=pltpu.CompilerParams(vmem_limit_bytes=VMEM_BYTES),
        cost_estimate=pl.CostEstimate(
            flops=0, bytes_accessed=8 * experts * depth * FF, transcendentals=0
        ),
        name="slice_weights",
    )(gate, up)


def assemble_body(parts, width, *refs):
    source = refs[0]
    gate_ref, up_ref = refs[-2], refs[-1]
    for s in range(parts):
        columns = slice(s * width, (s + 1) * width)
        gate_ref[0, :, columns] = source[s, 0, :, :width].astype(F32)
        up_ref[0, :, columns] = source[s, 0, :, width:].astype(F32)


def assemble(source, start, local, buffers):
    parts, experts, depth, width2 = source.shape
    in_specs = [pl.BlockSpec((parts, 1, depth, width2), lambda e: (0, e, 0, 0))]
    args = [source]
    aliases = {}
    if buffers is not None:
        in_specs += [pl.BlockSpec(memory_space=pl.ANY)] * 2
        aliases = {1: 0, 2: 1}
        args += list(buffers)
    spec = pl.BlockSpec((1, depth, FF), lambda e: (start + e, 0, 0))
    return pl.pallas_call(
        functools.partial(assemble_body, parts, width2 // 2),
        grid=(experts,),
        in_specs=in_specs,
        out_specs=[spec, spec],
        out_shape=[jax.ShapeDtypeStruct((local, depth, FF), F32)] * 2,
        input_output_aliases=aliases,
        compiler_params=pltpu.CompilerParams(vmem_limit_bytes=VMEM_BYTES),
        cost_estimate=pl.CostEstimate(
            flops=0, bytes_accessed=6 * experts * depth * FF * 2, transcendentals=0
        ),
        name="assemble",
    )(*args)


def turn(x, cosine, sine):
    return x * cosine + pltpu.roll(x, HD // 2, 1) * sine


def probabilities(query, key):
    scores = matmul(query, key, ((1,), (1,))) * HD ** (-0.5)
    row = lax.broadcasted_iota(jnp.int32, scores.shape, 0)
    column = lax.broadcasted_iota(jnp.int32, scores.shape, 1)
    causal = row >= column
    scores = jnp.where(causal, scores, -1e30)
    powers = jnp.exp(scores - jnp.max(scores, axis=-1, keepdims=True))
    return powers / jnp.sum(powers, axis=-1, keepdims=True), causal


def attend_body(raw, scales, cosine, sine, gains, turned, attended):
    features = attended.shape[1]
    for part in range(2):
        scale = scales[:, part : part + 1]
        for at in range(0, features, HD):
            columns = slice(part * features + at, part * features + at + HD)
            x = raw[:, columns] * scale * gains[part : part + 1, at : at + HD]
            turned[:, columns] = turn(x, cosine[...], sine[...]).astype(BF)
    turned[:, 2 * features :] = raw[:, 2 * features :].astype(BF)
    for at in range(0, features, HD):
        query = turned[:, at : at + HD]
        key = turned[:, features + at : features + at + HD]
        value = turned[:, 2 * features + at : 2 * features + at + HD]
        probs, _ = probabilities(query, key)
        attended[:, at : at + HD] = matmul(probs.astype(BF), value, ((1,), (0,))).astype(BF)


def attend(raw, scales, cosine, sine, gains, count):
    total, features = raw.shape[0], raw.shape[1] // 3

    def block(x):
        return pl.BlockSpec((count, x.shape[1]), lambda i: (i, 0))

    return pl.pallas_call(
        attend_body,
        grid=(total // count,),
        in_specs=[block(x) for x in (raw, scales, cosine, sine)]
        + [pl.BlockSpec(gains.shape, lambda i: (0, 0))],
        out_specs=[
            pl.BlockSpec((count, 3 * features), lambda i: (i, 0)),
            pl.BlockSpec((count, features), lambda i: (i, 0)),
        ],
        out_shape=[
            jax.ShapeDtypeStruct((total, 3 * features), BF),
            jax.ShapeDtypeStruct((total, features), BF),
        ],
        compiler_params=pltpu.CompilerParams(vmem_limit_bytes=VMEM_BYTES),
        cost_estimate=pl.CostEstimate(
            flops=4 * total * count * features,
            bytes_accessed=20 * total * features,
            transcendentals=total * count,
        ),
        name="attend",
    )(raw, scales, cosine, sine, gains)


def attend_back_body(turned, grads, raw, scales, cosine, sine, gains, scaled, value_grads, sums, gain_grads):
    features = grads.shape[1]
    scale = HD ** (-0.5)
    dots = [0.0, 0.0]
    first = pl.program_id(0) == 0
    for at in range(0, features, HD):
        query = turned[:, at : at + HD]
        key = turned[:, features + at : features + at + HD]
        value = turned[:, 2 * features + at : 2 * features + at + HD]
        grad = grads[:, at : at + HD]
        probs, causal = probabilities(query, key)
        value_grads[:, at : at + HD] = matmul(probs.astype(BF), grad, ((0,), (0,))).astype(BF)
        prob_grads = matmul(grad, value, ((1,), (1,)))
        score_grads = probs * (prob_grads - jnp.sum(probs * prob_grads, axis=-1, keepdims=True))
        score_grads = jnp.where(causal, score_grads, 0.0).astype(BF)
        turned_grads = (
            matmul(score_grads, key, ((1,), (0,))) * scale,
            matmul(score_grads, query, ((0,), (0,))) * scale,
        )
        for part in range(2):
            columns = slice(part * features + at, part * features + at + HD)
            x = raw[:, columns]
            dy = turn(turned_grads[part], cosine[...], -sine[...])
            u = dy * gains[part : part + 1, at : at + HD]
            scaled[:, columns] = u
            dots[part] = dots[part] + jnp.sum(u * x, axis=-1, keepdims=True)
            gain_grad = jnp.sum(dy * x * scales[:, part : part + 1], axis=0, keepdims=True)
            old = gain_grads[part : part + 1, at : at + HD]
            gain_grads[part : part + 1, at : at + HD] = gain_grad + jnp.where(first, 0.0, old)
    sums[...] = jnp.concatenate(dots, axis=1)


def attend_back(turned, grads, raw, scales, cosine, sine, gains, count):
    total, features = grads.shape

    def block(x):
        return pl.BlockSpec((count, x.shape[1]), lambda i: (i, 0))

    out_shape = [
        jax.ShapeDtypeStruct((total, 2 * features), F32),
        jax.ShapeDtypeStruct((total, features), BF),
        jax.ShapeDtypeStruct((total, 2), F32),
    ]
    return pl.pallas_call(
        attend_back_body,
        grid=(total // count,),
        in_specs=[block(x) for x in (turned, grads, raw, scales, cosine, sine)]
        + [pl.BlockSpec(gains.shape, lambda i: (0, 0))],
        out_specs=[block(x) for x in out_shape] + [pl.BlockSpec(gains.shape, lambda i: (0, 0))],
        out_shape=[*out_shape, jax.ShapeDtypeStruct(gains.shape, F32)],
        compiler_params=pltpu.CompilerParams(vmem_limit_bytes=VMEM_BYTES),
        cost_estimate=pl.CostEstimate(
            flops=12 * total * count * features,
            bytes_accessed=30 * total * features,
            transcendentals=total * count,
        ),
        name="attend_back",
    )(turned, grads, raw, scales, cosine, sine, gains)


def pick_body(where, *refs):
    half = pl.num_programs(0) // 2

    def fill(out):
        width = out.shape[-1]
        at = 0
        for source in refs[:-2]:
            outer, _, _, own = source.shape
            if own >= width:
                for i in range(outer):
                    for column in range(0, own, width):
                        out[0, at] = source[i, 0, :, column : column + width]
                        at += 1
            else:
                for i in range(0, outer, width // own):
                    for k in range(width // own):
                        out[0, at, :, k * own : (k + 1) * own] = source[i + k, 0]
                    at += 1

    @pl.when(pl.program_id(0) < half)
    def _():
        fill(refs[-2])

    @pl.when(pl.program_id(0) >= half)
    def _():
        fill(refs[-1])


def pick_blocks(order, width, *sources):
    rows = sources[0].shape[2]
    half = order.shape[0] // 2
    outer = sum(x.shape[0] * x.shape[3] for x in sources) // width
    shape = (1, outer, rows, width)
    return pl.pallas_call(
        pick_body,
        grid_spec=pltpu.PrefetchScalarGridSpec(
            num_scalar_prefetch=1,
            grid=(2 * half,),
            in_specs=[
                pl.BlockSpec((x.shape[0], 1, *x.shape[2:]), lambda k, c: (0, c[k], 0, 0))
                for x in sources
            ],
            out_specs=[
                pl.BlockSpec(shape, lambda k, c: (jnp.minimum(k, half - 1), 0, 0, 0)),
                pl.BlockSpec(shape, lambda k, c: (jnp.maximum(k - half, 0), 0, 0, 0)),
            ],
        ),
        out_shape=[jax.ShapeDtypeStruct((half, *shape[1:]), BF)] * 2,
        compiler_params=pltpu.CompilerParams(vmem_limit_bytes=VMEM_BYTES),
        cost_estimate=pl.CostEstimate(
            flops=0, bytes_accessed=8 * half * outer * rows * width, transcendentals=0
        ),
        name="pick_blocks",
    )(order, *sources)


def tie(value, *after):
    return lax.optimization_barrier((value, *after))[0]


def split_low(x):
    top = x.astype(BF)
    return top, (x - top.astype(F32)).astype(BF)


def add_up(parts):
    total = parts[0].astype(F32)
    for part in parts[1:]:
        total = total + part.astype(F32)
    return total


def make_on_device(wide, narrow):
    planes = wide // 2
    local = E // wide
    heads = H // wide
    features = heads * HD
    if local == 8:
        sizes, early, groups = [2, 1, 1, 1, 1, 2], 3, [[0], [1, 2, 3], [4, 5]]
        parts = [[0], [1], [2], [3, 4], [5]]
    else:
        sizes = [1] * local
        early, groups = min(2, local), [[c] for c in range(local)]
        parts = groups
    calls = len(sizes)
    starts = [sum(sizes[:c]) for c in range(calls)]
    slice_ff = FF // narrow
    both_axes = ("wide", "narrow")

    def swap(x, axis, r):
        size = wide if axis == "wide" else narrow
        return lax.ppermute(x, axis, [(i, i ^ r) for i in range(size)])

    bits = [1 << i for i in reversed(range(narrow.bit_length() - 1))]
    near = [0]
    for bit in bits:
        near = near + [r ^ bit for r in near]

    def swap_marked(x, bit, small):
        rest = swap(x[:-small], "narrow", bit)
        marker = swap(x[-small:], "narrow", bit)
        return jnp.concatenate([rest, marker], axis=0), marker

    def gather_narrow(x, *after):
        for i, bit in enumerate(bits):
            if i and after:
                x = tie(x, *after)
            x = jnp.concatenate([x, swap(x, "narrow", bit)], axis=0)
        return x

    def scatter_narrow(keep, send, step=(), last=(), small=0):
        arrivals = []
        for bit in reversed(bits):
            marker = None
            if small and bit == bits[0]:
                came, marker = swap_marked(send[0], bit, small)
                came = came[None]
            else:
                came = swap(send, "narrow", bit)
            if last and bit == bits[0]:
                came = tie(came, *last)
            arrivals.append(came)
            if marker is not None:
                arrivals.append(marker)
            total = keep.astype(F32) + came.astype(F32)
            half = total.shape[0] // 2
            keep, send = total[:half], total[half:].astype(BF)
            if step:
                send = tie(send, *step)
        return total[0], arrivals

    def gather_planes(x):
        return [x] + [swap(x, "wide", 2 * q) for q in range(1, planes)]

    def cross(pieces):
        return [swap(piece, "wide", 1) for piece in pieces]

    def gather_wide(x):
        own = gather_planes(x)
        return own, cross(own)

    def join(own, other):
        return jnp.concatenate([piece for pair in zip(own, other) for piece in pair], axis=0)

    def scatter_wide(own, other):
        return scatter_plane(own, swap(other, "wide", 1))[0]

    def scatter_plane(own, came, *after):
        sums = [own[q].astype(F32) + came[q].astype(F32) for q in range(planes)]
        sent = [x.astype(BF) for x in sums[1:]]
        if after:
            sent = list(lax.optimization_barrier((*sent, *after))[: planes - 1])
        total = sums[0]
        for q in range(1, planes):
            total = total + swap(sent[q - 1], "wide", 2 * q).astype(F32)
        return total, sent

    def on_device(
        tokens, positions, routes, cotangent,
        w_query, w_key, w_value, w_output, w_router,
        gain_attn, gain_query, gain_key, gain_ffn,
        w_gate, w_up, w_down,
    ):
        count = tokens.shape[0]
        rows = w_query.shape[0]
        w = lax.axis_index("wide")
        n = lax.axis_index("narrow")
        where = jnp.stack([n, w * local, w]).astype(jnp.int32)
        wide_order = jnp.arange(wide) ^ w
        near_order = jnp.array(near) ^ n
        narrow_order = jnp.array([near.index(r) for r in range(narrow)])[jnp.arange(narrow) ^ n]

        def by_narrow(*x):
            return pick_blocks(near_order, 2 * features, *x)

        routed = jnp.any(
            routes[:, :, None] == jnp.arange(E, dtype=jnp.int32)[None, None, :], axis=1
        )
        earlier = matmul(
            jnp.tril(jnp.ones((count, count), BF), -1), routed.astype(BF), ((1,), (0,))
        )
        slots = jnp.where(routed, earlier, -1.0).astype(BF).T

        small = jnp.concatenate(
            [
                w_router.reshape(-1), gain_attn, gain_query, gain_key, gain_ffn,
                positions.astype(BF),
            ]
        )
        small_rows = -(-small.shape[0] // LANES)
        bundle_rows = -(-(E + small_rows) // 16) * 16
        small = jnp.pad(small, (0, (bundle_rows - E) * LANES - small.shape[0]))
        bundle = jnp.concatenate([slots, small.reshape(-1, LANES)], axis=0)
        bundle_z = lax.all_gather(bundle, "narrow")
        stacked = jnp.concatenate(
            [x.reshape(rows, wide, features) for x in (w_query, w_key, w_value)], axis=-1
        ).transpose(1, 0, 2)
        columns = lax.all_to_all(stacked, "wide", 0, 0, tiled=True)
        bundles = lax.all_gather(bundle_z, "wide")
        all_slots = bundles[:, :, :E, :]
        all_small = bundles[:, :, E:, :].reshape(wide, narrow, -1)
        base = rows * E
        plane_positions = lax.dynamic_index_in_dim(
            all_small[:, :, base + 4 * rows : base + 4 * rows + count], n, 1, keepdims=False
        )
        plane_positions = jnp.take(plane_positions, wide_order, axis=0).reshape(wide * count)
        router_full = all_small[:, :, :base].reshape(D, E)
        gains = [
            all_small[:, :, base + i * rows : base + (i + 1) * rows].reshape(D).astype(F32)
            for i in range(4)
        ]
        attn_gain, query_gain, key_gain, ffn_gain = gains
        query_gain = lax.dynamic_slice_in_dim(query_gain, w * features, features)
        key_gain = lax.dynamic_slice_in_dim(key_gain, w * features, features)
        expert_counts = jnp.sum((all_slots >= 0).astype(jnp.int32), axis=(0, 1, 3))

        tokens_near = gather_wide(tokens)
        plane_tokens = join(*tokens_near).astype(F32)
        plane_count = plane_tokens.shape[0]

        sliced = [
            slice_weights(w_gate, w_up, starts[p[0]], sum(sizes[c] for c in p), narrow)
            for p in parts
        ]
        expert_weights = []

        def send_weights(*after):
            part = tie(sliced[len(expert_weights)], *after)
            expert_weights.append(lax.all_to_all(part, "narrow", 0, 0, tiled=True))

        ups_z = gather_narrow(cotangent, bundle_z)
        output_rows = gather_narrow(w_output[None])
        send_weights(columns, bundles, ups_z)
        output_rows = jnp.take(output_rows, narrow_order, axis=0).reshape(features, D)
        ups_own = gather_planes(tie(ups_z, *tokens_near[0], *tokens_near[1]))
        columns = lax.optimization_barrier(
            (columns, expert_weights[0], *tokens_near[0], *tokens_near[1], *ups_own[:3])
        )[0]
        columns = gather_narrow(columns[None])
        gathered = columns
        columns = jnp.take(columns, narrow_order, axis=0)
        qkv = columns.transpose(1, 0, 2, 3).reshape(D, 3 * features)
        while len(expert_weights) < early:
            send_weights(gathered, *expert_weights[1:])

        local_slots = lax.dynamic_slice_in_dim(all_slots, w * local, local, axis=2)
        local_slots = jnp.take(jnp.take(local_slots, wide_order, axis=0), near_order, axis=1)
        pairs = narrow // 2
        local_slots = (
            local_slots.reshape(planes, 2, pairs, 2, local, count)
            .transpose(1, 0, 2, 4, 3, 5)
            .reshape(2, planes, pairs, local, 1, 2 * count)
        )
        row = jnp.arange(2 * CAP)[:, None]
        lane = jnp.arange(2 * count)[None, :]
        picks = (
            ((local_slots == (row % CAP).astype(BF)) & (row // CAP == lane // count))
            .astype(BF)
            .reshape(2, planes, pairs, local * 2 * CAP, 2 * count)
        )
        picks_own, picks_other = picks[0], picks[1]
        inverse = lax.rsqrt(jnp.mean(plane_tokens * plane_tokens, axis=-1, keepdims=True) + EPSILON)
        normed = (plane_tokens * inverse * attn_gain).astype(BF)
        raw = matmul(normed, tie(qkv, *ups_own), ((1,), (0,)))

        def row_sums(sums):
            sums = jnp.take(sums.reshape(2, wide, count), wide_order, axis=1)
            gathered = lax.all_gather(sums, "wide")
            sums = jnp.sum(gathered, axis=0)
            return jnp.take(sums, wide_order, axis=1).reshape(2, plane_count), gathered

        squares = jnp.stack(
            [
                jnp.sum(x * x, axis=-1)
                for x in (raw[:, :features], raw[:, features : 2 * features])
            ]
        )
        scales = lax.rsqrt(row_sums(squares)[0] / D + EPSILON).T
        frequency = THETA_BASE ** (-2.0 * jnp.arange(HD // 2, dtype=F32) / HD)
        angles = plane_positions.astype(F32)[:, None] * frequency[None, :]
        cosine, sine = jnp.cos(angles), jnp.sin(angles)
        cosine = jnp.concatenate([cosine, cosine], axis=1)
        sine = jnp.concatenate([-sine, sine], axis=1)
        head_gains = jnp.stack([query_gain, key_gain])
        turned, attended = attend(raw, scales, cosine, sine, head_gains, count)
        if early > 2:
            attended = tie(attended, expert_weights[1], sliced[2])
        branch = matmul(attended, output_rows, ((1,), (0,))).astype(BF)
        branch = branch.reshape(planes, 2, count, D)
        branch = scatter_wide(branch[:, 0], branch[:, 1])

        residual = tokens.astype(F32) + branch
        ffn_r = lax.rsqrt(jnp.mean(residual * residual, axis=-1, keepdims=True) + EPSILON)
        normed_ffn = (residual * ffn_r * ffn_gain).astype(BF)
        logits = matmul(normed_ffn, router_full, ((1,), (0,)))
        router_powers = jnp.exp(logits - jnp.max(logits, axis=-1, keepdims=True))
        router_probs = router_powers / jnp.sum(router_powers, axis=-1, keepdims=True)

        message = jnp.concatenate([normed_ffn, *split_low(router_probs)], axis=1)
        ups = dispatch(picks_own, ups_own, 0)
        ups = dispatch(picks_other, cross(ups_own), 1, ups)
        message = gather_narrow(tie(message, ups, expert_weights[-1]))
        if len(parts) > early:
            send_weights(message)
        tokens_own = gather_planes(message)
        while len(expert_weights) < len(parts):
            send_weights(*tokens_own)
        tokens_own[0] = tie(tokens_own[0], expert_weights[min(early, len(parts) - 1)])
        tokens_other = cross(tokens_own)
        expert_rows = dispatch(picks_own, tokens_own, 0)
        expert_rows = dispatch(picks_other, tokens_other, 1, expert_rows)

        came = []
        held = [None] * 4
        for c in range(calls):
            if c == 1:
                expert_rows = tie(expert_rows, expert_weights[-1])
            group = next(g for g in groups if c in g)
            part = next(i for i, p in enumerate(parts) if c in p)
            if c == group[0]:
                held[2] = None
            held = [*expert_chunk(
                where, expert_rows, ups, expert_weights[part], w_down, starts[c], sizes[c],
                starts[c] - starts[parts[part][0]], sum(sizes[g] for g in group), starts[c] - starts[group[0]], held,
            )]
            if c == group[-1]:
                came.append(held[2])
        results, row_grads, _, down_grad = held
        arrived = []

        def send_grads(*after):
            part = came[len(arrived)]
            part = tie(part, *after) if after else part
            arrived.append(lax.all_to_all(part, "narrow", 0, 0, tiled=True))

        grad_starts = [starts[group[0]] for group in groups]
        sent_early = len(groups) - 1
        for g in range(sent_early):
            send_grads(*([row_grads] if g else []))

        def combine_tokens(terms, *after):
            terms = tie(terms, *after) if after else terms
            other = cross(combine(picks_other, terms, 1))
            return list(combine(picks_own, terms, 0)), other

        def scatter_rest(plane_sum, last=(), small=0):
            blocks = plane_sum.reshape(narrow, count, plane_sum.shape[-1])
            return scatter_narrow(
                blocks[: narrow // 2], blocks[narrow // 2 :], (), last, small
            )

        own, other = combine_tokens(row_grads)
        plane_sum, sent = scatter_plane(own, other)
        mix_own, mix_other = combine_tokens(results, *sent)
        mix_sums = [mix_own[q].astype(F32) + mix_other[q].astype(F32) for q in range(planes)]
        mix_sent = [x.astype(BF) for x in mix_sums[1:]]
        plane_done = plane_sum.astype(BF)
        plane_sum = tie(plane_done, *arrived, *mix_other)
        mix_came = [
            swap(tie(mix_sent[q - 1], plane_done), "wide", 2 * q) for q in range(1, planes)[:2]
        ]
        ffn_message, ffn_came = scatter_rest(plane_sum, mix_came, 16)
        send_grads(ffn_came[-1])
        buffers = None
        for start, part in zip(grad_starts, arrived[:sent_early]):
            buffers = assemble(tie(part, ffn_came[-1]), start, local, buffers)
        ffn_message = tie(ffn_message, *buffers)

        upstream = cotangent.astype(F32)
        prob_grads = ffn_message[:, D : D + E] + ffn_message[:, D + E : D + 2 * E]
        logit_grads = (
            router_probs
            * (prob_grads - jnp.sum(router_probs * prob_grads, axis=-1, keepdims=True))
        ).astype(BF)
        ffn_grads = ffn_message[:, :D] + matmul(logit_grads, router_full, ((1,), (1,)))

        def norm_back(v, r, gain, dy):
            u = dy * gain
            return r * u - v * (r * r * r) * jnp.mean(u * v, axis=-1, keepdims=True)

        residual_grads = upstream + norm_back(residual, ffn_r, ffn_gain, ffn_grads)
        ffn_gain_part = jnp.sum(ffn_grads * residual * ffn_r, axis=0)
        message = jnp.concatenate(
            [residual_grads.astype(BF), logit_grads, jnp.zeros_like(logit_grads)], axis=1
        )

        plane_message = join(*gather_wide(message))
        plane_grads = plane_message[:, :D]
        attended_grads = matmul(plane_grads, output_rows, ((1,), (1,))).astype(BF)
        plane_rows = lax.dynamic_slice_in_dim(
            join([x[:count] for x in tokens_own], [x[:count] for x in tokens_other]),
            w * features,
            features,
            axis=1,
        )
        scaled, value_grads, dots, head_gain_parts = attend_back(
            turned, attended_grads, raw, scales, cosine, sine, head_gains, count
        )

        grad_output = matmul(attended, plane_grads, ((0,), (0,))).astype(BF)
        grad_value = matmul(normed, value_grads, ((0,), (0,))).astype(BF)
        early_parts = by_narrow(
            grad_output.reshape(1, narrow, rows, D),
            grad_value.reshape(wide, narrow, rows, features),
        )

        dots, dots_gathered = row_sums(dots.T)
        dots = dots.T / D
        shrink = scales * scales * scales * dots
        raw_grads = (
            scaled.reshape(plane_count, 2, features) * scales[:, :, None]
            - raw[:, : 2 * features].reshape(plane_count, 2, features) * shrink[:, :, None]
        ).astype(BF)
        raw_grads = jnp.concatenate([raw_grads.reshape(plane_count, 2 * features), value_grads], axis=1)
        mix_came += [
            swap(tie(mix_sent[q - 1], dots_gathered), "wide", 2 * q) for q in range(3, planes)
        ]
        grad_early, early_came = scatter_narrow(*early_parts)
        raw_grads = tie(raw_grads, arrived[-1], early_came[0])
        normed_grads = matmul(raw_grads, qkv, ((1,), (1,))).astype(BF)

        attn_gain_part = jnp.sum(normed_grads.astype(F32) * plane_tokens * inverse, axis=0)
        gain_parts = jnp.concatenate(
            [
                jnp.stack([attn_gain_part, ffn_gain_part]).reshape(2 * wide, features),
                head_gain_parts,
            ]
        ).T
        gain_columns = 2 * wide + 2
        router_part = matmul(plane_rows, plane_message[:, D : D + E], ((0,), (0,)))
        small_parts = jnp.concatenate([router_part.astype(BF), *split_low(gain_parts)], axis=1)
        small_parts = jnp.pad(
            small_parts, ((0, 0), (0, 2 * features - E - 2 * gain_columns))
        )
        plane_normed = normed_grads.reshape(planes, 2, count, D)
        normed_other = swap(plane_normed[:, 1], "wide", 1)
        normed_sums = [add_up([plane_normed[q, 0], normed_other[q]]) for q in range(planes)]
        normed_came = [
            swap(normed_sums[q].astype(BF), "wide", 2 * q)
            for q in range(1, planes)
        ]
        grad_raw = matmul(normed, raw_grads[:, : 2 * features], ((0,), (0,))).astype(BF)
        grad_raw, raw_came = scatter_narrow(
            *by_narrow(
                grad_raw.reshape(wide, narrow, rows, 2 * features),
                small_parts.reshape(1, narrow, rows, 2 * features),
            ),
            (),
            normed_came,
        )
        small_parts = grad_raw[wide]
        grad_router = small_parts[:, :E]
        gain_parts = small_parts[:, E : E + 2 * gain_columns]
        gain_parts = (gain_parts[:, :gain_columns] + gain_parts[:, gain_columns:]).T
        grad_gain_query, grad_gain_key = gain_parts[2 * wide], gain_parts[2 * wide + 1]
        blocks = D // (2 * features)
        grad_output = jnp.concatenate([grad_early[i] for i in range(blocks)], axis=1)
        grad_value = (
            grad_early[blocks:]
            .reshape(wide // 2, rows, 2, features)
            .transpose(0, 2, 1, 3)
            .reshape(wide, rows, features)
        )
        grad_qkv = jnp.concatenate([grad_raw[:wide], grad_value], axis=-1)
        mix_came[-1] = tie(mix_came[-1], raw_came[0])
        mixture = add_up([mix_sums[0], *mix_came]).astype(BF)
        block_out = (residual + scatter_rest(mixture)[0]).astype(BF)
        gain_rows = jnp.concatenate(
            [*split_low(gain_parts[:wide]), *split_low(gain_parts[wide : 2 * wide])], axis=1
        )
        gain_rows = jnp.pad(
            gain_rows[:, None, :], ((0, 0), (0, 15), (0, 3 * features - 4 * rows))
        )
        grad_qkv = jnp.concatenate([grad_qkv.astype(BF), gain_rows], axis=1)
        grad_qkv = lax.all_to_all(grad_qkv, "wide", 0, 0, tiled=True)
        gain_rows = jnp.sum(grad_qkv[:, rows, : 4 * rows].astype(F32), axis=0).reshape(4, rows)
        gain_sums = [gain_rows[0] + gain_rows[1], gain_rows[2] + gain_rows[3]]
        grad_qkv = grad_qkv[:, :rows].transpose(1, 0, 2).astype(F32)
        grad_query, grad_key, grad_value = [
            grad_qkv[..., i * features : (i + 1) * features].reshape(rows, D) for i in range(3)
        ]

        normed_grads = add_up([normed_sums[0], *normed_came])
        input_grad = (
            residual_grads
            + norm_back(tokens.astype(F32), inverse[:count], attn_gain, normed_grads)
        ).astype(BF)

        for start, part in zip(grad_starts[sent_early:], arrived[sent_early:]):
            buffers = assemble(tie(part, raw_came[1]), start, local, buffers)
        grad_gate, grad_up = buffers

        return (
            block_out, input_grad, grad_query, grad_key, grad_value,
            grad_output, grad_router,
            gain_sums[0], grad_gain_query, grad_gain_key, gain_sums[1],
            grad_gate, grad_up, down_grad, expert_counts,
        )

    return on_device


def solution(mesh):
    both = ("wide", "narrow")
    in_specs = (P(both, None), P(both), P(both, None), P(both, None))
    in_specs += (P(both, None),) * 5 + (P(both),) * 4 + (P("wide", "narrow", None),) * 3
    out_specs = (P(both, None),) * 7 + (P(both),) * 4 + (P("wide", "narrow", None),) * 3 + (P(),)
    return jax.shard_map(
        make_on_device(mesh.shape["wide"], mesh.shape["narrow"]),
        mesh=mesh,
        in_specs=in_specs,
        out_specs=out_specs,
        check_vma=False,
    )
```

```python
import functools

import jax
import jax.numpy as jnp
from jax import lax
from jax.experimental import pallas as pl
from jax.experimental.pallas import tpu as pltpu
from jax.sharding import PartitionSpec as P

D = 2048
H = 16
HD = 128
E = 64
TOPK = 8
CAP = 24
FF = 1024
LANES = 128
EXPERT_TILE = 768
EPSILON = 1e-05
THETA_BASE = 10000.0

BF = jnp.bfloat16
F32 = jnp.float32
VMEM_BYTES = 56 * 1024 * 1024


def matmul(a, b, dims):
    return lax.dot_general(a, b, (dims, ((), ())), preferred_element_type=F32)


def dispatch_body(pieces, each, *refs):
    picks = refs[0]
    sources = refs[1 : 1 + pieces]
    out = refs[-1]
    for q in range(pieces):
        rows = matmul(picks[q, 0], sources[q][...], ((1,), (0,))).astype(BF)
        out[:, q * each : (q + 1) * each, :] = rows.reshape(-1, each, rows.shape[-1])


def dispatch(picks, sources, half, buffer=None):
    pieces, pairs, slots, span = picks.shape
    width = sources[0].shape[1]
    each = 2 * CAP
    block = pieces * each
    in_specs = [pl.BlockSpec((pieces, 1, slots, span), lambda j: (0, j, 0, 0))]
    in_specs += [pl.BlockSpec((span, width), lambda j: (j, 0))] * pieces
    args = [picks, *sources]
    aliases = {}
    if buffer is not None:
        in_specs.append(pl.BlockSpec(memory_space=pl.ANY))
        aliases = {len(args): 0}
        args.append(buffer)
    return pl.pallas_call(
        functools.partial(dispatch_body, pieces, each),
        grid=(pairs,),
        in_specs=in_specs,
        out_specs=pl.BlockSpec(
            (slots // each, block, width), lambda j: (0, half * pairs + j, 0)
        ),
        out_shape=jax.ShapeDtypeStruct((slots // each, 2 * pairs * block, width), BF),
        input_output_aliases=aliases,
        compiler_params=pltpu.CompilerParams(vmem_limit_bytes=VMEM_BYTES),
        cost_estimate=pl.CostEstimate(
            flops=2 * pieces * pairs * slots * span * width,
            bytes_accessed=2 * pieces * pairs * (slots + span) * width,
            transcendentals=0,
        ),
        name="dispatch",
    )(*args)


def combine_body(pieces, each, picks, rows, *outs):
    for q in range(pieces):
        part = rows[:, q * each : (q + 1) * each, :].reshape(-1, rows.shape[-1])
        outs[q][...] = matmul(picks[q, 0], part, ((0,), (0,))).astype(BF)


def combine(picks, rows, half):
    pieces, pairs, slots, span = picks.shape
    each = 2 * CAP
    local, _, width = rows.shape
    return pl.pallas_call(
        functools.partial(combine_body, pieces, each),
        grid=(pairs,),
        in_specs=[
            pl.BlockSpec((pieces, 1, slots, span), lambda j: (0, j, 0, 0)),
            pl.BlockSpec((local, pieces * each, width), lambda j: (0, half * pairs + j, 0)),
        ],
        out_specs=[pl.BlockSpec((span, width), lambda j: (j, 0))] * pieces,
        out_shape=[jax.ShapeDtypeStruct((pairs * span, width), BF)] * pieces,
        compiler_params=pltpu.CompilerParams(vmem_limit_bytes=VMEM_BYTES),
        cost_estimate=pl.CostEstimate(
            flops=2 * pieces * pairs * slots * span * width,
            bytes_accessed=2 * pieces * pairs * (slots + span) * width,
            transcendentals=0,
        ),
        name="combine",
    )(picks, rows)


def expert_body(parts, tiles, start, aliased, *refs):
    where, rows_ref, ups_ref, weights_ref, down_ref = refs[:5]
    rest = refs[5 + aliased :]
    results_ref, row_grads_ref, weight_grads_ref, down_grad_ref, result_grads, *sums = rest
    tile = pl.program_id(1)
    width = FF // parts
    depth = D // parts
    slices = [slice(s * depth, (s + 1) * depth) for s in range(parts)]

    both = None
    for s in range(parts):
        term = matmul(rows_ref[0, :, slices[s]], weights_ref[s, 0], ((1,), (0,)))
        both = term if both is None else both + term
    gate_value = both[:, :width]
    up_value = both[:, width:]
    sigma = 1.0 / (1.0 + jnp.exp(-gate_value))
    silu = gate_value * sigma
    hidden = (silu * up_value).astype(BF)

    expert = where[1] + start + pl.program_id(0)
    lane = lax.broadcasted_iota(jnp.int32, (rows_ref.shape[1], LANES), 1)
    high = lane == expert
    low = lane == expert + E
    probs = rows_ref[0, :, D:].astype(F32)
    weight = jnp.sum(jnp.where(high | low, probs, 0.0), axis=1, keepdims=True)

    gate_grad = None
    hidden_grads = None
    for columns in slices:
        down = down_ref[0, :, columns]
        results = matmul(hidden, down, ((1,), (0,)))
        upstream = ups_ref[0, :, columns].astype(F32)
        dot = jnp.sum(upstream * results, axis=1, keepdims=True)
        gate_grad = dot if gate_grad is None else gate_grad + dot
        results_ref[0, :, columns] = (weight * results).astype(BF)
        part = (weight * upstream).astype(BF)
        result_grads[:, columns] = part
        term = matmul(part, down, ((1,), (1,)))
        hidden_grads = term if hidden_grads is None else hidden_grads + term

    gate_value_grads = (
        hidden_grads * up_value * (sigma * (1.0 + gate_value * (1.0 - sigma)))
    ).astype(BF)
    up_value_grads = (hidden_grads * silu).astype(BF)
    both_grads = jnp.concatenate([gate_value_grads, up_value_grads], axis=1)
    top = gate_grad.astype(BF)
    bottom = (gate_grad - top.astype(F32)).astype(BF)
    row_grads_ref[0, :, D:] = jnp.where(
        high, top.astype(F32), jnp.where(low, bottom.astype(F32), 0.0)
    ).astype(BF)
    for s in range(parts):
        row_grads_ref[0, :, slices[s]] = matmul(
            both_grads, weights_ref[s, 0], ((1,), (1,))
        ).astype(BF)

    def weight_term(s):
        return matmul(rows_ref[0, :, slices[s]], both_grads, ((0,), (0,)))

    def down_term(columns):
        return matmul(hidden, result_grads[:, columns], ((0,), (0,)))

    if tiles == 1:
        for s in range(parts):
            weight_grads_ref[s, 0] = weight_term(s).astype(BF)
            down_grad_ref[0, :, slices[s]] = down_term(slices[s])
        return
    weight_sums = sums[0]
    first = tile == 0

    @pl.when(first)
    def _():
        for s in range(parts):
            weight_sums[s] = weight_term(s)
            down_grad_ref[0, :, slices[s]] = down_term(slices[s])

    @pl.when(jnp.logical_not(first))
    def _():
        for s in range(parts):
            weight_sums[s] += weight_term(s)
            down_grad_ref[0, :, slices[s]] += down_term(slices[s])

    @pl.when(tile == tiles - 1)
    def _():
        for s in range(parts):
            weight_grads_ref[s, 0] = weight_sums[s].astype(BF)


def expert_chunk(where, rows, ups, weights, down, start, experts, offset, group, at, buffers):
    parts, _, depth, width2 = weights.shape
    local, total_rows, wide_row = rows.shape
    tile = EXPERT_TILE
    tiles = total_rows // tile
    slice_ff = down.shape[1]
    weight_spec = pl.BlockSpec((parts, 1, depth, width2), lambda e, i, c: (0, offset + e, 0, 0))
    down_spec = pl.BlockSpec((1, slice_ff, D), lambda e, i, c: (start + e, 0, 0))
    in_specs = [
        pl.BlockSpec((1, tile, wide_row), lambda e, i, c: (start + e, i, 0)),
        pl.BlockSpec((1, tile, D), lambda e, i, c: (start + e, i, 0)),
        weight_spec,
        down_spec,
    ]
    args = [where, rows, ups, weights, down]
    aliases = {}
    for index, buffer in enumerate(buffers):
        if buffer is not None:
            in_specs.append(pl.BlockSpec(memory_space=pl.ANY))
            aliases[len(args)] = index
            args.append(buffer)
    return pl.pallas_call(
        functools.partial(expert_body, parts, tiles, start, len(aliases)),
        grid_spec=pltpu.PrefetchScalarGridSpec(
            num_scalar_prefetch=1,
            grid=(experts, tiles),
            in_specs=in_specs,
            out_specs=[
                pl.BlockSpec((1, tile, D), lambda e, i, c: (start + e, i, 0)),
                pl.BlockSpec((1, tile, wide_row), lambda e, i, c: (start + e, i, 0)),
                pl.BlockSpec((parts, 1, depth, width2), lambda e, i, c: (0, at + e, 0, 0)),
                down_spec,
            ],
            scratch_shapes=[pltpu.VMEM((tile, D), BF)]
            + ([pltpu.VMEM((parts, depth, width2), F32)] if tiles > 1 else []),
        ),
        out_shape=[
            jax.ShapeDtypeStruct((local, total_rows, D), BF),
            jax.ShapeDtypeStruct((local, total_rows, wide_row), BF),
            jax.ShapeDtypeStruct((parts, group, depth, width2), BF),
            jax.ShapeDtypeStruct((local, slice_ff, D), F32),
        ],
        input_output_aliases=aliases,
        compiler_params=pltpu.CompilerParams(vmem_limit_bytes=VMEM_BYTES),
        cost_estimate=pl.CostEstimate(
            flops=18 * experts * total_rows * D * slice_ff,
            bytes_accessed=8 * experts * total_rows * D + 18 * experts * D * slice_ff,
            transcendentals=experts * total_rows * slice_ff,
        ),
        name="experts",
    )(*args)


def slice_body(parts, width, gate_ref, up_ref, out):
    for s in range(parts):
        columns = slice(s * width, (s + 1) * width)
        out[s, 0, :, :width] = gate_ref[0, :, columns]
        out[s, 0, :, width:] = up_ref[0, :, columns]


def slice_weights(gate, up, start, experts, parts):
    depth = gate.shape[1]
    width = FF // parts
    spec = pl.BlockSpec((1, depth, FF), lambda e: (start + e, 0, 0))
    return pl.pallas_call(
        functools.partial(slice_body, parts, width),
        grid=(experts,),
        in_specs=[spec, spec],
        out_specs=pl.BlockSpec((parts, 1, depth, 2 * width), lambda e: (0, e, 0, 0)),
        out_shape=jax.ShapeDtypeStruct((parts, experts, depth, 2 * width), BF),
        compiler_params=pltpu.CompilerParams(vmem_limit_bytes=VMEM_BYTES),
        cost_estimate=pl.CostEstimate(
            flops=0, bytes_accessed=8 * experts * depth * FF, transcendentals=0
        ),
        name="slice_weights",
    )(gate, up)


def assemble_body(parts, width, *refs):
    source = refs[0]
    gate_ref, up_ref = refs[-2], refs[-1]
    for s in range(parts):
        columns = slice(s * width, (s + 1) * width)
        gate_ref[0, :, columns] = source[s, 0, :, :width].astype(F32)
        up_ref[0, :, columns] = source[s, 0, :, width:].astype(F32)


def assemble(source, start, local, buffers):
    parts, experts, depth, width2 = source.shape
    in_specs = [pl.BlockSpec((parts, 1, depth, width2), lambda e: (0, e, 0, 0))]
    args = [source]
    aliases = {}
    if buffers is not None:
        in_specs += [pl.BlockSpec(memory_space=pl.ANY)] * 2
        aliases = {1: 0, 2: 1}
        args += list(buffers)
    spec = pl.BlockSpec((1, depth, FF), lambda e: (start + e, 0, 0))
    return pl.pallas_call(
        functools.partial(assemble_body, parts, width2 // 2),
        grid=(experts,),
        in_specs=in_specs,
        out_specs=[spec, spec],
        out_shape=[jax.ShapeDtypeStruct((local, depth, FF), F32)] * 2,
        input_output_aliases=aliases,
        compiler_params=pltpu.CompilerParams(vmem_limit_bytes=VMEM_BYTES),
        cost_estimate=pl.CostEstimate(
            flops=0, bytes_accessed=6 * experts * depth * FF * 2, transcendentals=0
        ),
        name="assemble",
    )(*args)


def turn(x, cosine, sine):
    return x * cosine + pltpu.roll(x, HD // 2, 1) * sine


def probabilities(query, key):
    scores = matmul(query, key, ((1,), (1,))) * HD ** (-0.5)
    row = lax.broadcasted_iota(jnp.int32, scores.shape, 0)
    column = lax.broadcasted_iota(jnp.int32, scores.shape, 1)
    causal = row >= column
    scores = jnp.where(causal, scores, -1e30)
    powers = jnp.exp(scores - jnp.max(scores, axis=-1, keepdims=True))
    return powers / jnp.sum(powers, axis=-1, keepdims=True), causal


def attend_body(raw, scales, cosine, sine, gains, turned, attended):
    features = attended.shape[1]
    for part in range(2):
        scale = scales[:, part : part + 1]
        for at in range(0, features, HD):
            columns = slice(part * features + at, part * features + at + HD)
            x = raw[:, columns] * scale * gains[part : part + 1, at : at + HD]
            turned[:, columns] = turn(x, cosine[...], sine[...]).astype(BF)
    turned[:, 2 * features :] = raw[:, 2 * features :].astype(BF)
    for at in range(0, features, HD):
        query = turned[:, at : at + HD]
        key = turned[:, features + at : features + at + HD]
        value = turned[:, 2 * features + at : 2 * features + at + HD]
        probs, _ = probabilities(query, key)
        attended[:, at : at + HD] = matmul(probs.astype(BF), value, ((1,), (0,))).astype(BF)


def attend(raw, scales, cosine, sine, gains, count):
    total, features = raw.shape[0], raw.shape[1] // 3

    def block(x):
        return pl.BlockSpec((count, x.shape[1]), lambda i: (i, 0))

    return pl.pallas_call(
        attend_body,
        grid=(total // count,),
        in_specs=[block(x) for x in (raw, scales, cosine, sine)]
        + [pl.BlockSpec(gains.shape, lambda i: (0, 0))],
        out_specs=[
            pl.BlockSpec((count, 3 * features), lambda i: (i, 0)),
            pl.BlockSpec((count, features), lambda i: (i, 0)),
        ],
        out_shape=[
            jax.ShapeDtypeStruct((total, 3 * features), BF),
            jax.ShapeDtypeStruct((total, features), BF),
        ],
        compiler_params=pltpu.CompilerParams(vmem_limit_bytes=VMEM_BYTES),
        cost_estimate=pl.CostEstimate(
            flops=4 * total * count * features,
            bytes_accessed=20 * total * features,
            transcendentals=total * count,
        ),
        name="attend",
    )(raw, scales, cosine, sine, gains)


def attend_back_body(turned, grads, raw, scales, cosine, sine, gains, scaled, value_grads, sums, gain_grads):
    features = grads.shape[1]
    scale = HD ** (-0.5)
    dots = [0.0, 0.0]
    first = pl.program_id(0) == 0
    for at in range(0, features, HD):
        query = turned[:, at : at + HD]
        key = turned[:, features + at : features + at + HD]
        value = turned[:, 2 * features + at : 2 * features + at + HD]
        grad = grads[:, at : at + HD]
        probs, causal = probabilities(query, key)
        value_grads[:, at : at + HD] = matmul(probs.astype(BF), grad, ((0,), (0,))).astype(BF)
        prob_grads = matmul(grad, value, ((1,), (1,)))
        score_grads = probs * (prob_grads - jnp.sum(probs * prob_grads, axis=-1, keepdims=True))
        score_grads = jnp.where(causal, score_grads, 0.0).astype(BF)
        turned_grads = (
            matmul(score_grads, key, ((1,), (0,))) * scale,
            matmul(score_grads, query, ((0,), (0,))) * scale,
        )
        for part in range(2):
            columns = slice(part * features + at, part * features + at + HD)
            x = raw[:, columns]
            dy = turn(turned_grads[part], cosine[...], -sine[...])
            u = dy * gains[part : part + 1, at : at + HD]
            scaled[:, columns] = u
            dots[part] = dots[part] + jnp.sum(u * x, axis=-1, keepdims=True)
            gain_grad = jnp.sum(dy * x * scales[:, part : part + 1], axis=0, keepdims=True)
            old = gain_grads[part : part + 1, at : at + HD]
            gain_grads[part : part + 1, at : at + HD] = gain_grad + jnp.where(first, 0.0, old)
    sums[...] = jnp.concatenate(dots, axis=1)


def attend_back(turned, grads, raw, scales, cosine, sine, gains, count):
    total, features = grads.shape

    def block(x):
        return pl.BlockSpec((count, x.shape[1]), lambda i: (i, 0))

    out_shape = [
        jax.ShapeDtypeStruct((total, 2 * features), F32),
        jax.ShapeDtypeStruct((total, features), BF),
        jax.ShapeDtypeStruct((total, 2), F32),
    ]
    return pl.pallas_call(
        attend_back_body,
        grid=(total // count,),
        in_specs=[block(x) for x in (turned, grads, raw, scales, cosine, sine)]
        + [pl.BlockSpec(gains.shape, lambda i: (0, 0))],
        out_specs=[block(x) for x in out_shape] + [pl.BlockSpec(gains.shape, lambda i: (0, 0))],
        out_shape=[*out_shape, jax.ShapeDtypeStruct(gains.shape, F32)],
        compiler_params=pltpu.CompilerParams(vmem_limit_bytes=VMEM_BYTES),
        cost_estimate=pl.CostEstimate(
            flops=12 * total * count * features,
            bytes_accessed=30 * total * features,
            transcendentals=total * count,
        ),
        name="attend_back",
    )(turned, grads, raw, scales, cosine, sine, gains)


def pick_body(where, *refs):
    half = pl.num_programs(0) // 2

    def fill(out):
        width = out.shape[-1]
        at = 0
        for source in refs[:-2]:
            outer, _, _, own = source.shape
            if own >= width:
                for i in range(outer):
                    for column in range(0, own, width):
                        out[0, at] = source[i, 0, :, column : column + width]
                        at += 1
            else:
                for i in range(0, outer, width // own):
                    for k in range(width // own):
                        out[0, at, :, k * own : (k + 1) * own] = source[i + k, 0]
                    at += 1

    @pl.when(pl.program_id(0) < half)
    def _():
        fill(refs[-2])

    @pl.when(pl.program_id(0) >= half)
    def _():
        fill(refs[-1])


def pick_blocks(order, width, *sources):
    rows = sources[0].shape[2]
    half = order.shape[0] // 2
    outer = sum(x.shape[0] * x.shape[3] for x in sources) // width
    shape = (1, outer, rows, width)
    return pl.pallas_call(
        pick_body,
        grid_spec=pltpu.PrefetchScalarGridSpec(
            num_scalar_prefetch=1,
            grid=(2 * half,),
            in_specs=[
                pl.BlockSpec((x.shape[0], 1, *x.shape[2:]), lambda k, c: (0, c[k], 0, 0))
                for x in sources
            ],
            out_specs=[
                pl.BlockSpec(shape, lambda k, c: (jnp.minimum(k, half - 1), 0, 0, 0)),
                pl.BlockSpec(shape, lambda k, c: (jnp.maximum(k - half, 0), 0, 0, 0)),
            ],
        ),
        out_shape=[jax.ShapeDtypeStruct((half, *shape[1:]), BF)] * 2,
        compiler_params=pltpu.CompilerParams(vmem_limit_bytes=VMEM_BYTES),
        cost_estimate=pl.CostEstimate(
            flops=0, bytes_accessed=8 * half * outer * rows * width, transcendentals=0
        ),
        name="pick_blocks",
    )(order, *sources)


def tie(value, *after):
    return lax.optimization_barrier((value, *after))[0]


def split_low(x):
    top = x.astype(BF)
    return top, (x - top.astype(F32)).astype(BF)


def add_up(parts):
    total = parts[0].astype(F32)
    for part in parts[1:]:
        total = total + part.astype(F32)
    return total


def make_on_device(wide, narrow):
    planes = wide // 2
    local = E // wide
    heads = H // wide
    features = heads * HD
    if local == 8:
        sizes, early, groups = [2, 1, 1, 1, 1, 2], 2, [[0], [1, 2, 3], [4, 5]]
        parts = [[0], [1, 2], [3, 4], [5]]
    else:
        sizes = [1] * local
        early, groups = min(2, local), [[c] for c in range(local)]
        parts = groups
    calls = len(sizes)
    starts = [sum(sizes[:c]) for c in range(calls)]
    slice_ff = FF // narrow
    both_axes = ("wide", "narrow")

    def swap(x, axis, r):
        size = wide if axis == "wide" else narrow
        return lax.ppermute(x, axis, [(i, i ^ r) for i in range(size)])

    bits = [1 << i for i in reversed(range(narrow.bit_length() - 1))]
    near = [0]
    for bit in bits:
        near = near + [r ^ bit for r in near]

    def swap_marked(x, bit, small):
        rest = swap(x[:-small], "narrow", bit)
        marker = swap(x[-small:], "narrow", bit)
        return jnp.concatenate([rest, marker], axis=0), marker

    def gather_narrow(x, *after):
        for i, bit in enumerate(bits):
            if i and after:
                x = tie(x, *after)
            x = jnp.concatenate([x, swap(x, "narrow", bit)], axis=0)
        return x

    def scatter_narrow(keep, send, step=(), last=(), small=0):
        arrivals = []
        for bit in reversed(bits):
            marker = None
            if small and bit == bits[0]:
                came, marker = swap_marked(send[0], bit, small)
                came = came[None]
            else:
                came = swap(send, "narrow", bit)
            if last and bit == bits[0]:
                came = tie(came, *last)
            arrivals.append(came)
            if marker is not None:
                arrivals.append(marker)
            total = keep.astype(F32) + came.astype(F32)
            half = total.shape[0] // 2
            keep, send = total[:half], total[half:].astype(BF)
            if step:
                send = tie(send, *step)
        return total[0], arrivals

    def gather_planes(x):
        return [x] + [swap(x, "wide", 2 * q) for q in range(1, planes)]

    def cross(pieces):
        return [swap(piece, "wide", 1) for piece in pieces]

    def gather_wide(x):
        own = gather_planes(x)
        return own, cross(own)

    def join(own, other):
        return jnp.concatenate([piece for pair in zip(own, other) for piece in pair], axis=0)

    def scatter_wide(own, other):
        return scatter_plane(own, swap(other, "wide", 1))[0]

    def scatter_plane(own, came, *after):
        sums = [own[q].astype(F32) + came[q].astype(F32) for q in range(planes)]
        sent = [x.astype(BF) for x in sums[1:]]
        if after:
            sent = list(lax.optimization_barrier((*sent, *after))[: planes - 1])
        total = sums[0]
        for q in range(1, planes):
            total = total + swap(sent[q - 1], "wide", 2 * q).astype(F32)
        return total, sent

    def on_device(
        tokens, positions, routes, cotangent,
        w_query, w_key, w_value, w_output, w_router,
        gain_attn, gain_query, gain_key, gain_ffn,
        w_gate, w_up, w_down,
    ):
        count = tokens.shape[0]
        rows = w_query.shape[0]
        w = lax.axis_index("wide")
        n = lax.axis_index("narrow")
        where = jnp.stack([n, w * local, w]).astype(jnp.int32)
        wide_order = jnp.arange(wide) ^ w
        near_order = jnp.array(near) ^ n
        narrow_order = jnp.array([near.index(r) for r in range(narrow)])[jnp.arange(narrow) ^ n]

        def by_narrow(*x):
            return pick_blocks(near_order, 2 * features, *x)

        routed = jnp.any(
            routes[:, :, None] == jnp.arange(E, dtype=jnp.int32)[None, None, :], axis=1
        )
        earlier = matmul(
            jnp.tril(jnp.ones((count, count), BF), -1), routed.astype(BF), ((1,), (0,))
        )
        slots = jnp.where(routed, earlier, -1.0).astype(BF).T

        small = jnp.concatenate(
            [
                w_router.reshape(-1), gain_attn, gain_query, gain_key, gain_ffn,
                positions.astype(BF),
            ]
        )
        small_rows = -(-small.shape[0] // LANES)
        bundle_rows = -(-(E + small_rows) // 16) * 16
        small = jnp.pad(small, (0, (bundle_rows - E) * LANES - small.shape[0]))
        bundle = jnp.concatenate([slots, small.reshape(-1, LANES)], axis=0)
        bundle_z = lax.all_gather(bundle, "narrow")
        stacked = jnp.concatenate(
            [x.reshape(rows, wide, features) for x in (w_query, w_key, w_value)], axis=-1
        ).transpose(1, 0, 2)
        columns = lax.all_to_all(stacked, "wide", 0, 0, tiled=True)
        bundles = lax.all_gather(bundle_z, "wide")
        all_slots = bundles[:, :, :E, :]
        all_small = bundles[:, :, E:, :].reshape(wide, narrow, -1)
        base = rows * E
        plane_positions = lax.dynamic_index_in_dim(
            all_small[:, :, base + 4 * rows : base + 4 * rows + count], n, 1, keepdims=False
        )
        plane_positions = jnp.take(plane_positions, wide_order, axis=0).reshape(wide * count)
        router_full = all_small[:, :, :base].reshape(D, E)
        gains = [
            all_small[:, :, base + i * rows : base + (i + 1) * rows].reshape(D).astype(F32)
            for i in range(4)
        ]
        attn_gain, query_gain, key_gain, ffn_gain = gains
        query_gain = lax.dynamic_slice_in_dim(query_gain, w * features, features)
        key_gain = lax.dynamic_slice_in_dim(key_gain, w * features, features)
        expert_counts = jnp.sum((all_slots >= 0).astype(jnp.int32), axis=(0, 1, 3))

        tokens_near = gather_wide(tokens)
        plane_tokens = join(*tokens_near).astype(F32)
        plane_count = plane_tokens.shape[0]

        sliced = [
            slice_weights(w_gate, w_up, starts[p[0]], sum(sizes[c] for c in p), narrow)
            for p in parts
        ]
        expert_weights = []

        def send_weights(*after):
            part = tie(sliced[len(expert_weights)], *after)
            expert_weights.append(lax.all_to_all(part, "narrow", 0, 0, tiled=True))

        ups_z = gather_narrow(cotangent, bundle_z)
        output_rows = gather_narrow(w_output[None])
        send_weights(columns, bundles, ups_z)
        output_rows = jnp.take(output_rows, narrow_order, axis=0).reshape(features, D)
        ups_own = gather_planes(tie(ups_z, *tokens_near[0], *tokens_near[1]))
        columns = lax.optimization_barrier(
            (columns, expert_weights[0], *tokens_near[0], *tokens_near[1], *ups_own[:3])
        )[0]
        columns = gather_narrow(columns[None])
        gathered = columns
        columns = jnp.take(columns, narrow_order, axis=0)
        qkv = columns.transpose(1, 0, 2, 3).reshape(D, 3 * features)
        while len(expert_weights) < early:
            send_weights(gathered, *expert_weights[1:])

        local_slots = lax.dynamic_slice_in_dim(all_slots, w * local, local, axis=2)
        local_slots = jnp.take(jnp.take(local_slots, wide_order, axis=0), near_order, axis=1)
        pairs = narrow // 2
        local_slots = (
            local_slots.reshape(planes, 2, pairs, 2, local, count)
            .transpose(1, 0, 2, 4, 3, 5)
            .reshape(2, planes, pairs, local, 1, 2 * count)
        )
        row = jnp.arange(2 * CAP)[:, None]
        lane = jnp.arange(2 * count)[None, :]
        picks = (
            ((local_slots == (row % CAP).astype(BF)) & (row // CAP == lane // count))
            .astype(BF)
            .reshape(2, planes, pairs, local * 2 * CAP, 2 * count)
        )
        picks_own, picks_other = picks[0], picks[1]
        inverse = lax.rsqrt(jnp.mean(plane_tokens * plane_tokens, axis=-1, keepdims=True) + EPSILON)
        normed = (plane_tokens * inverse * attn_gain).astype(BF)
        raw = matmul(normed, tie(qkv, *ups_own), ((1,), (0,)))

        def row_sums(sums):
            sums = jnp.take(sums.reshape(2, wide, count), wide_order, axis=1)
            gathered = lax.all_gather(sums, "wide")
            sums = jnp.sum(gathered, axis=0)
            return jnp.take(sums, wide_order, axis=1).reshape(2, plane_count), gathered

        squares = jnp.stack(
            [
                jnp.sum(x * x, axis=-1)
                for x in (raw[:, :features], raw[:, features : 2 * features])
            ]
        )
        scales = lax.rsqrt(row_sums(squares)[0] / D + EPSILON).T
        frequency = THETA_BASE ** (-2.0 * jnp.arange(HD // 2, dtype=F32) / HD)
        angles = plane_positions.astype(F32)[:, None] * frequency[None, :]
        cosine, sine = jnp.cos(angles), jnp.sin(angles)
        cosine = jnp.concatenate([cosine, cosine], axis=1)
        sine = jnp.concatenate([-sine, sine], axis=1)
        head_gains = jnp.stack([query_gain, key_gain])
        turned, attended = attend(raw, scales, cosine, sine, head_gains, count)
        if early > 2:
            attended = tie(attended, expert_weights[1], sliced[2])
        branch = matmul(attended, output_rows, ((1,), (0,))).astype(BF)
        branch = branch.reshape(planes, 2, count, D)
        branch = scatter_wide(branch[:, 0], branch[:, 1])

        residual = tokens.astype(F32) + branch
        ffn_r = lax.rsqrt(jnp.mean(residual * residual, axis=-1, keepdims=True) + EPSILON)
        normed_ffn = (residual * ffn_r * ffn_gain).astype(BF)
        logits = matmul(normed_ffn, router_full, ((1,), (0,)))
        router_powers = jnp.exp(logits - jnp.max(logits, axis=-1, keepdims=True))
        router_probs = router_powers / jnp.sum(router_powers, axis=-1, keepdims=True)

        message = jnp.concatenate([normed_ffn, *split_low(router_probs)], axis=1)
        ups = dispatch(picks_own, ups_own, 0)
        ups = dispatch(picks_other, cross(ups_own), 1, ups)
        message = gather_narrow(tie(message, ups, expert_weights[-1]))
        if len(parts) > early:
            send_weights(message)
        tokens_own = gather_planes(message)
        while len(expert_weights) < len(parts):
            send_weights(*tokens_own)
        tokens_own[0] = tie(tokens_own[0], expert_weights[min(early, len(parts) - 1)])
        tokens_other = cross(tokens_own)
        expert_rows = dispatch(picks_own, tokens_own, 0)
        expert_rows = dispatch(picks_other, tokens_other, 1, expert_rows)

        came = []
        held = [None] * 4
        for c in range(calls):
            if c == 1:
                expert_rows = tie(expert_rows, expert_weights[-1])
            group = next(g for g in groups if c in g)
            part = next(i for i, p in enumerate(parts) if c in p)
            if c == group[0]:
                held[2] = None
            held = [*expert_chunk(
                where, expert_rows, ups, expert_weights[part], w_down, starts[c], sizes[c],
                starts[c] - starts[parts[part][0]], sum(sizes[g] for g in group), starts[c] - starts[group[0]], held,
            )]
            if c == group[-1]:
                came.append(held[2])
        results, row_grads, _, down_grad = held
        arrived = []

        def send_grads(*after):
            part = came[len(arrived)]
            part = tie(part, *after) if after else part
            arrived.append(lax.all_to_all(part, "narrow", 0, 0, tiled=True))

        grad_starts = [starts[group[0]] for group in groups]
        sent_early = len(groups) - 1
        for g in range(sent_early):
            send_grads(*([row_grads] if g else []))

        def combine_tokens(terms, *after):
            terms = tie(terms, *after) if after else terms
            other = cross(combine(picks_other, terms, 1))
            return list(combine(picks_own, terms, 0)), other

        def scatter_rest(plane_sum, last=(), small=0):
            blocks = plane_sum.reshape(narrow, count, plane_sum.shape[-1])
            return scatter_narrow(
                blocks[: narrow // 2], blocks[narrow // 2 :], (), last, small
            )

        own, other = combine_tokens(row_grads)
        plane_sum, sent = scatter_plane(own, other)
        mix_own, mix_other = combine_tokens(results, *sent)
        mix_sums = [mix_own[q].astype(F32) + mix_other[q].astype(F32) for q in range(planes)]
        mix_sent = [x.astype(BF) for x in mix_sums[1:]]
        plane_done = plane_sum.astype(BF)
        plane_sum = tie(plane_done, *arrived, *mix_other)
        mix_came = [
            swap(tie(mix_sent[q - 1], plane_done), "wide", 2 * q) for q in range(1, planes)[:2]
        ]
        ffn_message, ffn_came = scatter_rest(plane_sum, mix_came, 16)
        send_grads(ffn_came[-1])
        buffers = None
        for start, part in zip(grad_starts, arrived[:sent_early]):
            buffers = assemble(tie(part, ffn_came[-1]), start, local, buffers)
        ffn_message = tie(ffn_message, *buffers)

        upstream = cotangent.astype(F32)
        prob_grads = ffn_message[:, D : D + E] + ffn_message[:, D + E : D + 2 * E]
        logit_grads = (
            router_probs
            * (prob_grads - jnp.sum(router_probs * prob_grads, axis=-1, keepdims=True))
        ).astype(BF)
        ffn_grads = ffn_message[:, :D] + matmul(logit_grads, router_full, ((1,), (1,)))

        def norm_back(v, r, gain, dy):
            u = dy * gain
            return r * u - v * (r * r * r) * jnp.mean(u * v, axis=-1, keepdims=True)

        residual_grads = upstream + norm_back(residual, ffn_r, ffn_gain, ffn_grads)
        ffn_gain_part = jnp.sum(ffn_grads * residual * ffn_r, axis=0)
        message = jnp.concatenate(
            [residual_grads.astype(BF), logit_grads, jnp.zeros_like(logit_grads)], axis=1
        )

        plane_message = join(*gather_wide(message))
        plane_grads = plane_message[:, :D]
        attended_grads = matmul(plane_grads, output_rows, ((1,), (1,))).astype(BF)
        plane_rows = lax.dynamic_slice_in_dim(
            join([x[:count] for x in tokens_own], [x[:count] for x in tokens_other]),
            w * features,
            features,
            axis=1,
        )
        scaled, value_grads, dots, head_gain_parts = attend_back(
            turned, attended_grads, raw, scales, cosine, sine, head_gains, count
        )

        grad_output = matmul(attended, plane_grads, ((0,), (0,))).astype(BF)
        grad_value = matmul(normed, value_grads, ((0,), (0,))).astype(BF)
        early_parts = by_narrow(
            grad_output.reshape(1, narrow, rows, D),
            grad_value.reshape(wide, narrow, rows, features),
        )

        dots, dots_gathered = row_sums(dots.T)
        dots = dots.T / D
        shrink = scales * scales * scales * dots
        raw_grads = (
            scaled.reshape(plane_count, 2, features) * scales[:, :, None]
            - raw[:, : 2 * features].reshape(plane_count, 2, features) * shrink[:, :, None]
        ).astype(BF)
        raw_grads = jnp.concatenate([raw_grads.reshape(plane_count, 2 * features), value_grads], axis=1)
        mix_came += [
            swap(tie(mix_sent[q - 1], dots_gathered), "wide", 2 * q) for q in range(3, planes)
        ]
        grad_early, early_came = scatter_narrow(*early_parts)
        raw_grads = tie(raw_grads, arrived[-1], early_came[0])
        normed_grads = matmul(raw_grads, qkv, ((1,), (1,))).astype(BF)

        attn_gain_part = jnp.sum(normed_grads.astype(F32) * plane_tokens * inverse, axis=0)
        gain_parts = jnp.concatenate(
            [
                jnp.stack([attn_gain_part, ffn_gain_part]).reshape(2 * wide, features),
                head_gain_parts,
            ]
        ).T
        gain_columns = 2 * wide + 2
        router_part = matmul(plane_rows, plane_message[:, D : D + E], ((0,), (0,)))
        small_parts = jnp.concatenate([router_part.astype(BF), *split_low(gain_parts)], axis=1)
        small_parts = jnp.pad(
            small_parts, ((0, 0), (0, 2 * features - E - 2 * gain_columns))
        )
        plane_normed = normed_grads.reshape(planes, 2, count, D)
        normed_other = swap(plane_normed[:, 1], "wide", 1)
        normed_sums = [add_up([plane_normed[q, 0], normed_other[q]]) for q in range(planes)]
        normed_came = [
            swap(normed_sums[q].astype(BF), "wide", 2 * q)
            for q in range(1, planes)
        ]
        grad_raw = matmul(normed, raw_grads[:, : 2 * features], ((0,), (0,))).astype(BF)
        grad_raw, raw_came = scatter_narrow(
            *by_narrow(
                grad_raw.reshape(wide, narrow, rows, 2 * features),
                small_parts.reshape(1, narrow, rows, 2 * features),
            ),
            (),
            normed_came,
        )
        small_parts = grad_raw[wide]
        grad_router = small_parts[:, :E]
        gain_parts = small_parts[:, E : E + 2 * gain_columns]
        gain_parts = (gain_parts[:, :gain_columns] + gain_parts[:, gain_columns:]).T
        grad_gain_query, grad_gain_key = gain_parts[2 * wide], gain_parts[2 * wide + 1]
        blocks = D // (2 * features)
        grad_output = jnp.concatenate([grad_early[i] for i in range(blocks)], axis=1)
        grad_value = (
            grad_early[blocks:]
            .reshape(wide // 2, rows, 2, features)
            .transpose(0, 2, 1, 3)
            .reshape(wide, rows, features)
        )
        grad_qkv = jnp.concatenate([grad_raw[:wide], grad_value], axis=-1)
        mix_came[-1] = tie(mix_came[-1], raw_came[0])
        mixture = add_up([mix_sums[0], *mix_came]).astype(BF)
        block_out = (residual + scatter_rest(mixture)[0]).astype(BF)
        gain_rows = jnp.concatenate(
            [*split_low(gain_parts[:wide]), *split_low(gain_parts[wide : 2 * wide])], axis=1
        )
        gain_rows = jnp.pad(
            gain_rows[:, None, :], ((0, 0), (0, 15), (0, 3 * features - 4 * rows))
        )
        grad_qkv = jnp.concatenate([grad_qkv.astype(BF), gain_rows], axis=1)
        grad_qkv = lax.all_to_all(grad_qkv, "wide", 0, 0, tiled=True)
        gain_rows = jnp.sum(grad_qkv[:, rows, : 4 * rows].astype(F32), axis=0).reshape(4, rows)
        gain_sums = [gain_rows[0] + gain_rows[1], gain_rows[2] + gain_rows[3]]
        grad_qkv = grad_qkv[:, :rows].transpose(1, 0, 2).astype(F32)
        grad_query, grad_key, grad_value = [
            grad_qkv[..., i * features : (i + 1) * features].reshape(rows, D) for i in range(3)
        ]

        normed_grads = add_up([normed_sums[0], *normed_came])
        input_grad = (
            residual_grads
            + norm_back(tokens.astype(F32), inverse[:count], attn_gain, normed_grads)
        ).astype(BF)

        for start, part in zip(grad_starts[sent_early:], arrived[sent_early:]):
            buffers = assemble(tie(part, raw_came[1]), start, local, buffers)
        grad_gate, grad_up = buffers

        return (
            block_out, input_grad, grad_query, grad_key, grad_value,
            grad_output, grad_router,
            gain_sums[0], grad_gain_query, grad_gain_key, gain_sums[1],
            grad_gate, grad_up, down_grad, expert_counts,
        )

    return on_device


def solution(mesh):
    both = ("wide", "narrow")
    in_specs = (P(both, None), P(both), P(both, None), P(both, None))
    in_specs += (P(both, None),) * 5 + (P(both),) * 4 + (P("wide", "narrow", None),) * 3
    out_specs = (P(both, None),) * 7 + (P(both),) * 4 + (P("wide", "narrow", None),) * 3 + (P(),)
    return jax.shard_map(
        make_on_device(mesh.shape["wide"], mesh.shape["narrow"]),
        mesh=mesh,
        in_specs=in_specs,
        out_specs=out_specs,
        check_vma=False,
    )
```

```python
import functools

import jax
import jax.numpy as jnp
from jax import lax
from jax.experimental import pallas as pl
from jax.experimental.pallas import tpu as pltpu
from jax.sharding import PartitionSpec as P

D = 2048
H = 16
HD = 128
E = 64
TOPK = 8
CAP = 24
FF = 1024
LANES = 128
EXPERT_TILE = 768
EPSILON = 1e-05
THETA_BASE = 10000.0

BF = jnp.bfloat16
F32 = jnp.float32
VMEM_BYTES = 56 * 1024 * 1024


def matmul(a, b, dims):
    return lax.dot_general(a, b, (dims, ((), ())), preferred_element_type=F32)


def dispatch_body(pieces, each, *refs):
    picks = refs[0]
    sources = refs[1 : 1 + pieces]
    out = refs[-1]
    for q in range(pieces):
        rows = matmul(picks[q, 0], sources[q][...], ((1,), (0,))).astype(BF)
        out[:, q * each : (q + 1) * each, :] = rows.reshape(-1, each, rows.shape[-1])


def dispatch(picks, sources, half, buffer=None):
    pieces, pairs, slots, span = picks.shape
    width = sources[0].shape[1]
    each = 2 * CAP
    block = pieces * each
    in_specs = [pl.BlockSpec((pieces, 1, slots, span), lambda j: (0, j, 0, 0))]
    in_specs += [pl.BlockSpec((span, width), lambda j: (j, 0))] * pieces
    args = [picks, *sources]
    aliases = {}
    if buffer is not None:
        in_specs.append(pl.BlockSpec(memory_space=pl.ANY))
        aliases = {len(args): 0}
        args.append(buffer)
    return pl.pallas_call(
        functools.partial(dispatch_body, pieces, each),
        grid=(pairs,),
        in_specs=in_specs,
        out_specs=pl.BlockSpec(
            (slots // each, block, width), lambda j: (0, half * pairs + j, 0)
        ),
        out_shape=jax.ShapeDtypeStruct((slots // each, 2 * pairs * block, width), BF),
        input_output_aliases=aliases,
        compiler_params=pltpu.CompilerParams(vmem_limit_bytes=VMEM_BYTES),
        cost_estimate=pl.CostEstimate(
            flops=2 * pieces * pairs * slots * span * width,
            bytes_accessed=2 * pieces * pairs * (slots + span) * width,
            transcendentals=0,
        ),
        name="dispatch",
    )(*args)


def combine_body(pieces, each, picks, rows, *outs):
    for q in range(pieces):
        part = rows[:, q * each : (q + 1) * each, :].reshape(-1, rows.shape[-1])
        outs[q][...] = matmul(picks[q, 0], part, ((0,), (0,))).astype(BF)


def combine(picks, rows, half):
    pieces, pairs, slots, span = picks.shape
    each = 2 * CAP
    local, _, width = rows.shape
    return pl.pallas_call(
        functools.partial(combine_body, pieces, each),
        grid=(pairs,),
        in_specs=[
            pl.BlockSpec((pieces, 1, slots, span), lambda j: (0, j, 0, 0)),
            pl.BlockSpec((local, pieces * each, width), lambda j: (0, half * pairs + j, 0)),
        ],
        out_specs=[pl.BlockSpec((span, width), lambda j: (j, 0))] * pieces,
        out_shape=[jax.ShapeDtypeStruct((pairs * span, width), BF)] * pieces,
        compiler_params=pltpu.CompilerParams(vmem_limit_bytes=VMEM_BYTES),
        cost_estimate=pl.CostEstimate(
            flops=2 * pieces * pairs * slots * span * width,
            bytes_accessed=2 * pieces * pairs * (slots + span) * width,
            transcendentals=0,
        ),
        name="combine",
    )(picks, rows)


def expert_body(parts, tiles, start, aliased, *refs):
    where, rows_ref, ups_ref, weights_ref, down_ref = refs[:5]
    rest = refs[5 + aliased :]
    results_ref, row_grads_ref, weight_grads_ref, down_grad_ref, result_grads, *sums = rest
    tile = pl.program_id(1)
    width = FF // parts
    depth = D // parts
    slices = [slice(s * depth, (s + 1) * depth) for s in range(parts)]

    both = None
    for s in range(parts):
        term = matmul(rows_ref[0, :, slices[s]], weights_ref[s, 0], ((1,), (0,)))
        both = term if both is None else both + term
    gate_value = both[:, :width]
    up_value = both[:, width:]
    sigma = 1.0 / (1.0 + jnp.exp(-gate_value))
    silu = gate_value * sigma
    hidden = (silu * up_value).astype(BF)

    expert = where[1] + start + pl.program_id(0)
    lane = lax.broadcasted_iota(jnp.int32, (rows_ref.shape[1], LANES), 1)
    high = lane == expert
    low = lane == expert + E
    probs = rows_ref[0, :, D:].astype(F32)
    weight = jnp.sum(jnp.where(high | low, probs, 0.0), axis=1, keepdims=True)

    gate_grad = None
    hidden_grads = None
    for columns in slices:
        down = down_ref[0, :, columns]
        results = matmul(hidden, down, ((1,), (0,)))
        upstream = ups_ref[0, :, columns].astype(F32)
        dot = jnp.sum(upstream * results, axis=1, keepdims=True)
        gate_grad = dot if gate_grad is None else gate_grad + dot
        results_ref[0, :, columns] = (weight * results).astype(BF)
        part = (weight * upstream).astype(BF)
        result_grads[:, columns] = part
        term = matmul(part, down, ((1,), (1,)))
        hidden_grads = term if hidden_grads is None else hidden_grads + term

    gate_value_grads = (
        hidden_grads * up_value * (sigma * (1.0 + gate_value * (1.0 - sigma)))
    ).astype(BF)
    up_value_grads = (hidden_grads * silu).astype(BF)
    both_grads = jnp.concatenate([gate_value_grads, up_value_grads], axis=1)
    top = gate_grad.astype(BF)
    bottom = (gate_grad - top.astype(F32)).astype(BF)
    row_grads_ref[0, :, D:] = jnp.where(
        high, top.astype(F32), jnp.where(low, bottom.astype(F32), 0.0)
    ).astype(BF)
    for s in range(parts):
        row_grads_ref[0, :, slices[s]] = matmul(
            both_grads, weights_ref[s, 0], ((1,), (1,))
        ).astype(BF)

    def weight_term(s):
        return matmul(rows_ref[0, :, slices[s]], both_grads, ((0,), (0,)))

    def down_term(columns):
        return matmul(hidden, result_grads[:, columns], ((0,), (0,)))

    if tiles == 1:
        for s in range(parts):
            weight_grads_ref[s, 0] = weight_term(s).astype(BF)
            down_grad_ref[0, :, slices[s]] = down_term(slices[s])
        return
    weight_sums = sums[0]
    first = tile == 0

    @pl.when(first)
    def _():
        for s in range(parts):
            weight_sums[s] = weight_term(s)
            down_grad_ref[0, :, slices[s]] = down_term(slices[s])

    @pl.when(jnp.logical_not(first))
    def _():
        for s in range(parts):
            weight_sums[s] += weight_term(s)
            down_grad_ref[0, :, slices[s]] += down_term(slices[s])

    @pl.when(tile == tiles - 1)
    def _():
        for s in range(parts):
            weight_grads_ref[s, 0] = weight_sums[s].astype(BF)


def expert_chunk(where, rows, ups, weights, down, start, experts, offset, group, at, buffers):
    parts, _, depth, width2 = weights.shape
    local, total_rows, wide_row = rows.shape
    tile = EXPERT_TILE
    tiles = total_rows // tile
    slice_ff = down.shape[1]
    weight_spec = pl.BlockSpec((parts, 1, depth, width2), lambda e, i, c: (0, offset + e, 0, 0))
    down_spec = pl.BlockSpec((1, slice_ff, D), lambda e, i, c: (start + e, 0, 0))
    in_specs = [
        pl.BlockSpec((1, tile, wide_row), lambda e, i, c: (start + e, i, 0)),
        pl.BlockSpec((1, tile, D), lambda e, i, c: (start + e, i, 0)),
        weight_spec,
        down_spec,
    ]
    args = [where, rows, ups, weights, down]
    aliases = {}
    for index, buffer in enumerate(buffers):
        if buffer is not None:
            in_specs.append(pl.BlockSpec(memory_space=pl.ANY))
            aliases[len(args)] = index
            args.append(buffer)
    return pl.pallas_call(
        functools.partial(expert_body, parts, tiles, start, len(aliases)),
        grid_spec=pltpu.PrefetchScalarGridSpec(
            num_scalar_prefetch=1,
            grid=(experts, tiles),
            in_specs=in_specs,
            out_specs=[
                pl.BlockSpec((1, tile, D), lambda e, i, c: (start + e, i, 0)),
                pl.BlockSpec((1, tile, wide_row), lambda e, i, c: (start + e, i, 0)),
                pl.BlockSpec((parts, 1, depth, width2), lambda e, i, c: (0, at + e, 0, 0)),
                down_spec,
            ],
            scratch_shapes=[pltpu.VMEM((tile, D), BF)]
            + ([pltpu.VMEM((parts, depth, width2), F32)] if tiles > 1 else []),
        ),
        out_shape=[
            jax.ShapeDtypeStruct((local, total_rows, D), BF),
            jax.ShapeDtypeStruct((local, total_rows, wide_row), BF),
            jax.ShapeDtypeStruct((parts, group, depth, width2), BF),
            jax.ShapeDtypeStruct((local, slice_ff, D), F32),
        ],
        input_output_aliases=aliases,
        compiler_params=pltpu.CompilerParams(vmem_limit_bytes=VMEM_BYTES),
        cost_estimate=pl.CostEstimate(
            flops=18 * experts * total_rows * D * slice_ff,
            bytes_accessed=8 * experts * total_rows * D + 18 * experts * D * slice_ff,
            transcendentals=experts * total_rows * slice_ff,
        ),
        name="experts",
    )(*args)


def slice_body(parts, width, gate_ref, up_ref, out):
    for s in range(parts):
        columns = slice(s * width, (s + 1) * width)
        out[s, 0, :, :width] = gate_ref[0, :, columns]
        out[s, 0, :, width:] = up_ref[0, :, columns]


def slice_weights(gate, up, start, experts, parts):
    depth = gate.shape[1]
    width = FF // parts
    spec = pl.BlockSpec((1, depth, FF), lambda e: (start + e, 0, 0))
    return pl.pallas_call(
        functools.partial(slice_body, parts, width),
        grid=(experts,),
        in_specs=[spec, spec],
        out_specs=pl.BlockSpec((parts, 1, depth, 2 * width), lambda e: (0, e, 0, 0)),
        out_shape=jax.ShapeDtypeStruct((parts, experts, depth, 2 * width), BF),
        compiler_params=pltpu.CompilerParams(vmem_limit_bytes=VMEM_BYTES),
        cost_estimate=pl.CostEstimate(
            flops=0, bytes_accessed=8 * experts * depth * FF, transcendentals=0
        ),
        name="slice_weights",
    )(gate, up)


def assemble_body(parts, width, *refs):
    source = refs[0]
    gate_ref, up_ref = refs[-2], refs[-1]
    for s in range(parts):
        columns = slice(s * width, (s + 1) * width)
        gate_ref[0, :, columns] = source[s, 0, :, :width].astype(F32)
        up_ref[0, :, columns] = source[s, 0, :, width:].astype(F32)


def assemble(source, start, local, buffers):
    parts, experts, depth, width2 = source.shape
    in_specs = [pl.BlockSpec((parts, 1, depth, width2), lambda e: (0, e, 0, 0))]
    args = [source]
    aliases = {}
    if buffers is not None:
        in_specs += [pl.BlockSpec(memory_space=pl.ANY)] * 2
        aliases = {1: 0, 2: 1}
        args += list(buffers)
    spec = pl.BlockSpec((1, depth, FF), lambda e: (start + e, 0, 0))
    return pl.pallas_call(
        functools.partial(assemble_body, parts, width2 // 2),
        grid=(experts,),
        in_specs=in_specs,
        out_specs=[spec, spec],
        out_shape=[jax.ShapeDtypeStruct((local, depth, FF), F32)] * 2,
        input_output_aliases=aliases,
        compiler_params=pltpu.CompilerParams(vmem_limit_bytes=VMEM_BYTES),
        cost_estimate=pl.CostEstimate(
            flops=0, bytes_accessed=6 * experts * depth * FF * 2, transcendentals=0
        ),
        name="assemble",
    )(*args)


def turn(x, cosine, sine):
    return x * cosine + pltpu.roll(x, HD // 2, 1) * sine


def probabilities(query, key):
    scores = matmul(query, key, ((1,), (1,))) * HD ** (-0.5)
    row = lax.broadcasted_iota(jnp.int32, scores.shape, 0)
    column = lax.broadcasted_iota(jnp.int32, scores.shape, 1)
    causal = row >= column
    scores = jnp.where(causal, scores, -1e30)
    powers = jnp.exp(scores - jnp.max(scores, axis=-1, keepdims=True))
    return powers / jnp.sum(powers, axis=-1, keepdims=True), causal


def attend_body(raw, scales, cosine, sine, gains, turned, attended):
    features = attended.shape[1]
    for part in range(2):
        scale = scales[:, part : part + 1]
        for at in range(0, features, HD):
            columns = slice(part * features + at, part * features + at + HD)
            x = raw[:, columns] * scale * gains[part : part + 1, at : at + HD]
            turned[:, columns] = turn(x, cosine[...], sine[...]).astype(BF)
    turned[:, 2 * features :] = raw[:, 2 * features :].astype(BF)
    for at in range(0, features, HD):
        query = turned[:, at : at + HD]
        key = turned[:, features + at : features + at + HD]
        value = turned[:, 2 * features + at : 2 * features + at + HD]
        probs, _ = probabilities(query, key)
        attended[:, at : at + HD] = matmul(probs.astype(BF), value, ((1,), (0,))).astype(BF)


def attend(raw, scales, cosine, sine, gains, count):
    total, features = raw.shape[0], raw.shape[1] // 3

    def block(x):
        return pl.BlockSpec((count, x.shape[1]), lambda i: (i, 0))

    return pl.pallas_call(
        attend_body,
        grid=(total // count,),
        in_specs=[block(x) for x in (raw, scales, cosine, sine)]
        + [pl.BlockSpec(gains.shape, lambda i: (0, 0))],
        out_specs=[
            pl.BlockSpec((count, 3 * features), lambda i: (i, 0)),
            pl.BlockSpec((count, features), lambda i: (i, 0)),
        ],
        out_shape=[
            jax.ShapeDtypeStruct((total, 3 * features), BF),
            jax.ShapeDtypeStruct((total, features), BF),
        ],
        compiler_params=pltpu.CompilerParams(vmem_limit_bytes=VMEM_BYTES),
        cost_estimate=pl.CostEstimate(
            flops=4 * total * count * features,
            bytes_accessed=20 * total * features,
            transcendentals=total * count,
        ),
        name="attend",
    )(raw, scales, cosine, sine, gains)


def attend_back_body(turned, grads, raw, scales, cosine, sine, gains, scaled, value_grads, sums, gain_grads):
    features = grads.shape[1]
    scale = HD ** (-0.5)
    dots = [0.0, 0.0]
    first = pl.program_id(0) == 0
    for at in range(0, features, HD):
        query = turned[:, at : at + HD]
        key = turned[:, features + at : features + at + HD]
        value = turned[:, 2 * features + at : 2 * features + at + HD]
        grad = grads[:, at : at + HD]
        probs, causal = probabilities(query, key)
        value_grads[:, at : at + HD] = matmul(probs.astype(BF), grad, ((0,), (0,))).astype(BF)
        prob_grads = matmul(grad, value, ((1,), (1,)))
        score_grads = probs * (prob_grads - jnp.sum(probs * prob_grads, axis=-1, keepdims=True))
        score_grads = jnp.where(causal, score_grads, 0.0).astype(BF)
        turned_grads = (
            matmul(score_grads, key, ((1,), (0,))) * scale,
            matmul(score_grads, query, ((0,), (0,))) * scale,
        )
        for part in range(2):
            columns = slice(part * features + at, part * features + at + HD)
            x = raw[:, columns]
            dy = turn(turned_grads[part], cosine[...], -sine[...])
            u = dy * gains[part : part + 1, at : at + HD]
            scaled[:, columns] = u
            dots[part] = dots[part] + jnp.sum(u * x, axis=-1, keepdims=True)
            gain_grad = jnp.sum(dy * x * scales[:, part : part + 1], axis=0, keepdims=True)
            old = gain_grads[part : part + 1, at : at + HD]
            gain_grads[part : part + 1, at : at + HD] = gain_grad + jnp.where(first, 0.0, old)
    sums[...] = jnp.concatenate(dots, axis=1)


def attend_back(turned, grads, raw, scales, cosine, sine, gains, count):
    total, features = grads.shape

    def block(x):
        return pl.BlockSpec((count, x.shape[1]), lambda i: (i, 0))

    out_shape = [
        jax.ShapeDtypeStruct((total, 2 * features), F32),
        jax.ShapeDtypeStruct((total, features), BF),
        jax.ShapeDtypeStruct((total, 2), F32),
    ]
    return pl.pallas_call(
        attend_back_body,
        grid=(total // count,),
        in_specs=[block(x) for x in (turned, grads, raw, scales, cosine, sine)]
        + [pl.BlockSpec(gains.shape, lambda i: (0, 0))],
        out_specs=[block(x) for x in out_shape] + [pl.BlockSpec(gains.shape, lambda i: (0, 0))],
        out_shape=[*out_shape, jax.ShapeDtypeStruct(gains.shape, F32)],
        compiler_params=pltpu.CompilerParams(vmem_limit_bytes=VMEM_BYTES),
        cost_estimate=pl.CostEstimate(
            flops=12 * total * count * features,
            bytes_accessed=30 * total * features,
            transcendentals=total * count,
        ),
        name="attend_back",
    )(turned, grads, raw, scales, cosine, sine, gains)


def pick_body(where, *refs):
    half = pl.num_programs(0) // 2

    def fill(out):
        width = out.shape[-1]
        at = 0
        for source in refs[:-2]:
            outer, _, _, own = source.shape
            if own >= width:
                for i in range(outer):
                    for column in range(0, own, width):
                        out[0, at] = source[i, 0, :, column : column + width]
                        at += 1
            else:
                for i in range(0, outer, width // own):
                    for k in range(width // own):
                        out[0, at, :, k * own : (k + 1) * own] = source[i + k, 0]
                    at += 1

    @pl.when(pl.program_id(0) < half)
    def _():
        fill(refs[-2])

    @pl.when(pl.program_id(0) >= half)
    def _():
        fill(refs[-1])


def pick_blocks(order, width, *sources):
    rows = sources[0].shape[2]
    half = order.shape[0] // 2
    outer = sum(x.shape[0] * x.shape[3] for x in sources) // width
    shape = (1, outer, rows, width)
    return pl.pallas_call(
        pick_body,
        grid_spec=pltpu.PrefetchScalarGridSpec(
            num_scalar_prefetch=1,
            grid=(2 * half,),
            in_specs=[
                pl.BlockSpec((x.shape[0], 1, *x.shape[2:]), lambda k, c: (0, c[k], 0, 0))
                for x in sources
            ],
            out_specs=[
                pl.BlockSpec(shape, lambda k, c: (jnp.minimum(k, half - 1), 0, 0, 0)),
                pl.BlockSpec(shape, lambda k, c: (jnp.maximum(k - half, 0), 0, 0, 0)),
            ],
        ),
        out_shape=[jax.ShapeDtypeStruct((half, *shape[1:]), BF)] * 2,
        compiler_params=pltpu.CompilerParams(vmem_limit_bytes=VMEM_BYTES),
        cost_estimate=pl.CostEstimate(
            flops=0, bytes_accessed=8 * half * outer * rows * width, transcendentals=0
        ),
        name="pick_blocks",
    )(order, *sources)


def tie(value, *after):
    return lax.optimization_barrier((value, *after))[0]


def split_low(x):
    top = x.astype(BF)
    return top, (x - top.astype(F32)).astype(BF)


def add_up(parts):
    total = parts[0].astype(F32)
    for part in parts[1:]:
        total = total + part.astype(F32)
    return total


def make_on_device(wide, narrow):
    planes = wide // 2
    local = E // wide
    heads = H // wide
    features = heads * HD
    if local == 8:
        sizes, early, groups = [2, 3, 3], 2, [[0], [1], [2]]
        parts = groups
    else:
        sizes = [1] * local
        early, groups = min(2, local), [[c] for c in range(local)]
        parts = groups
    calls = len(sizes)
    starts = [sum(sizes[:c]) for c in range(calls)]
    slice_ff = FF // narrow
    both_axes = ("wide", "narrow")

    def swap(x, axis, r):
        size = wide if axis == "wide" else narrow
        return lax.ppermute(x, axis, [(i, i ^ r) for i in range(size)])

    bits = [1 << i for i in reversed(range(narrow.bit_length() - 1))]
    near = [0]
    for bit in bits:
        near = near + [r ^ bit for r in near]

    def swap_marked(x, bit, small):
        rest = swap(x[:-small], "narrow", bit)
        marker = swap(x[-small:], "narrow", bit)
        return jnp.concatenate([rest, marker], axis=0), marker

    def gather_narrow(x, *after):
        for i, bit in enumerate(bits):
            if i and after:
                x = tie(x, *after)
            x = jnp.concatenate([x, swap(x, "narrow", bit)], axis=0)
        return x

    def scatter_narrow(keep, send, step=(), last=(), small=0):
        arrivals = []
        for bit in reversed(bits):
            marker = None
            if small and bit == bits[0]:
                came, marker = swap_marked(send[0], bit, small)
                came = came[None]
            else:
                came = swap(send, "narrow", bit)
            if last and bit == bits[0]:
                came = tie(came, *last)
            arrivals.append(came)
            if marker is not None:
                arrivals.append(marker)
            total = keep.astype(F32) + came.astype(F32)
            half = total.shape[0] // 2
            keep, send = total[:half], total[half:].astype(BF)
            if step:
                send = tie(send, *step)
        return total[0], arrivals

    def gather_planes(x):
        return [x] + [swap(x, "wide", 2 * q) for q in range(1, planes)]

    def cross(pieces):
        return [swap(piece, "wide", 1) for piece in pieces]

    def gather_wide(x):
        own = gather_planes(x)
        return own, cross(own)

    def join(own, other):
        return jnp.concatenate([piece for pair in zip(own, other) for piece in pair], axis=0)

    def scatter_wide(own, other):
        return scatter_plane(own, swap(other, "wide", 1))[0]

    def scatter_plane(own, came, *after):
        sums = [own[q].astype(F32) + came[q].astype(F32) for q in range(planes)]
        sent = [x.astype(BF) for x in sums[1:]]
        if after:
            sent = list(lax.optimization_barrier((*sent, *after))[: planes - 1])
        total = sums[0]
        for q in range(1, planes):
            total = total + swap(sent[q - 1], "wide", 2 * q).astype(F32)
        return total, sent

    def on_device(
        tokens, positions, routes, cotangent,
        w_query, w_key, w_value, w_output, w_router,
        gain_attn, gain_query, gain_key, gain_ffn,
        w_gate, w_up, w_down,
    ):
        count = tokens.shape[0]
        rows = w_query.shape[0]
        w = lax.axis_index("wide")
        n = lax.axis_index("narrow")
        where = jnp.stack([n, w * local, w]).astype(jnp.int32)
        wide_order = jnp.arange(wide) ^ w
        near_order = jnp.array(near) ^ n
        narrow_order = jnp.array([near.index(r) for r in range(narrow)])[jnp.arange(narrow) ^ n]

        def by_narrow(*x):
            return pick_blocks(near_order, 2 * features, *x)

        routed = jnp.any(
            routes[:, :, None] == jnp.arange(E, dtype=jnp.int32)[None, None, :], axis=1
        )
        earlier = matmul(
            jnp.tril(jnp.ones((count, count), BF), -1), routed.astype(BF), ((1,), (0,))
        )
        slots = jnp.where(routed, earlier, -1.0).astype(BF).T

        small = jnp.concatenate(
            [
                w_router.reshape(-1), gain_attn, gain_query, gain_key, gain_ffn,
                positions.astype(BF),
            ]
        )
        small_rows = -(-small.shape[0] // LANES)
        bundle_rows = -(-(E + small_rows) // 16) * 16
        small = jnp.pad(small, (0, (bundle_rows - E) * LANES - small.shape[0]))
        bundle = jnp.concatenate([slots, small.reshape(-1, LANES)], axis=0)
        bundle_z = lax.all_gather(bundle, "narrow")
        stacked = jnp.concatenate(
            [x.reshape(rows, wide, features) for x in (w_query, w_key, w_value)], axis=-1
        ).transpose(1, 0, 2)
        columns = lax.all_to_all(stacked, "wide", 0, 0, tiled=True)
        bundles = lax.all_gather(bundle_z, "wide")
        all_slots = bundles[:, :, :E, :]
        all_small = bundles[:, :, E:, :].reshape(wide, narrow, -1)
        base = rows * E
        plane_positions = lax.dynamic_index_in_dim(
            all_small[:, :, base + 4 * rows : base + 4 * rows + count], n, 1, keepdims=False
        )
        plane_positions = jnp.take(plane_positions, wide_order, axis=0).reshape(wide * count)
        router_full = all_small[:, :, :base].reshape(D, E)
        gains = [
            all_small[:, :, base + i * rows : base + (i + 1) * rows].reshape(D).astype(F32)
            for i in range(4)
        ]
        attn_gain, query_gain, key_gain, ffn_gain = gains
        query_gain = lax.dynamic_slice_in_dim(query_gain, w * features, features)
        key_gain = lax.dynamic_slice_in_dim(key_gain, w * features, features)
        expert_counts = jnp.sum((all_slots >= 0).astype(jnp.int32), axis=(0, 1, 3))

        tokens_near = gather_wide(tokens)
        plane_tokens = join(*tokens_near).astype(F32)
        plane_count = plane_tokens.shape[0]

        sliced = [
            slice_weights(w_gate, w_up, starts[p[0]], sum(sizes[c] for c in p), narrow)
            for p in parts
        ]
        expert_weights = []

        def send_weights(*after):
            part = tie(sliced[len(expert_weights)], *after)
            expert_weights.append(lax.all_to_all(part, "narrow", 0, 0, tiled=True))

        ups_z = gather_narrow(cotangent, bundle_z)
        output_rows = gather_narrow(w_output[None])
        send_weights(columns, bundles, ups_z)
        output_rows = jnp.take(output_rows, narrow_order, axis=0).reshape(features, D)
        ups_own = gather_planes(tie(ups_z, *tokens_near[0], *tokens_near[1]))
        columns = lax.optimization_barrier(
            (columns, expert_weights[0], *tokens_near[0], *tokens_near[1], *ups_own[:3])
        )[0]
        columns = gather_narrow(columns[None])
        gathered = columns
        columns = jnp.take(columns, narrow_order, axis=0)
        qkv = columns.transpose(1, 0, 2, 3).reshape(D, 3 * features)
        while len(expert_weights) < early:
            send_weights(gathered, *expert_weights[1:])

        local_slots = lax.dynamic_slice_in_dim(all_slots, w * local, local, axis=2)
        local_slots = jnp.take(jnp.take(local_slots, wide_order, axis=0), near_order, axis=1)
        pairs = narrow // 2
        local_slots = (
            local_slots.reshape(planes, 2, pairs, 2, local, count)
            .transpose(1, 0, 2, 4, 3, 5)
            .reshape(2, planes, pairs, local, 1, 2 * count)
        )
        row = jnp.arange(2 * CAP)[:, None]
        lane = jnp.arange(2 * count)[None, :]
        picks = (
            ((local_slots == (row % CAP).astype(BF)) & (row // CAP == lane // count))
            .astype(BF)
            .reshape(2, planes, pairs, local * 2 * CAP, 2 * count)
        )
        picks_own, picks_other = picks[0], picks[1]
        inverse = lax.rsqrt(jnp.mean(plane_tokens * plane_tokens, axis=-1, keepdims=True) + EPSILON)
        normed = (plane_tokens * inverse * attn_gain).astype(BF)
        raw = matmul(normed, tie(qkv, *ups_own), ((1,), (0,)))

        def row_sums(sums):
            sums = jnp.take(sums.reshape(2, wide, count), wide_order, axis=1)
            gathered = lax.all_gather(sums, "wide")
            sums = jnp.sum(gathered, axis=0)
            return jnp.take(sums, wide_order, axis=1).reshape(2, plane_count), gathered

        squares = jnp.stack(
            [
                jnp.sum(x * x, axis=-1)
                for x in (raw[:, :features], raw[:, features : 2 * features])
            ]
        )
        scales = lax.rsqrt(row_sums(squares)[0] / D + EPSILON).T
        frequency = THETA_BASE ** (-2.0 * jnp.arange(HD // 2, dtype=F32) / HD)
        angles = plane_positions.astype(F32)[:, None] * frequency[None, :]
        cosine, sine = jnp.cos(angles), jnp.sin(angles)
        cosine = jnp.concatenate([cosine, cosine], axis=1)
        sine = jnp.concatenate([-sine, sine], axis=1)
        head_gains = jnp.stack([query_gain, key_gain])
        turned, attended = attend(raw, scales, cosine, sine, head_gains, count)
        if early > 2:
            attended = tie(attended, expert_weights[1], sliced[2])
        branch = matmul(attended, output_rows, ((1,), (0,))).astype(BF)
        branch = branch.reshape(planes, 2, count, D)
        branch = scatter_wide(branch[:, 0], branch[:, 1])

        residual = tokens.astype(F32) + branch
        ffn_r = lax.rsqrt(jnp.mean(residual * residual, axis=-1, keepdims=True) + EPSILON)
        normed_ffn = (residual * ffn_r * ffn_gain).astype(BF)
        logits = matmul(normed_ffn, router_full, ((1,), (0,)))
        router_powers = jnp.exp(logits - jnp.max(logits, axis=-1, keepdims=True))
        router_probs = router_powers / jnp.sum(router_powers, axis=-1, keepdims=True)

        message = jnp.concatenate([normed_ffn, *split_low(router_probs)], axis=1)
        ups = dispatch(picks_own, ups_own, 0)
        ups = dispatch(picks_other, cross(ups_own), 1, ups)
        message = gather_narrow(tie(message, ups, expert_weights[-1]))
        if len(parts) > early:
            send_weights(message)
        tokens_own = gather_planes(message)
        while len(expert_weights) < len(parts):
            send_weights(*tokens_own)
        if len(parts) > early + 1:
            tokens_own[0] = tie(tokens_own[0], expert_weights[early])
        tokens_other = cross(tokens_own)
        expert_rows = dispatch(picks_own, tokens_own, 0)
        expert_rows = dispatch(picks_other, tokens_other, 1, expert_rows)

        came = []
        held = [None] * 4
        for c in range(calls):
            if c == 1:
                expert_rows = tie(expert_rows, expert_weights[-1])
            group = next(g for g in groups if c in g)
            part = next(i for i, p in enumerate(parts) if c in p)
            if c == group[0]:
                held[2] = None
            held = [*expert_chunk(
                where, expert_rows, ups, expert_weights[part], w_down, starts[c], sizes[c],
                starts[c] - starts[parts[part][0]], sum(sizes[g] for g in group), starts[c] - starts[group[0]], held,
            )]
            if c == group[-1]:
                came.append(held[2])
        results, row_grads, _, down_grad = held
        arrived = []

        def send_grads(*after):
            part = came[len(arrived)]
            part = tie(part, *after) if after else part
            arrived.append(lax.all_to_all(part, "narrow", 0, 0, tiled=True))

        grad_starts = [starts[group[0]] for group in groups]
        sent_early = len(groups) - 1
        for g in range(sent_early):
            send_grads(*([row_grads] if g else []))

        def combine_tokens(terms, *after):
            terms = tie(terms, *after) if after else terms
            other = cross(combine(picks_other, terms, 1))
            return list(combine(picks_own, terms, 0)), other

        def scatter_rest(plane_sum, last=(), small=0):
            blocks = plane_sum.reshape(narrow, count, plane_sum.shape[-1])
            return scatter_narrow(
                blocks[: narrow // 2], blocks[narrow // 2 :], (), last, small
            )

        own, other = combine_tokens(row_grads)
        plane_sum, sent = scatter_plane(own, other)
        mix_own, mix_other = combine_tokens(results, *sent)
        mix_sums = [mix_own[q].astype(F32) + mix_other[q].astype(F32) for q in range(planes)]
        mix_sent = [x.astype(BF) for x in mix_sums[1:]]
        plane_done = plane_sum.astype(BF)
        plane_sum = tie(plane_done, *arrived, *mix_other)
        mix_came = [
            swap(tie(mix_sent[q - 1], plane_done), "wide", 2 * q) for q in range(1, planes)[:2]
        ]
        ffn_message, ffn_came = scatter_rest(plane_sum, mix_came, 16)
        send_grads(ffn_came[-1])
        buffers = None
        for start, part in zip(grad_starts, arrived[:sent_early]):
            buffers = assemble(tie(part, ffn_came[-1]), start, local, buffers)
        ffn_message = tie(ffn_message, *buffers)

        upstream = cotangent.astype(F32)
        prob_grads = ffn_message[:, D : D + E] + ffn_message[:, D + E : D + 2 * E]
        logit_grads = (
            router_probs
            * (prob_grads - jnp.sum(router_probs * prob_grads, axis=-1, keepdims=True))
        ).astype(BF)
        ffn_grads = ffn_message[:, :D] + matmul(logit_grads, router_full, ((1,), (1,)))

        def norm_back(v, r, gain, dy):
            u = dy * gain
            return r * u - v * (r * r * r) * jnp.mean(u * v, axis=-1, keepdims=True)

        residual_grads = upstream + norm_back(residual, ffn_r, ffn_gain, ffn_grads)
        ffn_gain_part = jnp.sum(ffn_grads * residual * ffn_r, axis=0)
        message = jnp.concatenate(
            [residual_grads.astype(BF), logit_grads, jnp.zeros_like(logit_grads)], axis=1
        )

        plane_message = join(*gather_wide(message))
        plane_grads = plane_message[:, :D]
        attended_grads = matmul(plane_grads, output_rows, ((1,), (1,))).astype(BF)
        plane_rows = lax.dynamic_slice_in_dim(
            join([x[:count] for x in tokens_own], [x[:count] for x in tokens_other]),
            w * features,
            features,
            axis=1,
        )
        scaled, value_grads, dots, head_gain_parts = attend_back(
            turned, attended_grads, raw, scales, cosine, sine, head_gains, count
        )

        grad_output = matmul(attended, plane_grads, ((0,), (0,))).astype(BF)
        grad_value = matmul(normed, value_grads, ((0,), (0,))).astype(BF)
        early_parts = by_narrow(
            grad_output.reshape(1, narrow, rows, D),
            grad_value.reshape(wide, narrow, rows, features),
        )

        dots, dots_gathered = row_sums(dots.T)
        dots = dots.T / D
        shrink = scales * scales * scales * dots
        raw_grads = (
            scaled.reshape(plane_count, 2, features) * scales[:, :, None]
            - raw[:, : 2 * features].reshape(plane_count, 2, features) * shrink[:, :, None]
        ).astype(BF)
        raw_grads = jnp.concatenate([raw_grads.reshape(plane_count, 2 * features), value_grads], axis=1)
        mix_came += [
            swap(tie(mix_sent[q - 1], dots_gathered), "wide", 2 * q) for q in range(3, planes)
        ]
        grad_early, early_came = scatter_narrow(*early_parts)
        raw_grads = tie(raw_grads, arrived[-1], early_came[0])
        normed_grads = matmul(raw_grads, qkv, ((1,), (1,))).astype(BF)

        attn_gain_part = jnp.sum(normed_grads.astype(F32) * plane_tokens * inverse, axis=0)
        gain_parts = jnp.concatenate(
            [
                jnp.stack([attn_gain_part, ffn_gain_part]).reshape(2 * wide, features),
                head_gain_parts,
            ]
        ).T
        gain_columns = 2 * wide + 2
        router_part = matmul(plane_rows, plane_message[:, D : D + E], ((0,), (0,)))
        small_parts = jnp.concatenate([router_part.astype(BF), *split_low(gain_parts)], axis=1)
        small_parts = jnp.pad(
            small_parts, ((0, 0), (0, 2 * features - E - 2 * gain_columns))
        )
        plane_normed = normed_grads.reshape(planes, 2, count, D)
        normed_other = swap(plane_normed[:, 1], "wide", 1)
        normed_sums = [add_up([plane_normed[q, 0], normed_other[q]]) for q in range(planes)]
        normed_came = [
            swap(normed_sums[q].astype(BF), "wide", 2 * q)
            for q in range(1, planes)
        ]
        grad_raw = matmul(normed, raw_grads[:, : 2 * features], ((0,), (0,))).astype(BF)
        grad_raw, raw_came = scatter_narrow(
            *by_narrow(
                grad_raw.reshape(wide, narrow, rows, 2 * features),
                small_parts.reshape(1, narrow, rows, 2 * features),
            ),
            (),
            normed_came,
        )
        small_parts = grad_raw[wide]
        grad_router = small_parts[:, :E]
        gain_parts = small_parts[:, E : E + 2 * gain_columns]
        gain_parts = (gain_parts[:, :gain_columns] + gain_parts[:, gain_columns:]).T
        grad_gain_query, grad_gain_key = gain_parts[2 * wide], gain_parts[2 * wide + 1]
        blocks = D // (2 * features)
        grad_output = jnp.concatenate([grad_early[i] for i in range(blocks)], axis=1)
        grad_value = (
            grad_early[blocks:]
            .reshape(wide // 2, rows, 2, features)
            .transpose(0, 2, 1, 3)
            .reshape(wide, rows, features)
        )
        grad_qkv = jnp.concatenate([grad_raw[:wide], grad_value], axis=-1)
        mix_came[-1] = tie(mix_came[-1], raw_came[0])
        mixture = add_up([mix_sums[0], *mix_came]).astype(BF)
        block_out = (residual + scatter_rest(mixture)[0]).astype(BF)
        gain_rows = jnp.concatenate(
            [*split_low(gain_parts[:wide]), *split_low(gain_parts[wide : 2 * wide])], axis=1
        )
        gain_rows = jnp.pad(
            gain_rows[:, None, :], ((0, 0), (0, 15), (0, 3 * features - 4 * rows))
        )
        grad_qkv = jnp.concatenate([grad_qkv.astype(BF), gain_rows], axis=1)
        grad_qkv = lax.all_to_all(grad_qkv, "wide", 0, 0, tiled=True)
        gain_rows = jnp.sum(grad_qkv[:, rows, : 4 * rows].astype(F32), axis=0).reshape(4, rows)
        gain_sums = [gain_rows[0] + gain_rows[1], gain_rows[2] + gain_rows[3]]
        grad_qkv = grad_qkv[:, :rows].transpose(1, 0, 2).astype(F32)
        grad_query, grad_key, grad_value = [
            grad_qkv[..., i * features : (i + 1) * features].reshape(rows, D) for i in range(3)
        ]

        normed_grads = add_up([normed_sums[0], *normed_came])
        input_grad = (
            residual_grads
            + norm_back(tokens.astype(F32), inverse[:count], attn_gain, normed_grads)
        ).astype(BF)

        for start, part in zip(grad_starts[sent_early:], arrived[sent_early:]):
            buffers = assemble(tie(part, raw_came[1]), start, local, buffers)
        grad_gate, grad_up = buffers

        return (
            block_out, input_grad, grad_query, grad_key, grad_value,
            grad_output, grad_router,
            gain_sums[0], grad_gain_query, grad_gain_key, gain_sums[1],
            grad_gate, grad_up, down_grad, expert_counts,
        )

    return on_device


def solution(mesh):
    both = ("wide", "narrow")
    in_specs = (P(both, None), P(both), P(both, None), P(both, None))
    in_specs += (P(both, None),) * 5 + (P(both),) * 4 + (P("wide", "narrow", None),) * 3
    out_specs = (P(both, None),) * 7 + (P(both),) * 4 + (P("wide", "narrow", None),) * 3 + (P(),)
    return jax.shard_map(
        make_on_device(mesh.shape["wide"], mesh.shape["narrow"]),
        mesh=mesh,
        in_specs=in_specs,
        out_specs=out_specs,
        check_vma=False,
    )
```
